32 devices in a mesh: dp: 8 (over z, core), tensor: 4 (over y, x).
Axes of the slice: x: 2, y: 2, z: 4, core: 2. Of those that a mesh axis runs over, the one named last changes fastest.
Arguments:
- tokens: bfloat16 [8192, 2048], P(('dp', 'tensor')), may hold values from -6 to 6
- gain_attn: bfloat16 [2048], P('dp'), may hold values from 0.099609375 to 1.8984375
- w_query: bfloat16 [2048, 2048], P('dp', 'tensor'), may hold values from -0.125 to 0.125
- w_key: bfloat16 [2048, 2048], P('dp', 'tensor'), may hold values from -0.125 to 0.125
- w_value: bfloat16 [2048, 2048], P('dp', 'tensor'), may hold values from -0.125 to 0.125
- w_out: bfloat16 [2048, 2048], P('tensor', 'dp'), may hold values from -0.5 to 0.5
- gain_mlp: bfloat16 [2048], P('dp'), may hold values from 0.099609375 to 1.8984375
- w_gate: bfloat16 [2048, 8192], P('dp', 'tensor'), may hold values from -0.125 to 0.125
- w_up: bfloat16 [2048, 8192], P('dp', 'tensor'), may hold values from -0.125 to 0.125
- w_down: bfloat16 [8192, 2048], P('tensor', 'dp'), may hold values from -0.0625 to 0.0625
- cotangent: bfloat16 [8192, 2048], P(('dp', 'tensor')), may hold values from -6 to 6
Outputs:
- output: bfloat16 [8192, 2048], P(('dp', 'tensor'))
- grad_tokens: bfloat16 [8192, 2048], P(('dp', 'tensor'))
- grad_gain_attn: float32 [2048], P('dp')
- grad_query: float32 [2048, 2048], P('dp', 'tensor')
- grad_key: float32 [2048, 2048], P('dp', 'tensor')
- grad_value: float32 [2048, 2048], P('dp', 'tensor')
- grad_out: float32 [2048, 2048], P('tensor', 'dp')
- grad_gain_mlp: float32 [2048], P('dp')
- grad_gate: float32 [2048, 8192], P('dp', 'tensor')
- grad_up: float32 [2048, 8192], P('dp', 'tensor')
- grad_down: float32 [8192, 2048], P('tensor', 'dp')
The draws below stay inside these ranges and needn't reach their ends.
All inputs are finite; a program needn't handle non-finite values.
Results may differ from the reference program's by a relative error of at most 0.023.
Values may be sent and summed in bfloat16 or wider, within the bound.
A program may use at most 256 MiB of HBM per device.

```python
import jax
import jax.numpy as jnp
from jax import lax

D = 2048
HEAD_DIM = 64
FF = 8192
LEN = 1024
TOKENS = 8192


def with_spikes(values, rng, source, target, shards_of, factor):
    def block_of(position):
        return (jnp.arange(values.shape[position]) // (values.shape[position] // shards_of)).reshape((-1,) + (1,) * (values.ndim - 1 - position))

    one_side = jax.random.permutation(rng, shards_of)[block_of(target)]
    second = (block_of(target) + shards_of // 2) % shards_of
    return jnp.where((block_of(source) == one_side) | (block_of(source) == second), factor * values, values)


def block_levels(key, shape, cuts, smallest, largest):
    gain, own = 1.0, jax.random.fold_in(key, 6)
    for position, shards_of in cuts:
        heights = jnp.exp(jax.random.uniform(jax.random.fold_in(own, position), (shards_of,), jnp.float32, smallest / len(cuts), largest / len(cuts)))
        gain = gain * jnp.repeat(heights, shape[position] // shards_of).reshape([-1 if axis == position else 1 for axis in range(len(shape))])
    return gain


def noise(key, shape, width, most, shards=(), kind=jnp.bfloat16):
    values = width * jax.random.normal(key, shape, jnp.float32)
    if shards:
        values = values * block_levels(key, shape, shards, -0.22, 0.18)
    return jnp.clip(values, -most, most).astype(kind)


def noise_with(key, extent, width, reach, split, heavy, kind=jnp.bfloat16):
    values = width * jax.random.normal(key, extent, jnp.float32)
    if split:
        values = values * block_levels(key, extent, split, -0.22, 0.18)
    return jnp.clip(with_spikes(values, jax.random.fold_in(key, 3), *heavy), -reach, reach).astype(kind)


def setup_inputs(seed: int = 0) -> dict:
    key_list = jax.random.split(jax.random.key(seed), 12)
    tokens = noise_with(key_list[0], (TOKENS, D), 1.0, 6.0, ((0, 32),), (0, 1, 32, 2.75))
    gain_attn = jnp.clip(1.0 + 0.18 * jax.random.normal(key_list[1], (D,), jnp.float32), 0.099609375, 1.8984375).astype(jnp.bfloat16)
    w_query = noise(key_list[2], (D, D), D ** -0.5, 0.125, ((0, 8), (1, 4)))
    w_key = noise(key_list[3], (D, D), D ** -0.5, 0.125, ((0, 8), (1, 4)))
    w_value = noise(key_list[4], (D, D), D ** -0.5, 0.125, ((0, 8), (1, 4)))
    w_out = noise(key_list[5], (D, D), (D // 16) ** -0.5, 0.5, ((0, 4), (1, 8)))
    gain_mlp = jnp.clip(1.0 + 0.18 * jax.random.normal(key_list[6], (D,), jnp.float32), 0.099609375, 1.8984375).astype(jnp.bfloat16)
    w_gate = noise(key_list[7], (D, FF), D ** -0.5, 0.125, ((0, 8), (1, 4)))
    w_up = noise(key_list[8], (D, FF), D ** -0.5, 0.125, ((0, 8), (1, 4)))
    w_down = noise(key_list[9], (FF, D), FF ** -0.5, 0.0625, ((0, 4), (1, 8)))
    cotangent = noise_with(key_list[10], (TOKENS, D), 1.0, 6.0, ((0, 32),), (0, 1, 32, 2.75))
    return dict(tokens=tokens, gain_attn=gain_attn, w_query=w_query, w_key=w_key, w_value=w_value, w_out=w_out, gain_mlp=gain_mlp, w_gate=w_gate, w_up=w_up, w_down=w_down, cotangent=cotangent)


@jax.custom_vjp
def low(v):
    return lax.optimization_barrier(v.astype(jnp.bfloat16)).astype(jnp.float32)

@jax.custom_vjp
def low_back(v):
    return v

def low_keep(v):
    return (low(v), None)

def low_pass(kept, grad):
    return (grad,)

def back_keep(v):
    return (v, None)

def back_low(kept, grad):
    return (low(grad),)
low.defvjp(low_keep, low_pass)
low_back.defvjp(back_keep, back_low)
norm_eps = 1e-05
rope_base = 130000.0
masked_score = -1e+30

def dotted(operand, weight):
    return jnp.dot(operand, weight, precision=lax.Precision.HIGHEST)

def norm_rows(values, norm_gain):
    inverse = lax.rsqrt(lax.optimization_barrier(jnp.mean(values * values, axis=-1, keepdims=True)) + norm_eps)
    return values * inverse * norm_gain

def rotary_tables(row_count, seq_len, head_dim):
    half_dim = head_dim // 2
    frequency = rope_base ** (-jnp.arange(half_dim, dtype=jnp.float32) * 2.0 / head_dim)
    positions = (jnp.arange(row_count, dtype=jnp.int32) % seq_len).astype(jnp.float32)
    angles = positions[:, None] * frequency[None, :]
    angles = jnp.concatenate([angles, angles], axis=1)
    return (jnp.cos(angles), jnp.sin(angles))

def rotate(values, cosine, sine_table):
    half_dim = values.shape[-1] // 2
    turned = jnp.concatenate([-values[..., half_dim:], values[..., :half_dim]], axis=-1)
    return values * cosine[:, None, :] + turned * sine_table[:, None, :]

def attend_sequence(seq_block):
    query_proj, key_proj, value_proj = seq_block
    head_count = D // HEAD_DIM
    cosine, sine_table = rotary_tables(LEN, LEN, HEAD_DIM)
    query_rot = low(rotate(query_proj.reshape(LEN, head_count, HEAD_DIM), cosine, sine_table))
    key_rot = low(rotate(key_proj.reshape(LEN, head_count, HEAD_DIM), cosine, sine_table))
    value_heads = value_proj.reshape(LEN, head_count, HEAD_DIM)
    scores = jnp.einsum('qhd,khd->hqk', query_rot, key_rot, precision=lax.Precision.HIGHEST)
    scores = low_back(scores * HEAD_DIM ** (-0.5))
    causal = jnp.arange(LEN)[:, None] >= jnp.arange(LEN)[None, :]
    scores = jnp.where(causal[None], scores, masked_score)
    row_max = lax.optimization_barrier(jnp.max(scores, axis=-1, keepdims=True))
    exp_scores = jnp.exp(scores - row_max)
    attn_probs = low(exp_scores / lax.optimization_barrier(jnp.sum(exp_scores, axis=-1, keepdims=True)))
    attn_mixed = jnp.einsum('hqk,khd->qhd', attn_probs, value_heads, precision=lax.Precision.HIGHEST)
    return attn_mixed.reshape(LEN, D)

def forward(tokens, gain_attn, w_query, w_key, w_value, w_out, gain_mlp, w_gate, w_up, w_down):
    normed = low(norm_rows(tokens, gain_attn))
    query_proj = low_back(dotted(normed, w_query))
    key_proj = low_back(dotted(normed, w_key))
    value_proj = low(low_back(dotted(normed, w_value)))
    seq_count = tokens.shape[0] // LEN
    attn_mixed = lax.map(jax.checkpoint(attend_sequence), (query_proj.reshape(seq_count, LEN, D), key_proj.reshape(seq_count, LEN, D), value_proj.reshape(seq_count, LEN, D)))
    attn_mixed = low(low_back(attn_mixed.reshape(seq_count * LEN, D)))
    residual = tokens + low_back(dotted(attn_mixed, w_out))
    normed_mlp = low(norm_rows(residual, gain_mlp))
    gate_act = low_back(dotted(normed_mlp, w_gate))
    up_act = low_back(dotted(normed_mlp, w_up))
    hidden = low(gate_act * jax.nn.sigmoid(gate_act) * up_act)
    return residual + low_back(dotted(hidden, w_down))

def reference(tokens, gain_attn, w_query, w_key, w_value, w_out, gain_mlp, w_gate, w_up, w_down, cotangent):
    inputs = [array.astype(jnp.float32) for array in (tokens, gain_attn, w_query, w_key, w_value, w_out, gain_mlp, w_gate, w_up, w_down)]
    result, pullback = jax.vjp(forward, *inputs)
    grads = pullback(cotangent.astype(jnp.float32))
    return (result.astype(jnp.bfloat16), grads[0].astype(jnp.bfloat16), grads[1], grads[2], grads[3], grads[4], grads[5], grads[6], grads[7], grads[8], grads[9])
```

```python
import functools

import jax
import jax.numpy as jnp
import numpy as np
from jax import lax
from jax.experimental import pallas as pl
from jax.experimental.pallas import tpu as pltpu
from jax.sharding import PartitionSpec as P

HEAD_DIM = 64
LEN = 1024
MESH = pl.DeviceIdType.MESH
BF16 = jnp.bfloat16
F32 = jnp.float32

norm_eps = 1e-05
rope_base = 130000.0
masked_score = -1e30


def dot(a, b):
    return jnp.dot(a, b, preferred_element_type=F32)


def dot_t(a, b):
    return lax.dot_general(a, b, (((1,), (1,)), ((), ())), preferred_element_type=F32)


def t_dot(a, b):
    return lax.dot_general(a, b, (((0,), (0,)), ((), ())), preferred_element_type=F32)


def aligned(index, size):
    return pl.ds(pl.multiple_of(index * size, size), size)


class Place:
    def __init__(self, n, ring):
        me = lax.axis_index("dp")
        self.n, self.ring = n, ring
        self.z, self.c = me // 2, me % 2
        self.right, self.left = me + 2, me - 2
        self.sib = me + 1 - 2 * self.c
        self.has_r, self.has_l = self.z < n - 1, self.z > 0
        t = lax.axis_index("tensor")
        odd = t % 2
        self.t = t
        self.p = (1 - odd) * (t // 2) + odd * (ring - 1 - t // 2)

    def member(self, offset):
        p = (self.p + offset + self.ring) % self.ring
        back = (p >= self.ring // 2).astype(jnp.int32)
        return (1 - back) * (2 * p) + back * (2 * (self.ring - 1 - p) + 1)

    def barrier(self, with_ring=True):
        sem = pltpu.get_barrier_semaphore()

        def greet(peer):
            pl.semaphore_signal(sem, inc=1, device_id=peer, device_id_type=MESH)

        greet({"dp": self.sib})
        if with_ring:
            greet({"tensor": self.member(1)})
            greet({"tensor": self.member(-1)})

        @pl.when(self.has_r)
        def _():
            greet({"dp": self.right})

        @pl.when(self.has_l)
        def _():
            greet({"dp": self.left})

        peers = self.has_r.astype(jnp.int32) + self.has_l.astype(jnp.int32)
        pl.semaphore_wait(sem, peers + (3 if with_ring else 1))

    def neighbour(self, d):
        return self.right if d == 0 else self.left

    def sends_to(self, d):
        return self.has_r if d == 0 else self.has_l

    def along(self, d, k):
        return self.z + k if d == 0 else self.z - k

    def depth(self, d):
        return self.z if d == 0 else self.n - 1 - self.z


class LineGather:
    def __init__(self, at, own, full, send, recv, sib_send, sib_recv, own_sem):
        self.at, self.own, self.full = at, own, full
        self.send, self.recv = send, recv
        self.sib_send, self.sib_recv, self.own_sem = sib_send, sib_recv, own_sem

    def hop(self, a, h, d):
        at = self.at
        dst = self.full.at[a, at.along(d, 1 - h), at.c]
        src = self.own.at[a] if h == 1 else dst
        return pltpu.make_async_remote_copy(
            src, dst, self.send.at[d, h - 1, a], self.recv.at[d, h - 1, a],
            device_id={"dp": at.neighbour(d)}, device_id_type=MESH)

    def sends(self, h, d):
        return self.at.sends_to(d) & (self.at.depth(d) >= h - 1)

    def arrives(self, h, d):
        return self.at.depth(d) >= h

    def to_sib(self, a):
        part = self.full.at[a, :, self.at.c]
        return pltpu.make_async_remote_copy(
            part, part, self.sib_send.at[a], self.sib_recv.at[a],
            device_id={"dp": self.at.sib}, device_id_type=MESH)

    def own_copy(self, a):
        return pltpu.make_async_copy(
            self.own.at[a], self.full.at[a, self.at.z, self.at.c], self.own_sem.at[a])

    def event(self, a, e):
        n = self.at.n
        if e == 0:
            self.own_copy(a).start()
        for d in range(2):
            if e > 0:
                @pl.when(self.arrives(e, d))
                def _():
                    self.hop(a, e, d).wait_recv()

            if e < n - 1:
                @pl.when(self.sends(e + 1, d))
                def _():
                    self.hop(a, e + 1, d).start()

        if e == n - 1:
            self.own_copy(a).wait()
            self.to_sib(a).start()

    def finish(self, a):
        self.to_sib(a).wait_recv()
        self.to_sib(a).wait_send()
        for h in range(1, self.at.n):
            for d in range(2):
                @pl.when(self.sends(h, d))
                def _():
                    self.hop(a, h, d).wait_send()


class LineSum:
    def __init__(self, at, chunks, sums, land, out, stage, got, send, recv, load, out_sem):
        self.at, self.chunks = at, chunks
        self.sums, self.land, self.out = sums, land, out
        self.stage, self.got = stage, got
        self.send, self.recv, self.load, self.out_sem = send, recv, load, out_sem

    def valid(self, j):
        return (j >= 0) & (j < self.chunks)

    def copy(self, j, s, d, staged):
        at = self.at
        src = self.stage.at[d, s - 2, j % (at.n // 2)] if staged else self.sums.at[j, at.along(d, at.n - s)]
        return pltpu.make_async_remote_copy(
            src, self.land.at[d, j, s - 1], self.send.at[d, s - 1, j], self.recv.at[d, s - 1, j],
            device_id={"dp": at.neighbour(d)}, device_id_type=MESH)

    def arrival(self, j, s, d):
        return pltpu.make_async_remote_copy(
            self.land.at[d, j, s - 1], self.land.at[d, j, s - 1],
            self.send.at[d, s - 1, j], self.recv.at[d, s - 1, j],
            device_id={"dp": self.at.sib}, device_id_type=MESH)

    def arrives(self, s, d):
        depth = self.at.depth(d)
        return (depth > 0) & (depth <= s)

    def get(self, src, k):
        return pltpu.make_async_copy(src, self.got.at[k], self.load.at[k])

    def receive(self, j, s, d, before):
        if before == 0:
            self.arrival(j, s, d).wait_recv()
        elif s > before:
            @pl.when(self.at.depth(d) > 1)
            def _():
                self.arrival(j, s, d).wait_recv()

    def event(self, j, e, before=0):
        at, n = self.at, self.at.n
        if e == 0:
            for s in range(1, n):
                for d in range(2):
                    @pl.when(at.sends_to(d) & (at.depth(d) == 0))
                    def _():
                        self.copy(j, s, d, False).start()

        elif e < n - 1:
            s = e + 1
            for d in range(2):
                @pl.when(at.sends_to(d) & (at.depth(d) > 0) & (at.depth(d) < s))
                def _():
                    self.get(self.sums.at[j, at.along(d, n - s)], 0).start()
                    self.receive(j, s - 1, d, before)
                    self.get(self.land.at[d, j, s - 2], 1).start()
                    self.get(self.sums.at[j, at.along(d, n - s)], 0).wait()
                    self.get(self.land.at[d, j, s - 2], 1).wait()
                    self.stage[d, s - 2, j % (n // 2)] = self.got[0] + self.got[1]
                    self.copy(j, s, d, True).start()
        else:
            self.get(self.sums.at[j, at.z], 0).start()
            for d in range(2):
                @pl.when(at.depth(d) > 0)
                def _():
                    self.receive(j, n - 1, d, before)
                    self.get(self.land.at[d, j, n - 2], 1 + d).start()

            self.get(self.sums.at[j, at.z], 0).wait()
            for d in range(2):
                @pl.when(at.depth(d) > 0)
                def _():
                    self.get(self.land.at[d, j, n - 2], 1 + d).wait()
                    self.got[0] = self.got[0] + self.got[1 + d]

            result = pltpu.make_async_copy(self.got.at[0], self.out.at[j], self.out_sem)
            result.start()
            result.wait()
            self.sent(j, n, before)

    def sent(self, j, events, first=0):
        at, n = self.at, self.at.n
        for s in range(1, n):
            for d in range(2):
                if first == 0 and events > 0:
                    @pl.when(at.sends_to(d) & (at.depth(d) == 0))
                    def _():
                        self.copy(j, s, d, False).wait_send()

                if s >= 2 and first <= s - 1 < events:
                    @pl.when(at.sends_to(d) & (at.depth(d) > 0) & (at.depth(d) < s))
                    def _():
                        self.copy(j, s, d, True).wait_send()

    def drain(self, j, events):
        at, n = self.at, self.at.n
        if events == 0:
            return
        for d in range(2):
            for s in range(max(events, 1), n):
                if s == events:
                    @pl.when(self.arrives(s, d))
                    def _():
                        self.arrival(j, s, d).wait_recv()
                else:
                    @pl.when(at.depth(d) == 1)
                    def _():
                        self.arrival(j, s, d).wait_recv()
        if events < n:
            self.sent(j, events)


class RingGather:
    def __init__(self, at, own, full, send, recv):
        self.at, self.own, self.full, self.send, self.recv = at, own, full, send, recv

    def copy(self, h, d):
        at = self.at
        way = 1 if d == 0 else -1
        owner = at.member(-way * (h - 1))
        rows = self.full.shape[1]
        part = pl.ds(0, rows)
        if h == at.ring // 2:
            part = pl.ds(d * (rows // 2), rows // 2)
        dst = self.full.at[owner, part]
        src = self.own.at[part] if h == 1 else dst
        return pltpu.make_async_remote_copy(
            src, dst, self.send.at[d, h - 1], self.recv.at[d, h - 1],
            device_id={"tensor": at.member(way)}, device_id_type=MESH)

    def start(self, h):
        for d in range(2):
            self.copy(h, d).start()

    def wait(self, h):
        for d in range(2):
            self.copy(h, d).wait_recv()

    def sent(self):
        for h in range(1, self.at.ring // 2 + 1):
            for d in range(2):
                self.copy(h, d).wait_send()


class RingSum:
    def __init__(self, at, part, land, send, recv):
        self.at, self.part, self.land, self.send, self.recv = at, part, land, send, recv
        self.stages = at.ring // 2

    def rows_of(self, k, d):
        rows = self.part.shape[1]
        return pl.ds(d * (rows // 2), rows // 2) if k == 0 else pl.ds(0, rows)

    def target(self, k, d):
        return self.at.member((1 if d == 0 else -1) * (self.stages - k))

    def copy(self, k, d):
        r = self.rows_of(k, d)
        return pltpu.make_async_remote_copy(
            self.part.at[self.target(k, d), r], self.land.at[d, k, r],
            self.send.at[d, k], self.recv.at[d, k],
            device_id={"tensor": self.at.member(1 if d == 0 else -1)}, device_id_type=MESH)

    def start(self, k, d):
        self.copy(k, d).start()

    def add(self, k, d):
        self.copy(k, d).wait_recv()
        block = self.target(k + 1, d)
        rows = self.part.shape[1]
        half = rows // 2
        quarter = max(half // 4, 16)
        first = d * half if k == 0 else 0
        count = (half if k == 0 else rows) // quarter

        @pl.loop(0, count)
        def _(i):
            r = pl.ds(pl.multiple_of(first + i * quarter, quarter), quarter)
            self.part[block, r] = self.part[block, r] + self.land[d, k, r]

    def sent(self):
        for k in range(self.stages):
            for d in range(2):
                self.copy(k, d).wait_send()


def group_lanes(heads, width):
    return lax.broadcasted_iota(jnp.int32, (1, width), 1) // HEAD_DIM


def rope(values, cosine, sine, back=False):
    width = values.shape[-1]
    half = HEAD_DIM // 2
    first = lax.broadcasted_iota(jnp.int32, (1, width), 1) % HEAD_DIM < half
    ahead = pltpu.roll(values, width - half, 1)
    behind = pltpu.roll(values, half, 1)
    turned = jnp.where(first, -ahead, behind)
    return values * cosine - turned * sine if back else values * cosine + turned * sine


def inverse_rms(values):
    return lax.rsqrt(jnp.mean(values * values, axis=-1, keepdims=True) + norm_eps)


def causal_softmax(q_rows, keys, first_row):
    scores = dot_t(q_rows, keys) * HEAD_DIM ** (-0.5)
    row = first_row + lax.broadcasted_iota(jnp.int32, scores.shape, 0)
    column = lax.broadcasted_iota(jnp.int32, scores.shape, 1)
    scores = jnp.where(row >= column, scores, masked_score)
    exp_scores = jnp.exp(scores - jnp.max(scores, axis=-1, keepdims=True))
    return exp_scores * (1.0 / jnp.sum(exp_scores, axis=-1, keepdims=True))


def only(mask, values):
    return jnp.where(mask, values, jnp.zeros_like(values))


def forward_kernel(
    n, ring, pre, q_tile,
    tokens, cotangent, w_own, ff_own, cosine, sine,
    w_full, ff_full, normed_out, q_out, k_out, v_out, mixed_out, residual_out, x_full, dy_full,
    tok, wv, gains, q, k, v, mixed, acc, part, land, xrow, resid,
    a_send, a_recv, a_sib_send, a_sib_recv, a_own,
    f_send, f_recv, f_sib_send, f_sib_recv, f_own,
    t_send, t_recv, c_send, c_recv, x_send, x_recv, s_send, s_recv, io, load,
):
    at = Place(n, ring)
    groups, unit, bs = w_own.shape
    local, width = tokens.shape
    rows = local * ring
    heads = bs // HEAD_DIM
    att = LineGather(at, w_own, w_full, a_send, a_recv, a_sib_send, a_sib_recv, a_own)
    feed = LineGather(at, ff_own, ff_full, f_send, f_recv, f_sib_send, f_sib_recv, f_own)
    tok_ring = RingGather(at, tokens, tok, t_send, t_recv)
    cot_ring = RingGather(at, cotangent, dy_full, c_send, c_recv)
    x_ring = RingGather(at, xrow, x_full, x_send, x_recv)
    sums = RingSum(at, part, land, s_send, s_recv)

    own_tok = pltpu.make_async_copy(tokens, tok.at[at.t], io.at[0])
    own_cot = pltpu.make_async_copy(cotangent, dy_full.at[at.t], io.at[1])
    own_tok.start()
    own_cot.start()
    at.barrier()

    def weights(index):
        return (att, index) if index < groups else (feed, index - groups)

    def half_tick(tick):
        for e in range(n - 1, -1, -1):
            if (tick - e) % 2 == 0 and 0 <= (tick - e) // 2 < groups + pre:
                line, a = weights((tick - e) // 2)
                line.event(a, e)

    def loads(g):
        return [
            pltpu.make_async_copy(w_full.at[g, :, :, pl.ds(i * bs, bs)], wv.at[i], load.at[i])
            for i in range(3)
        ]

    done = [0]

    def run_to(tick):
        while done[0] <= tick:
            half_tick(done[0])
            done[0] += 1

    run_to(0)
    tok_ring.start(1)
    run_to(1)
    tok_ring.wait(1)
    tok_ring.start(2)
    run_to(2)
    for h in range(3, ring // 2 + 1):
        tok_ring.wait(h - 1)
        tok_ring.start(h)
    tok_ring.wait(ring // 2)
    cot_ring.start(1)
    run_to(n - 1)
    att.finish(0)
    gain_load = pltpu.make_async_copy(w_full.at[0, :, :, pl.ds(4 * bs, 16)], gains, load.at[4])
    gain_load.start()
    for copy in loads(0):
        copy.start()
    gain_load.wait()
    own_tok.wait()
    tok_ring.sent()

    def norm_into(values, scale, row, store):
        for i in range(2 * n):
            gain = gains[i // 2, i % 2, row : row + 1, :].astype(F32)
            cols = pl.ds(i * bs, bs)
            store(cols, (values(cols) * scale * gain).astype(BF16))

    norm_tile = min(64, local)

    @pl.loop(0, ring)
    def _(m):
        @pl.loop(0, local // norm_tile)
        def _(i):
            r = aligned(i, norm_tile)
            scale = inverse_rms(tok[m, r].astype(F32))

            def store(cols, value):
                tok[m, r, cols] = value

            norm_into(lambda cols: tok[m, r, cols].astype(F32), scale, 0, store)

    normed_store = pltpu.make_async_copy(tok, normed_out, io.at[2])
    normed_store.start()

    def project(g):
        cols = pl.ds(g * bs, bs)

        @pl.loop(0, ring)
        def _(m):
            r = aligned(m, local)
            x = tok[m]
            query = dot(x, wv[0].reshape(width, bs))
            key = dot(x, wv[1].reshape(width, bs))
            q[r, cols] = rope(query, cosine[r, :], sine[r, :]).astype(BF16)
            k[r, cols] = rope(key, cosine[r, :], sine[r, :]).astype(BF16)
            v[r, cols] = dot(x, wv[2].reshape(width, bs)).astype(BF16)

    def attend(g, between):
        cols = pl.ds(g * bs, bs)
        lanes = group_lanes(heads, bs)
        for i in range(rows // q_tile):
            r = pl.ds(i * q_tile, q_tile)
            keys = pl.ds(0, (i + 1) * q_tile)
            acc[...] = jnp.zeros_like(acc)

            @pl.loop(0, heads)
            def _(h):
                mask = lanes == h
                probs = causal_softmax(only(mask, q[r, cols]), k[keys, cols], i * q_tile)
                acc[...] += dot(probs.astype(BF16), only(mask, v[keys, cols]))

            mixed[r, cols] = acc[...].astype(BF16)
            between(i)

    def nothing(i):
        pass

    for copy in loads(0):
        copy.wait()
    project(0)
    run_to(n)
    cot_ring.wait(1)
    cot_ring.start(2)
    attend(0, nothing)
    for g in range(1, groups):
        run_to(2 * g + n - 1)
        att.finish(g)
        for copy in loads(g):
            copy.start()
        for copy in loads(g):
            copy.wait()
        project(g)
        run_to(2 * g + n)
        attend(g, nothing)
    for h in range(3, ring // 2 + 1):
        cot_ring.wait(h - 1)
        cot_ring.start(h)
    cot_ring.wait(ring // 2)
    stores = [
        pltpu.make_async_copy(ref, out, io.at[3 + i])
        for i, (ref, out) in enumerate(((q, q_out), (k, k_out), (v, v_out), (mixed, mixed_out)))
    ]
    for copy in stores:
        copy.start()
    out_loads = [
        pltpu.make_async_copy(w_full.at[g, :, :, pl.ds(3 * bs, bs)], wv.at[g], load.at[g])
        for g in range(groups)
    ]
    for copy in out_loads:
        copy.start()
    for copy in out_loads:
        copy.wait()

    def out_share(offset):
        m = at.member(offset)
        r = aligned(m, local)
        for b in range(n):
            block = sum(
                dot_t(mixed[r, g * bs : (g + 1) * bs], wv[g, b].reshape(2 * bs, bs))
                for g in range(groups)
            )
            part[m, :, b * 2 * bs : (b + 1) * 2 * bs] = block.astype(BF16)

    out_share(ring // 2)
    for d in range(2):
        sums.start(0, d)
    run_to(done[0])
    for kk in range(1, ring // 2):
        for d in range(2):
            out_share((1 if d == 0 else -1) * (ring // 2 - kk))
        for d in range(2):
            sums.add(kk - 1, d)
            sums.start(kk, d)
        run_to(done[0])
    out_share(0)
    own_again = pltpu.make_async_copy(tokens, xrow, io.at[7])
    own_again.start()
    own_again.wait()
    for d in range(2):
        sums.add(ring // 2 - 1, d)

    @pl.loop(0, local // norm_tile)
    def _(i):
        r = aligned(i, norm_tile)
        value = xrow[r].astype(F32) + part[at.t, r].astype(F32)
        resid[r] = value
        scale = inverse_rms(value)

        def store(cols, value):
            xrow[r, cols] = value

        norm_into(lambda cols: resid[r, cols], scale, 1, store)

    x_ring.start(1)
    own_x = pltpu.make_async_copy(xrow, x_full.at[at.t], io.at[0])
    resid_store = pltpu.make_async_copy(resid, residual_out, io.at[7])
    own_x.start()
    resid_store.start()
    run_to(done[0])
    for h in range(2, ring // 2 + 1):
        x_ring.wait(h - 1)
        x_ring.start(h)
        run_to(done[0])
    run_to(2 * (groups + pre - 1) + n - 1)
    x_ring.wait(ring // 2)
    for line in (cot_ring, x_ring):
        line.sent()
    sums.sent()
    for a in range(pre):
        feed.finish(a)
    for copy in (own_cot, normed_store, own_x, resid_store, *stores):
        copy.wait()


def forward_part(n, ring, pre, tokens, cotangent, w_own, ff_own, cosine, sine, q_tile=256):
    groups, unit, bs = w_own.shape
    chunks, ff_unit, _ = ff_own.shape
    local, width = tokens.shape
    rows = local * ring
    cols = groups * bs
    any_ = pl.BlockSpec(memory_space=pl.ANY)
    vmem = pl.BlockSpec(memory_space=pltpu.VMEM)
    dma = pltpu.SemaphoreType.DMA
    shape = jax.ShapeDtypeStruct
    half = ring // 2
    return pl.pallas_call(
        functools.partial(forward_kernel, n, ring, pre, min(q_tile, rows)),
        out_shape=[
            shape((groups, n, 2, unit, bs), BF16),
            shape((chunks, n, 2, ff_unit, bs), BF16),
            shape((ring, local, width), BF16),
            shape((rows, cols), BF16),
            shape((rows, cols), BF16),
            shape((rows, cols), BF16),
            shape((rows, cols), BF16),
            shape((local, width), F32),
            shape((ring, local, width), BF16),
            shape((ring, local, width), BF16),
        ],
        in_specs=[any_] * 4 + [vmem] * 2,
        out_specs=[any_] * 10,
        scratch_shapes=[
            pltpu.VMEM((ring, local, width), BF16),
            pltpu.VMEM((max(4, groups), n, 2, bs, bs), BF16),
            pltpu.VMEM((n, 2, 16, bs), BF16),
            pltpu.VMEM((rows, cols), BF16),
            pltpu.VMEM((rows, cols), BF16),
            pltpu.VMEM((rows, cols), BF16),
            pltpu.VMEM((rows, cols), BF16),
            pltpu.VMEM((min(q_tile, rows), bs), F32),
            pltpu.VMEM((ring, local, width), BF16),
            pltpu.VMEM((2, half, local, width), BF16),
            pltpu.VMEM((local, width), BF16),
            pltpu.VMEM((local, width), F32),
            dma((2, n - 1, groups)), dma((2, n - 1, groups)),
            dma((groups,)), dma((groups,)), dma((groups,)),
            dma((2, n - 1, chunks)), dma((2, n - 1, chunks)),
            dma((chunks,)), dma((chunks,)), dma((chunks,)),
            dma((2, half)), dma((2, half)), dma((2, half)), dma((2, half)),
            dma((2, half)), dma((2, half)), dma((2, half)), dma((2, half)),
            dma((8,)), dma((5,)),
        ],
        compiler_params=pltpu.CompilerParams(
            collective_id=1, has_side_effects=True, vmem_limit_bytes=56 * 2**20),
    )(tokens, cotangent, w_own, ff_own, cosine, sine)


def feed_kernel(
    n, ring, pre, cut, tile,
    w_own, w_in, x_hbm, dy_hbm,
    w_full, out_hbm, dn_hbm, summed, landed, result,
    x, dy, oacc, dacc, wv, pg, core_in, hid, dgate, dup, stage, got,
    g_send, g_recv, g_sib_send, g_sib_recv, g_own,
    r_send, r_recv, r_load, r_out, core_send, core_recv, store_sem, load_sem, io_sem,
):
    at = Place(n, ring)
    c = at.c
    chunks, unit, bs = w_own.shape
    rows, width = x.shape
    weights = LineGather(at, w_own, w_full, g_send, g_recv, g_sib_send, g_sib_recv, g_own)
    grads = LineSum(at, chunks, summed, landed, result, stage, got, r_send, r_recv, r_load, r_out)
    lag = max(0, n - pre)

    def loads(j):
        return [
            pltpu.make_async_copy(
                w_full.at[j, :, :, pl.ds(i * bs, bs)], wv.at[j % 2, i], load_sem.at[j % 2, i])
            for i in range(3)
        ]

    def core_copy(j):
        return pltpu.make_async_remote_copy(
            pg.at[1 - c], core_in.at[j % 2], core_send.at[j % 2], core_recv.at[j % 2],
            device_id={"dp": at.sib}, device_id_type=MESH)

    def store(j):
        return pltpu.make_async_copy(pg.at[c], summed.at[j], store_sem)

    x_in = pltpu.make_async_copy(x_hbm, x, io_sem.at[0])
    dy_in = pltpu.make_async_copy(dy_hbm, dy, io_sem.at[1])
    x_in.start()
    dy_in.start()
    if pre > 0:
        for copy in loads(0):
            copy.start()
    at.barrier(False)

    @pl.loop(0, rows // 64)
    def _(i):
        r = aligned(i, 64)
        oacc[r] = jnp.zeros((64, width), F32)
        dacc[r] = jnp.zeros((64, width), F32)

    x_in.wait()
    dy_in.wait()

    def weight_grads(cc):
        @pl.loop(0, n)
        def _(k):
            cols = aligned(2 * k + cc, bs)
            pg[cc, k, pl.ds(0, bs)] = t_dot(x[:, cols], dgate[...]).astype(BF16)
            pg[cc, k, pl.ds(bs, bs)] = t_dot(x[:, cols], dup[...]).astype(BF16)
            pg[cc, k, pl.ds(2 * bs, bs)] = t_dot(dy[:, cols], hid[...]).astype(BF16)

    def compute(j):
        slot = j % 2
        for copy in loads(j):
            copy.wait()

        @pl.loop(0, rows // tile)
        def _(m):
            r = aligned(m, tile)
            gate = dot(x[r, :], wv[slot, 0].reshape(width, bs))
            up = dot(x[r, :], wv[slot, 1].reshape(width, bs))
            dh = dot(dy[r, :], wv[slot, 2].reshape(width, bs))
            s = jax.nn.sigmoid(gate)
            gs = gate * s
            hid[r, :] = (gs * up).astype(BF16)
            dup[r, :] = (dh * gs).astype(BF16)
            dgate[r, :] = (dh * up * (s + gs * (1 - s))).astype(BF16)

        weight_grads(1 - c)
        core_copy(j).start()

        @pl.loop(0, rows // tile)
        def _(m):
            r = aligned(m, tile)

            @pl.loop(0, n)
            def _(k):
                cols = aligned(k, 2 * bs)
                oacc[r, cols] += dot_t(hid[r, :], wv[slot, 2, k].reshape(2 * bs, bs))
                dacc[r, cols] += dot_t(dgate[r, :], wv[slot, 0, k].reshape(2 * bs, bs)) + dot_t(
                    dup[r, :], wv[slot, 1, k].reshape(2 * bs, bs))

        weight_grads(c)
        core_copy(j).wait_recv()

        @pl.loop(0, n)
        def _(k):
            pg[c, k] = pg[c, k] + core_in[slot, k]

        store(j).start()
        core_copy(j).wait_send()

    @pl.loop(0, lag + chunks)
    def _(step):
        for e in range(n - 1, -1, -1):
            a = pre + step - e

            @pl.when((a >= pre) & (a < chunks))
            def _():
                weights.event(a, e)

        j = step - lag

        @pl.when((j >= 1) & (j <= chunks))
        def _():
            store(j - 1).wait()

        tick = j - 1
        for e in range(n - 1, -1, -1):
            q = tick - e + 2 * n
            r = q // 2 - n

            @pl.when((q % 2 == 0) & (tick < cut) & (r >= 0) & (r < chunks))
            def _():
                grads.event(r, e)

        @pl.when((j >= 0) & (j < chunks))
        def _():
            compute(j)

        whole = pre + step - (n - 1)

        @pl.when((whole >= pre) & (whole < chunks))
        def _():
            weights.finish(whole)

        @pl.when((j + 1 >= 0) & (j + 1 < chunks))
        def _():
            for copy in loads(j + 1):
                copy.start()

    store(chunks - 1).wait()
    x[...] = oacc[...].astype(BF16)
    dy[...] = dacc[...].astype(BF16)
    x_out = pltpu.make_async_copy(x, out_hbm, io_sem.at[0])
    dy_out = pltpu.make_async_copy(dy, dn_hbm, io_sem.at[1])
    x_out.start()
    dy_out.start()
    for j in range(chunks):
        grads.drain(j, min(n, max(0, cut - 2 * j)))
    x_out.wait()
    dy_out.wait()


def feed_part(n, ring, pre, cut, w_own, w_full, x, dy, tile=512):
    chunks, unit, bs = w_own.shape
    rows, width = x.shape
    any_ = pl.BlockSpec(memory_space=pl.ANY)
    dma = pltpu.SemaphoreType.DMA
    shape = jax.ShapeDtypeStruct
    return pl.pallas_call(
        functools.partial(feed_kernel, n, ring, pre, cut, min(tile, rows)),
        out_shape=[
            shape(w_full.shape, BF16),
            shape((rows, width), BF16),
            shape((rows, width), BF16),
            shape((chunks, n, unit, bs), BF16),
            shape((2, chunks, n - 1, unit, bs), BF16),
            shape((chunks, unit, bs), BF16),
        ],
        in_specs=[any_] * 4,
        out_specs=[any_] * 6,
        input_output_aliases={1: 0},
        scratch_shapes=[
            pltpu.VMEM((rows, width), BF16),
            pltpu.VMEM((rows, width), BF16),
            pltpu.VMEM((rows, width), F32),
            pltpu.VMEM((rows, width), F32),
            pltpu.VMEM((2, 3, n, 2, bs, bs), BF16),
            pltpu.VMEM((2, n, unit, bs), BF16),
            pltpu.VMEM((2, n, unit, bs), BF16),
            pltpu.VMEM((rows, bs), BF16),
            pltpu.VMEM((rows, bs), BF16),
            pltpu.VMEM((rows, bs), BF16),
            pltpu.VMEM((2, n - 2, n // 2, unit, bs), BF16),
            pltpu.VMEM((3, unit, bs), BF16),
            dma((2, n - 1, chunks)), dma((2, n - 1, chunks)),
            dma((chunks,)), dma((chunks,)), dma((chunks,)),
            dma((2, n - 1, chunks)), dma((2, n - 1, chunks)),
            dma((3,)), dma,
            dma((2,)), dma((2,)), dma, dma((2, 3)), dma((2,)),
        ],
        compiler_params=pltpu.CompilerParams(
            collective_id=2, has_side_effects=True, vmem_limit_bytes=60 * 2**20),
    )(w_own, w_full, x, dy)


def backward_kernel(
    n, ring, cut, q_tile,
    dn_in, out_in, residual, cotangent, tokens, normed_in, q_in, k_in, v_in, mixed_in,
    w_full, cosine, sine, ff_summed, ff_landed_in, ff_result_in,
    output, grad_tokens, gain_grads, ff_landed, ff_result, att_result, att_summed, att_landed,
    part, land, dres_full, normed, wv, gains, q, k, v, mixed, dmix, dq, dk, dv, dproj,
    resid, dres, small, lined, gsum, pg, core_in, ff_stage, ff_got, att_stage, att_got,
    s1_send, s1_recv, s2_send, s2_recv, s3_send, s3_recv, x_send, x_recv, free_sem,
    f_send, f_recv, f_load, f_out, a_send, a_recv, a_load, a_out,
    core_send, core_recv, store_sem, io, load,
):
    at = Place(n, ring)
    c = at.c
    groups, _, _, _, bs = w_full.shape
    local, width = tokens.shape
    rows = local * ring
    heads = bs // HEAD_DIM
    chunks = ff_result.shape[0]
    half = ring // 2
    feed = LineSum(at, chunks, ff_summed, ff_landed, ff_result, ff_stage, ff_got,
                   f_send, f_recv, f_load, f_out)
    att = LineSum(at, groups, att_summed, att_landed, att_result, att_stage, att_got,
                  a_send, a_recv, a_load, a_out)
    sums1 = RingSum(at, part, land, s1_send, s1_recv)
    sums2 = RingSum(at, part, land, s2_send, s2_recv)
    sums3 = RingSum(at, part, land, s3_send, s3_recv)
    dres_ring = RingGather(at, small, dres_full, x_send, x_recv)

    def fetch(src, dst, i):
        return pltpu.make_async_copy(src, dst, io.at[i])

    part_in = fetch(dn_in, part, 0)
    part_in.start()
    resid_in = fetch(residual, resid, 1)
    resid_in.start()
    cot_in = fetch(cotangent, lined, 2)
    cot_in.start()
    gains_in = fetch(w_full.at[0, :, :, pl.ds(4 * bs, 16)], gains, 3)
    gains_in.start()
    saved = [
        fetch(src, dst, 4 + i)
        for i, (src, dst) in enumerate(
            ((normed_in, normed), (q_in, q), (k_in, k), (v_in, v), (mixed_in, mixed)))
    ]
    for copy in saved:
        copy.start()
    at.barrier()

    done = [cut]
    last = 2 * (chunks - 1) + n - 1

    def feed_tick():
        tick = done[0]
        if tick > last:
            return
        for e in range(n - 1, -1, -1):
            if (tick - e) % 2 == 0 and 0 <= (tick - e) // 2 < chunks:
                j = (tick - e) // 2
                feed.event(j, e, min(n, max(0, cut - 2 * j)))
        done[0] += 1

    def gain_of(row, i):
        return gains[i // 2, i % 2, row : row + 1, :].astype(F32)

    tile = min(64, local)

    def norm_back(value_of, grad_of, row, emit):
        gsum[row : row + 1, :] = jnp.zeros((1, width), F32)

        @pl.loop(0, local // tile)
        def _(i):
            r = aligned(i, tile)
            value = value_of(r, pl.ds(0, width))
            scale = inverse_rms(value)
            inner = jnp.zeros((tile, 1), F32)
            for b in range(2 * n):
                cols = pl.ds(b * bs, bs)
                value = value_of(r, cols)
                grad = grad_of(r, cols)
                gsum[row : row + 1, cols] += jnp.sum(grad * value * scale, axis=0, keepdims=True)
                inner += jnp.sum(grad * gain_of(row, b) * value, axis=-1, keepdims=True)
            pull = scale * scale * scale * (inner / width)
            for b in range(2 * n):
                cols = pl.ds(b * bs, bs)
                emit(r, cols, scale * grad_of(r, cols) * gain_of(row, b) - value_of(r, cols) * pull)

    def ring_sum(sums, between):
        for kk in range(half):
            between()
            for d in range(2):
                sums.add(kk, d)
                if kk < half - 1:
                    sums.start(kk + 1, d)

    part_in.wait()
    for d in range(2):
        sums1.start(0, d)
    for copy in (resid_in, cot_in, gains_in):
        copy.wait()
    ring_sum(sums1, feed_tick)

    def emit_residual(r, cols, value):
        total = lined[r, cols].astype(F32) + value
        dres[r, cols] = total
        small[r, cols] = total.astype(BF16)

    norm_back(lambda r, cols: resid[r, cols], lambda r, cols: part[at.t, r, cols].astype(F32),
              1, emit_residual)
    dres_ring.start(1)
    own_dres = fetch(small, dres_full.at[at.t], 0)
    own_dres.start()

    def loads(g):
        return [
            pltpu.make_async_copy(w_full.at[g, :, :, pl.ds(i * bs, bs)], wv.at[i, g], load.at[i, g])
            for i in range(4)
        ]

    for g in range(groups):
        for copy in loads(g):
            copy.start()
    sums1.sent()
    second_in = fetch(out_in, part, 1)
    second_in.start()
    for h in range(2, half + 1):
        feed_tick()
        dres_ring.wait(h - 1)
        dres_ring.start(h)
    feed_tick()
    second_in.wait()
    own_dres.wait()
    dres_ring.wait(half)
    for d in range(2):
        sums2.start(0, d)
    for copy in saved:
        copy.wait()
    for g in range(groups):
        for copy in loads(g):
            copy.wait()

    def core_copy(g):
        return pltpu.make_async_remote_copy(
            pg.at[1 - c], core_in.at[g], core_send.at[g], core_recv.at[g],
            device_id={"dp": at.sib}, device_id_type=MESH)

    def store(g):
        return pltpu.make_async_copy(pg.at[c], att_summed.at[g], store_sem)

    def attend_back(g, between):
        gcols = pl.ds(g * bs, bs)
        lanes = group_lanes(heads, bs)
        dk[...] = jnp.zeros_like(dk)
        dv[...] = jnp.zeros_like(dv)
        for i in range(rows // q_tile):
            r = pl.ds(i * q_tile, q_tile)
            keys = pl.ds(0, (i + 1) * q_tile)
            dq[r] = jnp.zeros((q_tile, bs), F32)

            @pl.loop(0, heads)
            def _(h):
                mask = lanes == h
                qh = only(mask, q[r, gcols])
                dmh = only(mask, dmix[r])
                probs = causal_softmax(qh, k[keys, gcols], i * q_tile)
                d_probs = dot_t(dmh, v[keys, gcols])
                inner = jnp.sum(d_probs * probs, axis=-1, keepdims=True)
                d_scores = (probs * (d_probs - inner)).astype(BF16)
                dq[r] += dot(d_scores, only(mask, k[keys, gcols]))
                dk[keys] += t_dot(d_scores, qh)
                dv[keys] += t_dot(probs.astype(BF16), dmh)

            between(i)

    def weight_grads(g, cc):
        gcols = pl.ds(g * bs, bs)

        @pl.loop(0, n)
        def _(b):
            cols = aligned(2 * b + cc, bs)
            x = normed[:, :, cols].reshape(rows, bs)
            for i in range(3):
                pg[cc, b, pl.ds(i * bs, bs)] = t_dot(
                    x, dproj[i, :, gcols]).astype(BF16)
            pg[cc, b, pl.ds(3 * bs, bs)] = t_dot(
                dres_full[:, :, cols].reshape(rows, bs), mixed[:, gcols]).astype(BF16)

    second = [0]

    def second_sum(i):
        if second[0] < half:
            kk = second[0]
            for d in range(2):
                sums2.add(kk, d)
                if kk < half - 1:
                    sums2.start(kk + 1, d)
            second[0] += 1

    def between(i):
        feed_tick()
        if i % 2 == 1:
            second_sum(i)

    for g in range(groups):
        gcols = pl.ds(g * bs, bs)

        @pl.loop(0, ring)
        def _(m):
            r = aligned(m, local)
            dmix[r] = dot(dres_full[m], wv[3, g].reshape(width, bs)).astype(BF16)

        attend_back(g, between)

        @pl.loop(0, ring)
        def _(m):
            r = aligned(m, local)
            for i, ref in enumerate((dq, dk)):
                value = ref[r] * HEAD_DIM ** (-0.5)
                dproj[i, r, gcols] = rope(value, cosine[r, :], sine[r, :], back=True).astype(BF16)
            dproj[2, r, gcols] = dv[r].astype(BF16)

        if g > 0:
            store(g - 1).wait()
            core_copy(g - 1).wait_send()
            att.event(g - 1, 0)
        weight_grads(g, 1 - c)
        core_copy(g).start()
        weight_grads(g, c)
        core_copy(g).wait_recv()

        @pl.loop(0, n)
        def _(b):
            pg[c, b] = pg[c, b] + core_in[g, b]

        store(g).start()

    while second[0] < half:
        second_sum(0)
    sums2.sent()

    @pl.loop(0, local // tile)
    def _(i):
        r = aligned(i, tile)
        lined[r] = (resid[r] + part[at.t, r].astype(F32)).astype(BF16)

    out_store = fetch(lined, output, 0)
    out_store.start()
    for way in (1, -1):
        pl.semaphore_signal(
            free_sem, inc=1, device_id={"tensor": at.member(way)}, device_id_type=MESH)
    store(groups - 1).wait()
    att.event(groups - 1, 0)

    def share(offset):
        m = at.member(offset)
        r = aligned(m, local)
        for b in range(n):
            block = sum(
                dot_t(dproj[i, r, g * bs : (g + 1) * bs], wv[i, g, b].reshape(2 * bs, bs))
                for i in range(3) for g in range(groups)
            )
            part[m, :, b * 2 * bs : (b + 1) * 2 * bs] = block.astype(BF16)

    share(half)
    pl.semaphore_wait(free_sem, 2)
    for d in range(2):
        sums3.start(0, d)
    while done[0] <= last:
        feed_tick()
    tok_in = fetch(tokens, small, 1)
    dres_ring.sent()
    tok_in.start()
    for kk in range(1, half):
        for d in range(2):
            share((1 if d == 0 else -1) * (half - kk))
        for d in range(2):
            sums3.add(kk - 1, d)
            sums3.start(kk, d)
        for g in range(groups):
            att.event(g, kk)
    share(0)
    for e in range(half, n):
        for g in range(groups):
            att.event(g, e)
    for d in range(2):
        sums3.add(half - 1, d)
    tok_in.wait()
    out_store.wait()

    def emit_tokens(r, cols, value):
        lined[r, cols] = (dres[r, cols] + value).astype(BF16)

    norm_back(lambda r, cols: small[r, cols].astype(F32),
              lambda r, cols: part[at.t, r, cols].astype(F32), 0, emit_tokens)
    gsum[2:8, :] = jnp.zeros((6, width), F32)
    last_stores = [fetch(lined, grad_tokens, 0), fetch(gsum, gain_grads, 1)]
    for copy in last_stores:
        copy.start()
    for copy in last_stores:
        copy.wait()
    sums3.sent()
    core_copy(groups - 1).wait_send()


def backward_part(
    n, ring, cut, dn, out, residual, cotangent, tokens, normed, q, k, v, mixed,
    w_full, cosine, sine, ff_summed, ff_landed, ff_result, q_tile=256,
):
    groups, _, _, _, bs = w_full.shape
    chunks, unit, _ = ff_result.shape
    local, width = tokens.shape
    rows = local * ring
    cols = groups * bs
    half = ring // 2
    any_ = pl.BlockSpec(memory_space=pl.ANY)
    vmem = pl.BlockSpec(memory_space=pltpu.VMEM)
    dma = pltpu.SemaphoreType.DMA
    shape = jax.ShapeDtypeStruct
    big = (ring, local, width)
    return pl.pallas_call(
        functools.partial(backward_kernel, n, ring, cut, min(q_tile, rows)),
        out_shape=[
            shape((local, width), BF16),
            shape((local, width), BF16),
            shape((8, width), F32),
            shape(ff_landed.shape, BF16),
            shape(ff_result.shape, BF16),
            shape((groups, 4 * bs, bs), BF16),
            shape((groups, n, 4 * bs, bs), BF16),
            shape((2, groups, n - 1, 4 * bs, bs), BF16),
        ],
        in_specs=[any_] * 11 + [vmem] * 2 + [any_] * 3,
        out_specs=[any_] * 8,
        input_output_aliases={14: 3, 15: 4},
        scratch_shapes=[
            pltpu.VMEM(big, BF16),
            pltpu.VMEM((2, half, local, width), BF16),
            pltpu.VMEM(big, BF16),
            pltpu.VMEM(big, BF16),
            pltpu.VMEM((4, groups, n, 2, bs, bs), BF16),
            pltpu.VMEM((n, 2, 16, bs), BF16),
            pltpu.VMEM((rows, cols), BF16),
            pltpu.VMEM((rows, cols), BF16),
            pltpu.VMEM((rows, cols), BF16),
            pltpu.VMEM((rows, cols), BF16),
            pltpu.VMEM((rows, bs), BF16),
            pltpu.VMEM((rows, bs), F32),
            pltpu.VMEM((rows, bs), F32),
            pltpu.VMEM((rows, bs), F32),
            pltpu.VMEM((3, rows, cols), BF16),
            pltpu.VMEM((local, width), F32),
            pltpu.VMEM((local, width), F32),
            pltpu.VMEM((local, width), BF16),
            pltpu.VMEM((local, width), BF16),
            pltpu.VMEM((8, width), F32),
            pltpu.VMEM((2, n, 4 * bs, bs), BF16),
            pltpu.VMEM((groups, n, 4 * bs, bs), BF16),
            pltpu.VMEM((2, n - 2, n // 2, unit, bs), BF16),
            pltpu.VMEM((3, unit, bs), BF16),
            pltpu.VMEM((2, n - 2, n // 2, 4 * bs, bs), BF16),
            pltpu.VMEM((3, 4 * bs, bs), BF16),
            dma((2, half)), dma((2, half)), dma((2, half)), dma((2, half)),
            dma((2, half)), dma((2, half)), dma((2, half)), dma((2, half)),
            pltpu.SemaphoreType.REGULAR,
            dma((2, n - 1, chunks)), dma((2, n - 1, chunks)), dma((3,)), dma,
            dma((2, n - 1, groups)), dma((2, n - 1, groups)), dma((3,)), dma,
            dma((groups,)), dma((groups,)), dma, dma((9,)), dma((4, groups)),
        ],
        compiler_params=pltpu.CompilerParams(
            collective_id=3, has_side_effects=True, vmem_limit_bytes=63 * 2**20),
    )(dn, out, residual, cotangent, tokens, normed, q, k, v, mixed,
      w_full, cosine, sine, ff_summed, ff_landed, ff_result)


PREFETCH = 4
CUT = 6


def pack_attention(w_query, w_key, w_value, w_out, gain_attn, gain_mlp):
    bs = w_query.shape[0]
    groups = w_query.shape[1] // bs

    def columns(part):
        return part.reshape(bs, groups, bs).transpose(1, 0, 2)

    gains = jnp.pad(jnp.stack([gain_attn, gain_mlp]), ((0, 14), (0, 0)))
    return jnp.concatenate(
        [
            columns(w_query),
            columns(w_key),
            columns(w_value),
            w_out.reshape(groups, bs, bs).transpose(0, 2, 1),
            jnp.broadcast_to(gains[None], (groups, 16, bs)),
        ],
        axis=1,
    )


def pack_feed(w_gate, w_up, w_down):
    bs = w_gate.shape[0]
    chunks = w_gate.shape[1] // bs

    def columns(part):
        return part.reshape(bs, chunks, bs).transpose(1, 0, 2)

    return jnp.concatenate(
        [columns(w_gate), columns(w_up), w_down.reshape(chunks, bs, bs).transpose(0, 2, 1)], axis=1
    )


def columns_of(blocks, i):
    chunks, _, bs = blocks.shape
    part = blocks[:, i * bs : (i + 1) * bs]
    return part.transpose(1, 0, 2).reshape(bs, chunks * bs).astype(F32)


def rows_of(blocks, i):
    chunks, _, bs = blocks.shape
    part = blocks[:, i * bs : (i + 1) * bs]
    return part.transpose(0, 2, 1).reshape(chunks * bs, bs).astype(F32)


def rotary_tables(row_count, width):
    frequency = rope_base ** (-np.arange(HEAD_DIM // 2) * 2.0 / HEAD_DIM)
    angles = (np.arange(row_count) % LEN)[:, None] * frequency[None, :]
    angles = np.tile(angles, (1, width // (HEAD_DIM // 2)))
    return np.cos(angles).astype(np.float32), np.sin(angles).astype(np.float32)


def shards(
    tokens, gain_attn, w_query, w_key, w_value, w_out, gain_mlp, w_gate, w_up, w_down, cotangent
):
    dp, ring = lax.axis_size("dp"), lax.axis_size("tensor")
    n = dp // 2
    local, width = tokens.shape
    rows = local * ring
    assert rows == LEN
    bs = w_query.shape[0]
    cosine, sine = rotary_tables(rows, bs)
    att_own = pack_attention(w_query, w_key, w_value, w_out, gain_attn, gain_mlp)
    ff_own = pack_feed(w_gate, w_up, w_down)
    w_full, ff_full, normed, q, k, v, mixed, residual, x, dy = forward_part(
        n, ring, PREFETCH, tokens, cotangent, att_own, ff_own, cosine, sine
    )
    _, out, dn, summed, landed, result = feed_part(
        n, ring, PREFETCH, CUT, ff_own, ff_full, x.reshape(rows, width), dy.reshape(rows, width)
    )
    output, grad_tokens, gain_grads, _, ff_grads, att_grads, _, _ = backward_part(
        n, ring, CUT, dn.reshape(x.shape), out.reshape(x.shape), residual, cotangent, tokens,
        normed, q, k, v, mixed, w_full, cosine, sine, summed, landed, result,
    )
    gains = lax.psum(
        lax.psum_scatter(gain_grads[:2], "dp", scatter_dimension=1, tiled=True), "tensor"
    )
    return (
        output,
        grad_tokens,
        gains[0],
        columns_of(att_grads, 0),
        columns_of(att_grads, 1),
        columns_of(att_grads, 2),
        rows_of(att_grads, 3),
        gains[1],
        columns_of(ff_grads, 0),
        columns_of(ff_grads, 1),
        rows_of(ff_grads, 2),
    )


def solution(mesh):
    placed = (
        P(("dp", "tensor"), None),
        P("dp"),
        P("dp", "tensor"),
        P("dp", "tensor"),
        P("dp", "tensor"),
        P("tensor", "dp"),
        P("dp"),
        P("dp", "tensor"),
        P("dp", "tensor"),
        P("tensor", "dp"),
        P(("dp", "tensor"), None),
    )
    return jax.shard_map(
        shards,
        mesh=mesh,
        in_specs=placed,
        out_specs=(
            P(("dp", "tensor"), None),
            P(("dp", "tensor"), None),
            P("dp"),
            P("dp", "tensor"),
            P("dp", "tensor"),
            P("dp", "tensor"),
            P("tensor", "dp"),
            P("dp"),
            P("dp", "tensor"),
            P("dp", "tensor"),
            P("tensor", "dp"),
        ),
        check_vma=False,
    )
```

```python
import functools

import jax
import jax.numpy as jnp
import numpy as np
from jax import lax
from jax.experimental import pallas as pl
from jax.experimental.pallas import tpu as pltpu
from jax.sharding import PartitionSpec as P

HEAD_DIM = 64
LEN = 1024
MESH = pl.DeviceIdType.MESH
BF16 = jnp.bfloat16
F32 = jnp.float32

norm_eps = 1e-05
rope_base = 130000.0
masked_score = -1e30


def dot(a, b):
    return jnp.dot(a, b, preferred_element_type=F32)


def dot_t(a, b):
    return lax.dot_general(a, b, (((1,), (1,)), ((), ())), preferred_element_type=F32)


def t_dot(a, b):
    return lax.dot_general(a, b, (((0,), (0,)), ((), ())), preferred_element_type=F32)


def aligned(index, size):
    return pl.ds(pl.multiple_of(index * size, size), size)


class Place:
    def __init__(self, n, ring):
        me = lax.axis_index("dp")
        self.n, self.ring = n, ring
        self.z, self.c = me // 2, me % 2
        self.right, self.left = me + 2, me - 2
        self.sib = me + 1 - 2 * self.c
        self.has_r, self.has_l = self.z < n - 1, self.z > 0
        t = lax.axis_index("tensor")
        odd = t % 2
        self.t = t
        self.p = (1 - odd) * (t // 2) + odd * (ring - 1 - t // 2)

    def member(self, offset):
        p = (self.p + offset + self.ring) % self.ring
        back = (p >= self.ring // 2).astype(jnp.int32)
        return (1 - back) * (2 * p) + back * (2 * (self.ring - 1 - p) + 1)

    def barrier(self, with_ring=True, with_all=False):
        sem = pltpu.get_barrier_semaphore()

        def greet(peer):
            pl.semaphore_signal(sem, inc=1, device_id=peer, device_id_type=MESH)

        if with_all:
            for k in range(1, 2 * self.n):
                greet({"dp": (2 * self.z + self.c + k) % (2 * self.n)})
            for k in range(1, self.ring):
                greet({"tensor": (self.t + k) % self.ring})
            pl.semaphore_wait(sem, 2 * self.n - 1 + self.ring - 1)
            return
        greet({"dp": self.sib})
        if with_ring:
            greet({"tensor": self.member(1)})
            greet({"tensor": self.member(-1)})

        @pl.when(self.has_r)
        def _():
            greet({"dp": self.right})

        @pl.when(self.has_l)
        def _():
            greet({"dp": self.left})

        peers = self.has_r.astype(jnp.int32) + self.has_l.astype(jnp.int32)
        pl.semaphore_wait(sem, peers + (3 if with_ring else 1))

    def neighbour(self, d):
        return self.right if d == 0 else self.left

    def sends_to(self, d):
        return self.has_r if d == 0 else self.has_l

    def along(self, d, k):
        return self.z + k if d == 0 else self.z - k

    def depth(self, d):
        return self.z if d == 0 else self.n - 1 - self.z


class LineGather:
    def __init__(self, at, full, send, recv, sib_send, sib_recv):
        self.at, self.full = at, full
        self.send, self.recv = send, recv
        self.sib_send, self.sib_recv = sib_send, sib_recv

    def hop(self, a, h, d):
        at = self.at
        block = self.full.at[a, at.along(d, 1 - h), at.c]
        return pltpu.make_async_remote_copy(
            block, block, self.send.at[d, h - 1, a], self.recv.at[d, h - 1, a],
            device_id={"dp": at.neighbour(d)}, device_id_type=MESH)

    def sends(self, h, d):
        return self.at.sends_to(d) & (self.at.depth(d) >= h - 1)

    def arrives(self, h, d):
        return self.at.depth(d) >= h

    def to_sib(self, a):
        part = self.full.at[a, :, self.at.c]
        return pltpu.make_async_remote_copy(
            part, part, self.sib_send.at[a], self.sib_recv.at[a],
            device_id={"dp": self.at.sib}, device_id_type=MESH)

    def event(self, a, e):
        n = self.at.n
        for d in range(2):
            if e > 0:
                @pl.when(self.arrives(e, d))
                def _():
                    self.hop(a, e, d).wait_recv()

            if e < n - 1:
                @pl.when(self.sends(e + 1, d))
                def _():
                    self.hop(a, e + 1, d).start()

        if e == n - 1:
            self.to_sib(a).start()

    def finish(self, a):
        self.to_sib(a).wait_recv()
        self.to_sib(a).wait_send()
        for h in range(1, self.at.n):
            for d in range(2):
                @pl.when(self.sends(h, d))
                def _():
                    self.hop(a, h, d).wait_send()


class LineSum:
    def __init__(self, at, chunks, sums, land, out, stage, got, send, recv, load, out_sem):
        self.at, self.chunks = at, chunks
        self.sums, self.land, self.out = sums, land, out
        self.stage, self.got = stage, got
        self.send, self.recv, self.load, self.out_sem = send, recv, load, out_sem

    def valid(self, j):
        return (j >= 0) & (j < self.chunks)

    def copy(self, j, s, d, staged):
        at = self.at
        src = self.stage.at[d, s - 2, j % (at.n // 2)] if staged else self.sums.at[j, at.along(d, at.n - s)]
        return pltpu.make_async_remote_copy(
            src, self.land.at[d, j, s - 1], self.send.at[d, s - 1, j], self.recv.at[d, s - 1, j],
            device_id={"dp": at.neighbour(d)}, device_id_type=MESH)

    def arrival(self, j, s, d):
        return pltpu.make_async_remote_copy(
            self.land.at[d, j, s - 1], self.land.at[d, j, s - 1],
            self.send.at[d, s - 1, j], self.recv.at[d, s - 1, j],
            device_id={"dp": self.at.sib}, device_id_type=MESH)

    def arrives(self, s, d):
        depth = self.at.depth(d)
        return (depth > 0) & (depth <= s)

    def get(self, src, k):
        return pltpu.make_async_copy(src, self.got.at[k], self.load.at[k])

    def receive(self, j, s, d, before):
        if before == 0:
            self.arrival(j, s, d).wait_recv()
        elif s > before:
            @pl.when(self.at.depth(d) > 1)
            def _():
                self.arrival(j, s, d).wait_recv()

    def event(self, j, e, before=0):
        at, n = self.at, self.at.n
        if e == 0:
            for s in range(1, n):
                for d in range(2):
                    @pl.when(at.sends_to(d) & (at.depth(d) == 0))
                    def _():
                        self.copy(j, s, d, False).start()

        elif e < n - 1:
            s = e + 1
            for d in range(2):
                @pl.when(at.sends_to(d) & (at.depth(d) > 0) & (at.depth(d) < s))
                def _():
                    self.get(self.sums.at[j, at.along(d, n - s)], 0).start()
                    self.receive(j, s - 1, d, before)
                    self.get(self.land.at[d, j, s - 2], 1).start()
                    self.get(self.sums.at[j, at.along(d, n - s)], 0).wait()
                    self.get(self.land.at[d, j, s - 2], 1).wait()
                    self.stage[d, s - 2, j % (n // 2)] = self.got[0] + self.got[1]
                    self.copy(j, s, d, True).start()
        else:
            self.get(self.sums.at[j, at.z], 0).start()
            for d in range(2):
                @pl.when(at.depth(d) > 0)
                def _():
                    self.receive(j, n - 1, d, before)
                    self.get(self.land.at[d, j, n - 2], 1 + d).start()

            self.get(self.sums.at[j, at.z], 0).wait()
            for d in range(2):
                @pl.when(at.depth(d) > 0)
                def _():
                    self.get(self.land.at[d, j, n - 2], 1 + d).wait()
                    self.got[0] = self.got[0] + self.got[1 + d]

            result = pltpu.make_async_copy(self.got.at[0], self.out.at[j], self.out_sem)
            result.start()
            result.wait()
            self.sent(j, n, before)

    def sent(self, j, events, first=0):
        at, n = self.at, self.at.n
        for s in range(1, n):
            for d in range(2):
                if first == 0 and events > 0:
                    @pl.when(at.sends_to(d) & (at.depth(d) == 0))
                    def _():
                        self.copy(j, s, d, False).wait_send()

                if s >= 2 and first <= s - 1 < events:
                    @pl.when(at.sends_to(d) & (at.depth(d) > 0) & (at.depth(d) < s))
                    def _():
                        self.copy(j, s, d, True).wait_send()

    def drain(self, j, events):
        at, n = self.at, self.at.n
        if events == 0:
            return
        for d in range(2):
            for s in range(max(events, 1), n):
                if s == events:
                    @pl.when(self.arrives(s, d))
                    def _():
                        self.arrival(j, s, d).wait_recv()
                else:
                    @pl.when(at.depth(d) == 1)
                    def _():
                        self.arrival(j, s, d).wait_recv()
        if events < n:
            self.sent(j, events)


class RingGather:
    def __init__(self, at, own, full, send, recv):
        self.at, self.own, self.full, self.send, self.recv = at, own, full, send, recv

    def copy(self, h, d):
        at = self.at
        way = 1 if d == 0 else -1
        owner = at.member(-way * (h - 1))
        rows = self.full.shape[1]
        part = pl.ds(0, rows)
        if h == at.ring // 2:
            part = pl.ds(d * (rows // 2), rows // 2)
        dst = self.full.at[owner, part]
        src = self.own.at[part] if h == 1 else dst
        return pltpu.make_async_remote_copy(
            src, dst, self.send.at[d, h - 1], self.recv.at[d, h - 1],
            device_id={"tensor": at.member(way)}, device_id_type=MESH)

    def start(self, h):
        for d in range(2):
            self.copy(h, d).start()

    def wait(self, h):
        for d in range(2):
            self.copy(h, d).wait_recv()

    def sent(self):
        for h in range(1, self.at.ring // 2 + 1):
            for d in range(2):
                self.copy(h, d).wait_send()


class SmallSum:
    def __init__(self, axis, me, size, part_of, land, send, recv):
        self.axis, self.me, self.size, self.part_of = axis, me, size, part_of
        self.land, self.send, self.recv = land, send, recv

    def copy(self, k):
        peer = (self.me + k) % self.size
        return pltpu.make_async_remote_copy(
            self.part_of(peer), self.land.at[k - 1], self.send.at[k - 1], self.recv.at[k - 1],
            device_id={self.axis: peer}, device_id_type=MESH)

    def total(self):
        for k in range(1, self.size):
            self.copy(k).start()
        result = self.part_of(self.me)[...]
        for k in range(1, self.size):
            self.copy(k).wait_recv()
            result = result + self.land[k - 1]
        for k in range(1, self.size):
            self.copy(k).wait_send()
        return result


class RingSum:
    def __init__(self, at, part, land, send, recv):
        self.at, self.part, self.land, self.send, self.recv = at, part, land, send, recv
        self.stages = at.ring // 2

    def rows_of(self, k, d):
        rows = self.part.shape[1]
        return pl.ds(d * (rows // 2), rows // 2) if k == 0 else pl.ds(0, rows)

    def target(self, k, d):
        return self.at.member((1 if d == 0 else -1) * (self.stages - k))

    def copy(self, k, d):
        r = self.rows_of(k, d)
        return pltpu.make_async_remote_copy(
            self.part.at[self.target(k, d), r], self.land.at[d, k, r],
            self.send.at[d, k], self.recv.at[d, k],
            device_id={"tensor": self.at.member(1 if d == 0 else -1)}, device_id_type=MESH)

    def start(self, k, d):
        self.copy(k, d).start()

    def add(self, k, d):
        self.copy(k, d).wait_recv()
        block = self.target(k + 1, d)
        rows = self.part.shape[1]
        half = rows // 2
        quarter = max(half // 4, 16)
        first = d * half if k == 0 else 0
        count = (half if k == 0 else rows) // quarter

        @pl.loop(0, count)
        def _(i):
            r = pl.ds(pl.multiple_of(first + i * quarter, quarter), quarter)
            self.part[block, r] = self.part[block, r] + self.land[d, k, r]

    def sent(self):
        for k in range(self.stages):
            for d in range(2):
                self.copy(k, d).wait_send()


def group_lanes(heads, width):
    return lax.broadcasted_iota(jnp.int32, (1, width), 1) // HEAD_DIM


def rope(values, cosine, sine, back=False):
    width = values.shape[-1]
    half = HEAD_DIM // 2
    first = lax.broadcasted_iota(jnp.int32, (1, width), 1) % HEAD_DIM < half
    ahead = pltpu.roll(values, width - half, 1)
    behind = pltpu.roll(values, half, 1)
    turned = jnp.where(first, -ahead, behind)
    return values * cosine - turned * sine if back else values * cosine + turned * sine


def inverse_rms(values):
    return lax.rsqrt(jnp.mean(values * values, axis=-1, keepdims=True) + norm_eps)


def causal_softmax(q_rows, keys, first_row):
    scores = dot_t(q_rows, keys) * HEAD_DIM ** (-0.5)
    row = first_row + lax.broadcasted_iota(jnp.int32, scores.shape, 0)
    column = lax.broadcasted_iota(jnp.int32, scores.shape, 1)
    scores = jnp.where(row >= column, scores, masked_score)
    exp_scores = jnp.exp(scores - jnp.max(scores, axis=-1, keepdims=True))
    return exp_scores * (1.0 / jnp.sum(exp_scores, axis=-1, keepdims=True))


def only(mask, values):
    return jnp.where(mask, values, jnp.zeros_like(values))


def forward_kernel(
    n, ring, pre, q_tile,
    tokens, cotangent, w_in, ff_in, cosine, sine,
    w_full, ff_full, normed_out, q_out, k_out, v_out, mixed_out, residual_out, x_full, dy_full,
    tok, wv, gains, q, k, v, mixed, acc, part, land, xrow, resid,
    a_send, a_recv, a_sib_send, a_sib_recv,
    f_send, f_recv, f_sib_send, f_sib_recv,
    t_send, t_recv, c_send, c_recv, x_send, x_recv, s_send, s_recv, io, load,
):
    at = Place(n, ring)
    groups, _, _, _, bs = w_full.shape
    local, width = tokens.shape
    rows = local * ring
    heads = bs // HEAD_DIM
    att = LineGather(at, w_full, a_send, a_recv, a_sib_send, a_sib_recv)
    feed = LineGather(at, ff_full, f_send, f_recv, f_sib_send, f_sib_recv)
    tok_ring = RingGather(at, tokens, tok, t_send, t_recv)
    cot_ring = RingGather(at, cotangent, dy_full, c_send, c_recv)
    x_ring = RingGather(at, xrow, x_full, x_send, x_recv)
    sums = RingSum(at, part, land, s_send, s_recv)

    own_tok = pltpu.make_async_copy(tokens, tok.at[at.t], io.at[0])
    cot_in = pltpu.make_async_copy(cotangent, xrow, io.at[1])
    own_cot = pltpu.make_async_copy(xrow, dy_full.at[at.t], io.at[1])
    own_tok.start()
    cot_in.start()
    at.barrier()

    def weights(index):
        return (att, index) if index < groups else (feed, index - groups)

    def half_tick(tick):
        for e in range(n - 1, -1, -1):
            if (tick - e) % 2 == 0 and 0 <= (tick - e) // 2 < groups + pre:
                line, a = weights((tick - e) // 2)
                line.event(a, e)

    def loads(g):
        return [
            pltpu.make_async_copy(w_full.at[g, :, :, pl.ds(i * bs, bs)], wv.at[i], load.at[i])
            for i in range(3)
        ]

    done = [0]

    def run_to(tick):
        while done[0] <= tick:
            half_tick(done[0])
            done[0] += 1

    run_to(0)
    tok_ring.start(1)
    run_to(1)
    tok_ring.wait(1)
    tok_ring.start(2)
    cot_in.wait()
    own_cot.start()
    run_to(2)
    for h in range(3, ring // 2 + 1):
        tok_ring.wait(h - 1)
        tok_ring.start(h)
    tok_ring.wait(ring // 2)
    cot_ring.start(1)
    run_to(n - 1)
    att.finish(0)
    gain_load = pltpu.make_async_copy(w_full.at[0, :, :, pl.ds(4 * bs, 16)], gains, load.at[4])
    gain_load.start()
    for copy in loads(0):
        copy.start()
    gain_load.wait()
    own_tok.wait()
    tok_ring.sent()

    def norm_into(values, scale, row, store):
        for i in range(2 * n):
            gain = gains[i // 2, i % 2, row : row + 1, :].astype(F32)
            cols = pl.ds(i * bs, bs)
            store(cols, (values(cols) * scale * gain).astype(BF16))

    norm_tile = min(64, local)

    @pl.loop(0, ring)
    def _(m):
        @pl.loop(0, local // norm_tile)
        def _(i):
            r = aligned(i, norm_tile)
            scale = inverse_rms(tok[m, r].astype(F32))

            def store(cols, value):
                tok[m, r, cols] = value

            norm_into(lambda cols: tok[m, r, cols].astype(F32), scale, 0, store)

    normed_store = pltpu.make_async_copy(tok, normed_out, io.at[2])
    normed_store.start()

    def project(g):
        cols = pl.ds(g * bs, bs)

        @pl.loop(0, ring)
        def _(m):
            r = aligned(m, local)
            x = tok[m]
            query = dot(x, wv[0].reshape(width, bs))
            key = dot(x, wv[1].reshape(width, bs))
            q[r, cols] = rope(query, cosine[r, :], sine[r, :]).astype(BF16)
            k[r, cols] = rope(key, cosine[r, :], sine[r, :]).astype(BF16)
            v[r, cols] = dot(x, wv[2].reshape(width, bs)).astype(BF16)

    def attend(g, between):
        cols = pl.ds(g * bs, bs)
        lanes = group_lanes(heads, bs)
        for i in range(rows // q_tile):
            r = pl.ds(i * q_tile, q_tile)
            keys = pl.ds(0, (i + 1) * q_tile)
            acc[...] = jnp.zeros_like(acc)

            @pl.loop(0, heads)
            def _(h):
                mask = lanes == h
                probs = causal_softmax(only(mask, q[r, cols]), k[keys, cols], i * q_tile)
                acc[...] += dot(probs.astype(BF16), only(mask, v[keys, cols]))

            mixed[r, cols] = acc[...].astype(BF16)
            between(i)

    def nothing(i):
        pass

    for copy in loads(0):
        copy.wait()
    project(0)
    run_to(n)
    cot_ring.wait(1)
    cot_ring.start(2)
    attend(0, nothing)
    for g in range(1, groups):
        run_to(2 * g + n - 1)
        att.finish(g)
        for copy in loads(g):
            copy.start()
        for copy in loads(g):
            copy.wait()
        project(g)
        run_to(2 * g + n)
        attend(g, nothing)
    for h in range(3, ring // 2 + 1):
        cot_ring.wait(h - 1)
        cot_ring.start(h)
    cot_ring.wait(ring // 2)
    stores = [
        pltpu.make_async_copy(ref, out, io.at[3 + i])
        for i, (ref, out) in enumerate(((q, q_out), (k, k_out), (v, v_out), (mixed, mixed_out)))
    ]
    for copy in stores:
        copy.start()
    out_loads = [
        pltpu.make_async_copy(w_full.at[g, :, :, pl.ds(3 * bs, bs)], wv.at[g], load.at[g])
        for g in range(groups)
    ]
    for copy in out_loads:
        copy.start()
    for copy in out_loads:
        copy.wait()

    def out_share(offset):
        m = at.member(offset)
        r = aligned(m, local)
        for b in range(n):
            block = sum(
                dot_t(mixed[r, g * bs : (g + 1) * bs], wv[g, b].reshape(2 * bs, bs))
                for g in range(groups)
            )
            part[m, :, b * 2 * bs : (b + 1) * 2 * bs] = block.astype(BF16)

    out_share(ring // 2)
    for d in range(2):
        sums.start(0, d)
    run_to(done[0])
    for kk in range(1, ring // 2):
        for d in range(2):
            out_share((1 if d == 0 else -1) * (ring // 2 - kk))
        for d in range(2):
            sums.add(kk - 1, d)
            sums.start(kk, d)
        run_to(done[0])
    out_share(0)
    own_cot.wait()
    own_again = pltpu.make_async_copy(tokens, xrow, io.at[7])
    own_again.start()
    own_again.wait()
    for d in range(2):
        sums.add(ring // 2 - 1, d)

    @pl.loop(0, local // norm_tile)
    def _(i):
        r = aligned(i, norm_tile)
        value = xrow[r].astype(F32) + part[at.t, r].astype(F32)
        resid[r] = value
        scale = inverse_rms(value)

        def store(cols, value):
            xrow[r, cols] = value

        norm_into(lambda cols: resid[r, cols], scale, 1, store)

    x_ring.start(1)
    own_x = pltpu.make_async_copy(xrow, x_full.at[at.t], io.at[0])
    resid_store = pltpu.make_async_copy(resid, residual_out, io.at[7])
    own_x.start()
    resid_store.start()
    run_to(done[0])
    for h in range(2, ring // 2 + 1):
        x_ring.wait(h - 1)
        x_ring.start(h)
        run_to(done[0])
    run_to(2 * (groups + pre - 1) + n - 1)
    x_ring.wait(ring // 2)
    for line in (cot_ring, x_ring):
        line.sent()
    sums.sent()
    for a in range(pre):
        feed.finish(a)
    for copy in (normed_store, own_x, resid_store, *stores):
        copy.wait()


def forward_part(n, ring, pre, tokens, cotangent, w_full, ff_full, cosine, sine, q_tile=256):
    groups, bs = w_full.shape[0], w_full.shape[-1]
    chunks = ff_full.shape[0]
    local, width = tokens.shape
    rows = local * ring
    cols = groups * bs
    any_ = pl.BlockSpec(memory_space=pl.ANY)
    vmem = pl.BlockSpec(memory_space=pltpu.VMEM)
    dma = pltpu.SemaphoreType.DMA
    shape = jax.ShapeDtypeStruct
    half = ring // 2
    return pl.pallas_call(
        functools.partial(forward_kernel, n, ring, pre, min(q_tile, rows)),
        out_shape=[
            shape(w_full.shape, BF16),
            shape(ff_full.shape, BF16),
            shape((ring, local, width), BF16),
            shape((rows, cols), BF16),
            shape((rows, cols), BF16),
            shape((rows, cols), BF16),
            shape((rows, cols), BF16),
            shape((local, width), F32),
            shape((ring, local, width), BF16),
            shape((ring, local, width), BF16),
        ],
        in_specs=[any_] * 4 + [vmem] * 2,
        out_specs=[any_] * 10,
        input_output_aliases={2: 0, 3: 1},
        scratch_shapes=[
            pltpu.VMEM((ring, local, width), BF16),
            pltpu.VMEM((max(4, groups), n, 2, bs, bs), BF16),
            pltpu.VMEM((n, 2, 16, bs), BF16),
            pltpu.VMEM((rows, cols), BF16),
            pltpu.VMEM((rows, cols), BF16),
            pltpu.VMEM((rows, cols), BF16),
            pltpu.VMEM((rows, cols), BF16),
            pltpu.VMEM((min(q_tile, rows), bs), F32),
            pltpu.VMEM((ring, local, width), BF16),
            pltpu.VMEM((2, half, local, width), BF16),
            pltpu.VMEM((local, width), BF16),
            pltpu.VMEM((local, width), F32),
            dma((2, n - 1, groups)), dma((2, n - 1, groups)),
            dma((groups,)), dma((groups,)),
            dma((2, n - 1, chunks)), dma((2, n - 1, chunks)),
            dma((chunks,)), dma((chunks,)),
            dma((2, half)), dma((2, half)), dma((2, half)), dma((2, half)),
            dma((2, half)), dma((2, half)), dma((2, half)), dma((2, half)),
            dma((8,)), dma((5,)),
        ],
        compiler_params=pltpu.CompilerParams(
            collective_id=1, has_side_effects=True, vmem_limit_bytes=56 * 2**20),
    )(tokens, cotangent, w_full, ff_full, cosine, sine)


def feed_kernel(
    n, ring, pre, cut, tile,
    w_in, x_hbm, dy_hbm,
    w_full, out_hbm, dn_hbm, summed, landed, result,
    x, dy, oacc, dacc, wv, pg, core_in, hid, dgate, dup, stage, got,
    g_send, g_recv, g_sib_send, g_sib_recv,
    r_send, r_recv, r_load, r_out, core_send, core_recv, store_sem, load_sem, io_sem,
):
    at = Place(n, ring)
    c = at.c
    chunks, _, _, unit, bs = w_full.shape
    rows, width = x.shape
    weights = LineGather(at, w_full, g_send, g_recv, g_sib_send, g_sib_recv)
    grads = LineSum(at, chunks, summed, landed, result, stage, got, r_send, r_recv, r_load, r_out)
    lag = max(0, n - pre)

    def loads(j):
        return [
            pltpu.make_async_copy(
                w_full.at[j, :, :, pl.ds(i * bs, bs)], wv.at[j % 2, i], load_sem.at[j % 2, i])
            for i in range(3)
        ]

    def core_copy(j):
        return pltpu.make_async_remote_copy(
            pg.at[1 - c], core_in.at[j % 2], core_send.at[j % 2], core_recv.at[j % 2],
            device_id={"dp": at.sib}, device_id_type=MESH)

    def store(j):
        return pltpu.make_async_copy(pg.at[c], summed.at[j], store_sem)

    x_in = pltpu.make_async_copy(x_hbm, x, io_sem.at[0])
    dy_in = pltpu.make_async_copy(dy_hbm, dy, io_sem.at[1])
    x_in.start()
    dy_in.start()
    if pre > 0:
        for copy in loads(0):
            copy.start()
    at.barrier(False)

    @pl.loop(0, rows // 64)
    def _(i):
        r = aligned(i, 64)
        oacc[r] = jnp.zeros((64, width), F32)
        dacc[r] = jnp.zeros((64, width), F32)

    x_in.wait()
    dy_in.wait()

    def weight_grads(cc):
        @pl.loop(0, n)
        def _(k):
            cols = aligned(2 * k + cc, bs)
            pg[cc, k, pl.ds(0, bs)] = t_dot(x[:, cols], dgate[...]).astype(BF16)
            pg[cc, k, pl.ds(bs, bs)] = t_dot(x[:, cols], dup[...]).astype(BF16)
            pg[cc, k, pl.ds(2 * bs, bs)] = t_dot(dy[:, cols], hid[...]).astype(BF16)

    def compute(j):
        slot = j % 2
        for copy in loads(j):
            copy.wait()

        @pl.when(j + 1 < pre)
        def _():
            for copy in loads(j + 1):
                copy.start()

        @pl.loop(0, rows // tile)
        def _(m):
            r = aligned(m, tile)
            gate = dot(x[r, :], wv[slot, 0].reshape(width, bs))
            up = dot(x[r, :], wv[slot, 1].reshape(width, bs))
            dh = dot(dy[r, :], wv[slot, 2].reshape(width, bs))
            s = jax.nn.sigmoid(gate)
            gs = gate * s
            hid[r, :] = (gs * up).astype(BF16)
            dup[r, :] = (dh * gs).astype(BF16)
            dgate[r, :] = (dh * up * (s + gs * (1 - s))).astype(BF16)

        weight_grads(1 - c)
        core_copy(j).start()

        @pl.loop(0, rows // tile)
        def _(m):
            r = aligned(m, tile)

            @pl.loop(0, n)
            def _(k):
                cols = aligned(k, 2 * bs)
                oacc[r, cols] += dot_t(hid[r, :], wv[slot, 2, k].reshape(2 * bs, bs))
                dacc[r, cols] += dot_t(dgate[r, :], wv[slot, 0, k].reshape(2 * bs, bs)) + dot_t(
                    dup[r, :], wv[slot, 1, k].reshape(2 * bs, bs))

        weight_grads(c)
        core_copy(j).wait_recv()

        @pl.loop(0, n)
        def _(k):
            pg[c, k] = pg[c, k] + core_in[slot, k]

        store(j).start()
        core_copy(j).wait_send()

    @pl.loop(0, lag + chunks)
    def _(step):
        for e in range(n - 1, -1, -1):
            a = pre + step - e

            @pl.when((a >= pre) & (a < chunks))
            def _():
                weights.event(a, e)

        j = step - lag

        @pl.when((j >= 1) & (j <= chunks))
        def _():
            store(j - 1).wait()

        tick = j - 1
        for e in range(n - 1, -1, -1):
            q = tick - e + 2 * n
            r = q // 2 - n

            @pl.when((q % 2 == 0) & (tick < cut) & (r >= 0) & (r < chunks))
            def _():
                grads.event(r, e)

        @pl.when((j >= 0) & (j < chunks))
        def _():
            compute(j)

        whole = pre + step - (n - 1)

        @pl.when((whole >= pre) & (whole < chunks))
        def _():
            weights.finish(whole)

        @pl.when((j + 1 >= pre) & (j + 1 >= 0) & (j + 1 < chunks))
        def _():
            for copy in loads(j + 1):
                copy.start()

    store(chunks - 1).wait()
    x[...] = oacc[...].astype(BF16)
    dy[...] = dacc[...].astype(BF16)
    x_out = pltpu.make_async_copy(x, out_hbm, io_sem.at[0])
    dy_out = pltpu.make_async_copy(dy, dn_hbm, io_sem.at[1])
    x_out.start()
    dy_out.start()
    for j in range(chunks):
        grads.drain(j, min(n, max(0, cut - 2 * j)))
    x_out.wait()
    dy_out.wait()


def feed_part(n, ring, pre, cut, w_full, x, dy, tile=512):
    chunks, _, _, unit, bs = w_full.shape
    rows, width = x.shape
    any_ = pl.BlockSpec(memory_space=pl.ANY)
    dma = pltpu.SemaphoreType.DMA
    shape = jax.ShapeDtypeStruct
    return pl.pallas_call(
        functools.partial(feed_kernel, n, ring, pre, cut, min(tile, rows)),
        out_shape=[
            shape(w_full.shape, BF16),
            shape((rows, width), BF16),
            shape((rows, width), BF16),
            shape((chunks, n, unit, bs), BF16),
            shape((2, chunks, n - 1, unit, bs), BF16),
            shape((chunks, unit, bs), BF16),
        ],
        in_specs=[any_] * 3,
        out_specs=[any_] * 6,
        input_output_aliases={0: 0},
        scratch_shapes=[
            pltpu.VMEM((rows, width), BF16),
            pltpu.VMEM((rows, width), BF16),
            pltpu.VMEM((rows, width), F32),
            pltpu.VMEM((rows, width), F32),
            pltpu.VMEM((2, 3, n, 2, bs, bs), BF16),
            pltpu.VMEM((2, n, unit, bs), BF16),
            pltpu.VMEM((2, n, unit, bs), BF16),
            pltpu.VMEM((rows, bs), BF16),
            pltpu.VMEM((rows, bs), BF16),
            pltpu.VMEM((rows, bs), BF16),
            pltpu.VMEM((2, n - 2, n // 2, unit, bs), BF16),
            pltpu.VMEM((3, unit, bs), BF16),
            dma((2, n - 1, chunks)), dma((2, n - 1, chunks)),
            dma((chunks,)), dma((chunks,)),
            dma((2, n - 1, chunks)), dma((2, n - 1, chunks)),
            dma((3,)), dma,
            dma((2,)), dma((2,)), dma, dma((2, 3)), dma((2,)),
        ],
        compiler_params=pltpu.CompilerParams(
            collective_id=2, has_side_effects=True, vmem_limit_bytes=60 * 2**20),
    )(w_full, x, dy)


def backward_kernel(
    n, ring, cut, q_tile,
    dn_in, out_in, residual, cotangent, tokens, normed_in, q_in, k_in, v_in, mixed_in,
    w_full, cosine, sine, ff_summed, ff_landed_in, ff_result_in,
    output, grad_tokens, gain_grads, ff_landed, ff_result, att_result, att_summed, att_landed,
    part, land, dres_full, normed, wv, gains, q, k, v, mixed, dmix, dq, dk, dv, dproj,
    resid, dres, small, lined, gsum, pg, core_in, ff_stage, att_stage, att_got,
    s1_send, s1_recv, s2_send, s2_recv, s3_send, s3_recv, x_send, x_recv, free_sem,
    f_send, f_recv, f_load, f_out, a_send, a_recv, a_load, a_out,
    core_send, core_recv, store_sem, io, load,
    gparts, gland, gsecond, gone, gtwo, g_send, g_recv, h_send, h_recv,
):
    at = Place(n, ring)
    c = at.c
    groups, _, _, _, bs = w_full.shape
    local, width = tokens.shape
    rows = local * ring
    heads = bs // HEAD_DIM
    chunks = ff_result.shape[0]
    half = ring // 2
    ff_got = att_got.at[:, pl.ds(0, ff_result.shape[1])]
    feed = LineSum(at, chunks, ff_summed, ff_landed, ff_result, ff_stage, ff_got,
                   f_send, f_recv, f_load, f_out)
    att = LineSum(at, groups, att_summed, att_landed, att_result, att_stage, att_got,
                  a_send, a_recv, a_load, a_out)
    sums1 = RingSum(at, part, land, s1_send, s1_recv)
    sums2 = RingSum(at, part, land, s2_send, s2_recv)
    sums3 = RingSum(at, part, land, s3_send, s3_recv)
    dres_ring = RingGather(at, dres_full.at[at.t], dres_full, x_send, x_recv)

    def fetch(src, dst, i):
        return pltpu.make_async_copy(src, dst, io.at[i])

    part_in = fetch(dn_in, part, 0)
    part_in.start()
    resid_in = fetch(residual, resid, 1)
    resid_in.start()
    cot_in = fetch(cotangent, lined, 2)
    cot_in.start()
    gains_in = fetch(w_full.at[0, :, :, pl.ds(4 * bs, 16)], gains, 3)
    gains_in.start()
    saved = [
        fetch(src, dst, 4 + i)
        for i, (src, dst) in enumerate(
            ((normed_in, normed), (q_in, q), (k_in, k), (v_in, v), (mixed_in, mixed)))
    ]
    for copy in saved:
        copy.start()
    at.barrier(with_all=True)

    done = [cut]
    last = 2 * (chunks - 1) + n - 1

    def feed_tick():
        tick = done[0]
        if tick > last:
            return
        for e in range(n - 1, -1, -1):
            if (tick - e) % 2 == 0 and 0 <= (tick - e) // 2 < chunks:
                j = (tick - e) // 2
                feed.event(j, e, min(n, max(0, cut - 2 * j)))
        done[0] += 1

    def gain_of(row, i):
        return gains[i // 2, i % 2, row : row + 1, :].astype(F32)

    tile = min(64, local)

    def norm_back(value_of, grad_of, row, emit):
        gsum[row : row + 1, :] = jnp.zeros((1, width), F32)

        @pl.loop(0, local // tile)
        def _(i):
            r = aligned(i, tile)
            value = value_of(r, pl.ds(0, width))
            scale = inverse_rms(value)
            inner = jnp.zeros((tile, 1), F32)
            for b in range(2 * n):
                cols = pl.ds(b * bs, bs)
                value = value_of(r, cols)
                grad = grad_of(r, cols)
                gsum[row : row + 1, cols] += jnp.sum(grad * value * scale, axis=0, keepdims=True)
                inner += jnp.sum(grad * gain_of(row, b) * value, axis=-1, keepdims=True)
            pull = scale * scale * scale * (inner / width)
            for b in range(2 * n):
                cols = pl.ds(b * bs, bs)
                emit(r, cols, scale * grad_of(r, cols) * gain_of(row, b) - value_of(r, cols) * pull)

    def ring_sum(sums, between):
        for kk in range(half):
            between()
            for d in range(2):
                sums.add(kk, d)
                if kk < half - 1:
                    sums.start(kk + 1, d)

    part_in.wait()
    for d in range(2):
        sums1.start(0, d)
    for copy in (resid_in, cot_in, gains_in):
        copy.wait()
    ring_sum(sums1, feed_tick)

    def emit_residual(r, cols, value):
        total = lined[r, cols].astype(F32) + value
        dres[r, cols] = total
        dres_full[at.t, r, cols] = total.astype(BF16)

    norm_back(lambda r, cols: resid[r, cols], lambda r, cols: part[at.t, r, cols].astype(F32),
              1, emit_residual)
    dres_ring.start(1)

    def loads(g):
        return [
            pltpu.make_async_copy(w_full.at[g, :, :, pl.ds(i * bs, bs)], wv.at[i, g], load.at[i, g])
            for i in range(4)
        ]

    for g in range(groups):
        for copy in loads(g):
            copy.start()
    sums1.sent()
    second_in = fetch(out_in, part, 1)
    second_in.start()
    for h in range(2, half + 1):
        feed_tick()
        dres_ring.wait(h - 1)
        dres_ring.start(h)
    feed_tick()
    second_in.wait()
    dres_ring.wait(half)
    for d in range(2):
        sums2.start(0, d)
    for copy in saved:
        copy.wait()
    for g in range(groups):
        for copy in loads(g):
            copy.wait()

    def core_copy(g):
        return pltpu.make_async_remote_copy(
            pg.at[1 - c], core_in.at[g], core_send.at[g], core_recv.at[g],
            device_id={"dp": at.sib}, device_id_type=MESH)

    def store(g):
        return pltpu.make_async_copy(pg.at[c], att_summed.at[g], store_sem)

    def attend_back(g, between):
        gcols = pl.ds(g * bs, bs)
        lanes = group_lanes(heads, bs)
        dk[...] = jnp.zeros_like(dk)
        dv[...] = jnp.zeros_like(dv)
        for i in range(rows // q_tile):
            r = pl.ds(i * q_tile, q_tile)
            keys = pl.ds(0, (i + 1) * q_tile)
            dq[r] = jnp.zeros((q_tile, bs), F32)

            @pl.loop(0, heads)
            def _(h):
                mask = lanes == h
                qh = only(mask, q[r, gcols])
                dmh = only(mask, dmix[r])
                probs = causal_softmax(qh, k[keys, gcols], i * q_tile)
                d_probs = dot_t(dmh, v[keys, gcols])
                inner = jnp.sum(d_probs * probs, axis=-1, keepdims=True)
                d_scores = (probs * (d_probs - inner)).astype(BF16)
                dq[r] += dot(d_scores, only(mask, k[keys, gcols]))
                dk[keys] += t_dot(d_scores, qh)
                dv[keys] += t_dot(probs.astype(BF16), dmh)

            between(i)

    def weight_grads(g, cc):
        gcols = pl.ds(g * bs, bs)

        @pl.loop(0, n)
        def _(b):
            cols = aligned(2 * b + cc, bs)
            x = normed[:, :, cols].reshape(rows, bs)
            for i in range(3):
                pg[cc, b, pl.ds(i * bs, bs)] = t_dot(
                    x, dproj[i, :, gcols]).astype(BF16)
            pg[cc, b, pl.ds(3 * bs, bs)] = t_dot(
                dres_full[:, :, cols].reshape(rows, bs), mixed[:, gcols]).astype(BF16)

    second = [0]

    def second_sum(i):
        if second[0] < half:
            kk = second[0]
            for d in range(2):
                sums2.add(kk, d)
                if kk < half - 1:
                    sums2.start(kk + 1, d)
            second[0] += 1

    def between(i):
        feed_tick()
        if i % 2 == 1:
            second_sum(i)

    for g in range(groups):
        gcols = pl.ds(g * bs, bs)

        @pl.loop(0, ring)
        def _(m):
            r = aligned(m, local)
            dmix[r] = dot(dres_full[m], wv[3, g].reshape(width, bs)).astype(BF16)

        attend_back(g, between)

        @pl.loop(0, ring)
        def _(m):
            r = aligned(m, local)
            for i, ref in enumerate((dq, dk)):
                value = ref[r] * HEAD_DIM ** (-0.5)
                dproj[i, r, gcols] = rope(value, cosine[r, :], sine[r, :], back=True).astype(BF16)
            dproj[2, r, gcols] = dv[r].astype(BF16)

        if g > 0:
            store(g - 1).wait()
            core_copy(g - 1).wait_send()
            att.event(g - 1, 0)
        weight_grads(g, 1 - c)
        core_copy(g).start()
        weight_grads(g, c)
        core_copy(g).wait_recv()

        @pl.loop(0, n)
        def _(b):
            pg[c, b] = pg[c, b] + core_in[g, b]

        store(g).start()

    while second[0] < half:
        second_sum(0)
    sums2.sent()

    @pl.loop(0, local // tile)
    def _(i):
        r = aligned(i, tile)
        lined[r] = (resid[r] + part[at.t, r].astype(F32)).astype(BF16)

    out_store = fetch(lined, output, 0)
    out_store.start()
    for way in (1, -1):
        pl.semaphore_signal(
            free_sem, inc=1, device_id={"tensor": at.member(way)}, device_id_type=MESH)
    store(groups - 1).wait()
    att.event(groups - 1, 0)

    def share(offset):
        m = at.member(offset)
        r = aligned(m, local)
        for b in range(n):
            block = sum(
                dot_t(dproj[i, r, g * bs : (g + 1) * bs], wv[i, g, b].reshape(2 * bs, bs))
                for i in range(3) for g in range(groups)
            )
            part[m, :, b * 2 * bs : (b + 1) * 2 * bs] = block.astype(BF16)

    share(half)
    pl.semaphore_wait(free_sem, 2)
    for d in range(2):
        sums3.start(0, d)
    while done[0] <= last:
        feed_tick()
    tok_in = fetch(tokens, small, 1)
    dres_ring.sent()
    tok_in.start()
    for kk in range(1, half):
        for d in range(2):
            share((1 if d == 0 else -1) * (half - kk))
        for d in range(2):
            sums3.add(kk - 1, d)
            sums3.start(kk, d)
        for g in range(groups):
            att.event(g, kk)
    share(0)
    for e in range(half, n):
        for g in range(groups):
            att.event(g, e)
    for d in range(2):
        sums3.add(half - 1, d)
    tok_in.wait()
    out_store.wait()

    def emit_tokens(r, cols, value):
        lined[r, cols] = (dres[r, cols] + value).astype(BF16)

    norm_back(lambda r, cols: small[r, cols].astype(F32),
              lambda r, cols: part[at.t, r, cols].astype(F32), 0, emit_tokens)
    token_store = fetch(lined, grad_tokens, 0)
    token_store.start()
    for b in range(2 * n):
        gparts[b, 0:2] = gsum[0:2, b * bs : (b + 1) * bs]
        gparts[b, 2:8] = jnp.zeros((6, bs), F32)
    over_dp = SmallSum("dp", 2 * at.z + c, 2 * n, lambda i: gparts.at[i], gland, g_send, g_recv)
    gone[...] = over_dp.total()
    over_ring = SmallSum("tensor", at.t, ring, lambda i: gone, gsecond, h_send, h_recv)
    gtwo[...] = over_ring.total()
    gain_store = fetch(gtwo, gain_grads, 1)
    gain_store.start()
    token_store.wait()
    gain_store.wait()
    sums3.sent()
    core_copy(groups - 1).wait_send()


def backward_part(
    n, ring, cut, dn, out, residual, cotangent, tokens, normed, q, k, v, mixed,
    w_full, cosine, sine, ff_summed, ff_landed, ff_result, q_tile=256,
):
    groups, _, _, _, bs = w_full.shape
    chunks, unit, _ = ff_result.shape
    local, width = tokens.shape
    rows = local * ring
    cols = groups * bs
    half = ring // 2
    any_ = pl.BlockSpec(memory_space=pl.ANY)
    vmem = pl.BlockSpec(memory_space=pltpu.VMEM)
    dma = pltpu.SemaphoreType.DMA
    shape = jax.ShapeDtypeStruct
    big = (ring, local, width)
    return pl.pallas_call(
        functools.partial(backward_kernel, n, ring, cut, min(q_tile, rows)),
        out_shape=[
            shape((local, width), BF16),
            shape((local, width), BF16),
            shape((8, bs), F32),
            shape(ff_landed.shape, BF16),
            shape(ff_result.shape, BF16),
            shape((groups, 4 * bs, bs), BF16),
            shape((groups, n, 4 * bs, bs), BF16),
            shape((2, groups, n - 1, 4 * bs, bs), BF16),
        ],
        in_specs=[any_] * 11 + [vmem] * 2 + [any_] * 3,
        out_specs=[any_] * 8,
        input_output_aliases={14: 3, 15: 4},
        scratch_shapes=[
            pltpu.VMEM(big, BF16),
            pltpu.VMEM((2, half, local, width), BF16),
            pltpu.VMEM(big, BF16),
            pltpu.VMEM(big, BF16),
            pltpu.VMEM((4, groups, n, 2, bs, bs), BF16),
            pltpu.VMEM((n, 2, 16, bs), BF16),
            pltpu.VMEM((rows, cols), BF16),
            pltpu.VMEM((rows, cols), BF16),
            pltpu.VMEM((rows, cols), BF16),
            pltpu.VMEM((rows, cols), BF16),
            pltpu.VMEM((rows, bs), BF16),
            pltpu.VMEM((rows, bs), F32),
            pltpu.VMEM((rows, bs), F32),
            pltpu.VMEM((rows, bs), F32),
            pltpu.VMEM((3, rows, cols), BF16),
            pltpu.VMEM((local, width), F32),
            pltpu.VMEM((local, width), F32),
            pltpu.VMEM((local, width), BF16),
            pltpu.VMEM((local, width), BF16),
            pltpu.VMEM((8, width), F32),
            pltpu.VMEM((2, n, 4 * bs, bs), BF16),
            pltpu.VMEM((groups, n, 4 * bs, bs), BF16),
            pltpu.VMEM((2, n - 2, n // 2, unit, bs), BF16),
            pltpu.VMEM((2, n - 2, n // 2, 4 * bs, bs), BF16),
            pltpu.VMEM((3, 4 * bs, bs), BF16),
            dma((2, half)), dma((2, half)), dma((2, half)), dma((2, half)),
            dma((2, half)), dma((2, half)), dma((2, half)), dma((2, half)),
            pltpu.SemaphoreType.REGULAR,
            dma((2, n - 1, chunks)), dma((2, n - 1, chunks)), dma((3,)), dma,
            dma((2, n - 1, groups)), dma((2, n - 1, groups)), dma((3,)), dma,
            dma((groups,)), dma((groups,)), dma, dma((9,)), dma((4, groups)),
            pltpu.VMEM((2 * n, 8, bs), F32),
            pltpu.VMEM((2 * n - 1, 8, bs), F32),
            pltpu.VMEM((ring - 1, 8, bs), F32),
            pltpu.VMEM((8, bs), F32),
            pltpu.VMEM((8, bs), F32),
            dma((2 * n - 1,)), dma((2 * n - 1,)), dma((ring - 1,)), dma((ring - 1,)),
        ],
        compiler_params=pltpu.CompilerParams(
            collective_id=3, has_side_effects=True, vmem_limit_bytes=63 * 2**20),
    )(dn, out, residual, cotangent, tokens, normed, q, k, v, mixed,
      w_full, cosine, sine, ff_summed, ff_landed, ff_result)


PREFETCH = 4
CUT = 6


def pack_kernel(place, q, k, v, o, gain_attn, gain_mlp, gate, up, down, att, ff):
    bs = q.shape[0]
    for i, ref in enumerate((q, k, v)):
        att[i * bs : (i + 1) * bs] = ref[...]
    att[3 * bs : 4 * bs] = o[...].T
    row = lax.broadcasted_iota(jnp.int32, (16, bs), 0)
    first, second = (g[...].astype(F32) for g in (gain_attn, gain_mlp))
    gains = jnp.where(row == 0, first, jnp.where(row == 1, second, 0.0))
    att[4 * bs : 4 * bs + 16] = gains.astype(BF16)
    ff[0:bs] = gate[...]
    ff[bs : 2 * bs] = up[...]
    ff[2 * bs : 3 * bs] = down[...].T


def pack(w_query, w_key, w_value, w_out, gain_attn, gain_mlp, w_gate, w_up, w_down):
    bs = w_query.shape[0]
    n = lax.axis_size("dp") // 2
    groups, chunks = w_query.shape[1] // bs, w_gate.shape[1] // bs

    def at_group(j):
        return jnp.minimum(j, groups - 1)

    col = pl.BlockSpec((bs, bs), lambda j, p: (0, at_group(j)))
    row = pl.BlockSpec((bs, bs), lambda j, p: (at_group(j), 0))
    gain = pl.BlockSpec((1, bs), lambda j, p: (0, 0))
    wide = pl.BlockSpec((bs, bs), lambda j, p: (0, j))
    tall = pl.BlockSpec((bs, bs), lambda j, p: (j, 0))
    return pl.pallas_call(
        pack_kernel,
        out_shape=[
            jax.ShapeDtypeStruct((groups, n, 2, 4 * bs + 16, bs), BF16),
            jax.ShapeDtypeStruct((chunks, n, 2, 3 * bs, bs), BF16),
        ],
        grid_spec=pltpu.PrefetchScalarGridSpec(
            num_scalar_prefetch=1,
            grid=(chunks,),
            in_specs=[col, col, col, row, gain, gain, wide, wide, tall],
            out_specs=[
                pl.BlockSpec((None, None, None, 4 * bs + 16, bs),
                             lambda j, p: (at_group(j), p[0], p[1], 0, 0)),
                pl.BlockSpec((None, None, None, 3 * bs, bs), lambda j, p: (j, p[0], p[1], 0, 0)),
            ],
        ),
    )(jnp.stack([lax.axis_index("dp") // 2, lax.axis_index("dp") % 2]),
      w_query, w_key, w_value, w_out, gain_attn.reshape(1, bs), gain_mlp.reshape(1, bs),
      w_gate, w_up, w_down)


def unpack_kernel(att, ff, q, k, v, o, gate, up, down):
    bs = q.shape[0]
    for i, ref in enumerate((q, k, v)):
        ref[...] = att[0, i * bs : (i + 1) * bs].astype(F32)
    o[...] = att[0, 3 * bs : 4 * bs].astype(F32).T
    gate[...] = ff[0, 0:bs].astype(F32)
    up[...] = ff[0, bs : 2 * bs].astype(F32)
    down[...] = ff[0, 2 * bs : 3 * bs].astype(F32).T


def unpack(att, ff):
    groups, chunks, bs = att.shape[0], ff.shape[0], ff.shape[2]

    def at_group(j):
        return jnp.minimum(j, groups - 1)

    shape = jax.ShapeDtypeStruct
    col = pl.BlockSpec((bs, bs), lambda j: (0, at_group(j)))
    row = pl.BlockSpec((bs, bs), lambda j: (at_group(j), 0))
    wide = pl.BlockSpec((bs, bs), lambda j: (0, j))
    tall = pl.BlockSpec((bs, bs), lambda j: (j, 0))
    return pl.pallas_call(
        unpack_kernel,
        grid=(chunks,),
        out_shape=[shape((bs, groups * bs), F32)] * 3 + [shape((groups * bs, bs), F32)]
        + [shape((bs, chunks * bs), F32)] * 2 + [shape((chunks * bs, bs), F32)],
        in_specs=[
            pl.BlockSpec((1, 4 * bs, bs), lambda j: (at_group(j), 0, 0)),
            pl.BlockSpec((1, 3 * bs, bs), lambda j: (j, 0, 0)),
        ],
        out_specs=[col] * 3 + [row] + [wide] * 2 + [tall],
    )(att, ff)


def rotary_tables(row_count, width):
    frequency = rope_base ** (-np.arange(HEAD_DIM // 2) * 2.0 / HEAD_DIM)
    angles = (np.arange(row_count) % LEN)[:, None] * frequency[None, :]
    angles = np.tile(angles, (1, width // (HEAD_DIM // 2)))
    return np.cos(angles).astype(np.float32), np.sin(angles).astype(np.float32)


def shards(
    tokens, gain_attn, w_query, w_key, w_value, w_out, gain_mlp, w_gate, w_up, w_down, cotangent
):
    dp, ring = lax.axis_size("dp"), lax.axis_size("tensor")
    n = dp // 2
    local, width = tokens.shape
    rows = local * ring
    assert rows == LEN
    bs = w_query.shape[0]
    cosine, sine = rotary_tables(rows, bs)
    w_start, ff_start = pack(
        w_query, w_key, w_value, w_out, gain_attn, gain_mlp, w_gate, w_up, w_down
    )
    w_full, ff_full, normed, q, k, v, mixed, residual, x, dy = forward_part(
        n, ring, PREFETCH, tokens, cotangent, w_start, ff_start, cosine, sine
    )
    _, out, dn, summed, landed, result = feed_part(
        n, ring, PREFETCH, CUT, ff_full, x.reshape(rows, width), dy.reshape(rows, width)
    )
    output, grad_tokens, gain_grads, _, ff_grads, att_grads, _, _ = backward_part(
        n, ring, CUT, dn.reshape(x.shape), out.reshape(x.shape), residual, cotangent, tokens,
        normed, q, k, v, mixed, w_full, cosine, sine, summed, landed, result,
    )
    g_query, g_key, g_value, g_out, g_gate, g_up, g_down = unpack(att_grads, ff_grads)
    return (
        output,
        grad_tokens,
        gain_grads[0],
        g_query,
        g_key,
        g_value,
        g_out,
        gain_grads[1],
        g_gate,
        g_up,
        g_down,
    )


def solution(mesh):
    placed = (
        P(("dp", "tensor"), None),
        P("dp"),
        P("dp", "tensor"),
        P("dp", "tensor"),
        P("dp", "tensor"),
        P("tensor", "dp"),
        P("dp"),
        P("dp", "tensor"),
        P("dp", "tensor"),
        P("tensor", "dp"),
        P(("dp", "tensor"), None),
    )
    return jax.shard_map(
        shards,
        mesh=mesh,
        in_specs=placed,
        out_specs=(
            P(("dp", "tensor"), None),
            P(("dp", "tensor"), None),
            P("dp"),
            P("dp", "tensor"),
            P("dp", "tensor"),
            P("dp", "tensor"),
            P("tensor", "dp"),
            P("dp"),
            P("dp", "tensor"),
            P("dp", "tensor"),
            P("tensor", "dp"),
        ),
        check_vma=False,
    )
```

```python
import functools

import jax
import jax.numpy as jnp
import numpy as np
from jax import lax
from jax.experimental import pallas as pl
from jax.experimental.pallas import tpu as pltpu
from jax.sharding import PartitionSpec as P

HEAD_DIM = 64
LEN = 1024
MESH = pl.DeviceIdType.MESH
BF16 = jnp.bfloat16
F32 = jnp.float32

norm_eps = 1e-05
rope_base = 130000.0
masked_score = -1e30


def dot(a, b):
    return jnp.dot(a, b, preferred_element_type=F32)


def dot_t(a, b):
    return lax.dot_general(a, b, (((1,), (1,)), ((), ())), preferred_element_type=F32)


def t_dot(a, b):
    return lax.dot_general(a, b, (((0,), (0,)), ((), ())), preferred_element_type=F32)


def aligned(index, size):
    return pl.ds(pl.multiple_of(index * size, size), size)


class Place:
    def __init__(self, n, ring):
        me = lax.axis_index("dp")
        self.n, self.ring = n, ring
        self.z, self.c = me // 2, me % 2
        self.right, self.left = me + 2, me - 2
        self.sib = me + 1 - 2 * self.c
        self.has_r, self.has_l = self.z < n - 1, self.z > 0
        t = lax.axis_index("tensor")
        odd = t % 2
        self.t = t
        self.p = (1 - odd) * (t // 2) + odd * (ring - 1 - t // 2)

    def member(self, offset):
        p = (self.p + offset + self.ring) % self.ring
        back = (p >= self.ring // 2).astype(jnp.int32)
        return (1 - back) * (2 * p) + back * (2 * (self.ring - 1 - p) + 1)

    def barrier(self, with_ring=True, with_all=False):
        sem = pltpu.get_barrier_semaphore()

        def greet(peer):
            pl.semaphore_signal(sem, inc=1, device_id=peer, device_id_type=MESH)

        if with_all:
            for k in range(1, 2 * self.n):
                greet({"dp": (2 * self.z + self.c + k) % (2 * self.n)})
            for k in range(1, self.ring):
                greet({"tensor": (self.t + k) % self.ring})
            pl.semaphore_wait(sem, 2 * self.n - 1 + self.ring - 1)
            return

        greet({"dp": self.sib})
        if with_ring:
            greet({"tensor": self.member(1)})
            greet({"tensor": self.member(-1)})

        @pl.when(self.has_r)
        def _():
            greet({"dp": self.right})

        @pl.when(self.has_l)
        def _():
            greet({"dp": self.left})

        peers = self.has_r.astype(jnp.int32) + self.has_l.astype(jnp.int32)
        pl.semaphore_wait(sem, peers + (3 if with_ring else 1))

    def neighbour(self, d):
        return self.right if d == 0 else self.left

    def sends_to(self, d):
        return self.has_r if d == 0 else self.has_l

    def along(self, d, k):
        return self.z + k if d == 0 else self.z - k

    def depth(self, d):
        return self.z if d == 0 else self.n - 1 - self.z


class LineGather:
    def __init__(self, at, full, send, recv, sib_send, sib_recv):
        self.at, self.full = at, full
        self.send, self.recv = send, recv
        self.sib_send, self.sib_recv = sib_send, sib_recv

    def hop(self, a, h, d):
        at = self.at
        block = self.full.at[a, at.along(d, 1 - h), at.c]
        return pltpu.make_async_remote_copy(
            block, block, self.send.at[d, h - 1, a], self.recv.at[d, h - 1, a],
            device_id={"dp": at.neighbour(d)}, device_id_type=MESH)

    def sends(self, h, d):
        return self.at.sends_to(d) & (self.at.depth(d) >= h - 1)

    def arrives(self, h, d):
        return self.at.depth(d) >= h

    def to_sib(self, a):
        part = self.full.at[a, :, self.at.c]
        return pltpu.make_async_remote_copy(
            part, part, self.sib_send.at[a], self.sib_recv.at[a],
            device_id={"dp": self.at.sib}, device_id_type=MESH)

    def event(self, a, e):
        n = self.at.n
        for d in range(2):
            if e > 0:
                @pl.when(self.arrives(e, d))
                def _():
                    self.hop(a, e, d).wait_recv()

            if e < n - 1:
                @pl.when(self.sends(e + 1, d))
                def _():
                    self.hop(a, e + 1, d).start()

        if e == n - 1:
            self.to_sib(a).start()

    def finish(self, a):
        self.to_sib(a).wait_recv()
        self.to_sib(a).wait_send()
        for h in range(1, self.at.n):
            for d in range(2):
                @pl.when(self.sends(h, d))
                def _():
                    self.hop(a, h, d).wait_send()


class LineSum:
    def __init__(self, at, chunks, sums, land, out, stage, got, total, send, recv, load, out_sem):
        self.at, self.chunks = at, chunks
        self.sums, self.land, self.out = sums, land, out
        self.stage, self.got, self.total = stage, got, total
        self.send, self.recv, self.load, self.out_sem = send, recv, load, out_sem

    def valid(self, j):
        return (j >= 0) & (j < self.chunks)

    def copy(self, j, s, d, staged):
        at = self.at
        src = self.stage.at[d, s - 2, j % (at.n // 2)] if staged else self.sums.at[j, at.along(d, at.n - s)]
        return pltpu.make_async_remote_copy(
            src, self.land.at[d, j, s - 1], self.send.at[d, s - 1, j], self.recv.at[d, s - 1, j],
            device_id={"dp": at.neighbour(d)}, device_id_type=MESH)

    def arrival(self, j, s, d):
        return pltpu.make_async_remote_copy(
            self.land.at[d, j, s - 1], self.land.at[d, j, s - 1],
            self.send.at[d, s - 1, j], self.recv.at[d, s - 1, j],
            device_id={"dp": self.at.sib}, device_id_type=MESH)

    def arrives(self, s, d):
        depth = self.at.depth(d)
        return (depth > 0) & (depth <= s)

    def get(self, src, k):
        return pltpu.make_async_copy(src, self.got.at[k], self.load.at[k])

    def event(self, j, e):
        at, n = self.at, self.at.n
        if e == 0:
            for s in range(1, n):
                for d in range(2):
                    @pl.when(at.sends_to(d) & (at.depth(d) == 0))
                    def _():
                        self.copy(j, s, d, False).start()

        elif e < n - 1:
            s = e + 1
            here = [at.sends_to(d) & (at.depth(d) > 0) & (at.depth(d) < s) for d in range(2)]

            def own(d):
                return self.get(self.sums.at[j, at.along(d, n - s)], d)

            def came(d):
                return self.get(self.land.at[d, j, s - 2], 2 + d)

            for d in range(2):
                @pl.when(here[d])
                def _():
                    own(d).start()

            for d in range(2):
                @pl.when(here[d])
                def _():
                    self.arrival(j, s - 1, d).wait_recv()
                    came(d).start()

            for d in range(2):
                @pl.when(here[d])
                def _():
                    own(d).wait()
                    came(d).wait()
                    self.stage[d, s - 2, j % (n // 2)] = self.got[d] + self.got[2 + d]
                    self.copy(j, s, d, True).start()
        else:
            own = self.get(self.sums.at[j, at.z], 0)
            own.start()

            @pl.when(j > 0)
            def _():
                self.result(j - 1).wait()

            for d in range(2):
                @pl.when(at.depth(d) > 0)
                def _():
                    self.arrival(j, n - 1, d).wait_recv()
                    self.get(self.land.at[d, j, n - 2], 2 + d).start()

            own.wait()

            @pl.when(at.depth(0) == 0)
            def _():
                self.get(self.land.at[1, j, n - 2], 3).wait()
                self.total[...] = self.got[0] + self.got[3]

            @pl.when(at.depth(1) == 0)
            def _():
                self.get(self.land.at[0, j, n - 2], 2).wait()
                self.total[...] = self.got[0] + self.got[2]

            @pl.when((at.depth(0) > 0) & (at.depth(1) > 0))
            def _():
                for d in range(2):
                    self.get(self.land.at[d, j, n - 2], 2 + d).wait()
                self.total[...] = self.got[0] + self.got[2] + self.got[3]

            self.result(j).start()
            self.sent(j)

    def result(self, j):
        return pltpu.make_async_copy(self.total, self.out.at[j], self.out_sem)

    def sent(self, j):
        at, n = self.at, self.at.n
        for s in range(1, n):
            for d in range(2):
                @pl.when(at.sends_to(d) & (at.depth(d) == 0))
                def _():
                    self.copy(j, s, d, False).wait_send()

                if s >= 2:
                    @pl.when(at.sends_to(d) & (at.depth(d) > 0) & (at.depth(d) < s))
                    def _():
                        self.copy(j, s, d, True).wait_send()


class RingGather:
    def __init__(self, at, own, full, send, recv):
        self.at, self.own, self.full, self.send, self.recv = at, own, full, send, recv

    def copy(self, h, d):
        at = self.at
        way = 1 if d == 0 else -1
        owner = at.member(-way * (h - 1))
        rows = self.full.shape[1]
        part = pl.ds(0, rows)
        if h == at.ring // 2:
            part = pl.ds(d * (rows // 2), rows // 2)
        dst = self.full.at[owner, part]
        src = self.own.at[part] if h == 1 else dst
        return pltpu.make_async_remote_copy(
            src, dst, self.send.at[d, h - 1], self.recv.at[d, h - 1],
            device_id={"tensor": at.member(way)}, device_id_type=MESH)

    def start(self, h):
        for d in range(2):
            self.copy(h, d).start()

    def wait(self, h):
        for d in range(2):
            self.copy(h, d).wait_recv()

    def sent(self):
        for h in range(1, self.at.ring // 2 + 1):
            for d in range(2):
                self.copy(h, d).wait_send()


class SmallSum:
    def __init__(self, axis, me, size, part_of, land, send, recv):
        self.axis, self.me, self.size, self.part_of = axis, me, size, part_of
        self.land, self.send, self.recv = land, send, recv

    def copy(self, k):
        peer = (self.me + k) % self.size
        return pltpu.make_async_remote_copy(
            self.part_of(peer), self.land.at[k - 1], self.send.at[k - 1], self.recv.at[k - 1],
            device_id={self.axis: peer}, device_id_type=MESH)

    def total(self):
        for k in range(1, self.size):
            self.copy(k).start()
        result = self.part_of(self.me)[...]
        for k in range(1, self.size):
            self.copy(k).wait_recv()
            result = result + self.land[k - 1]
        for k in range(1, self.size):
            self.copy(k).wait_send()
        return result


class SmallGather:
    def __init__(self, axis, me, size, own, full, send, recv):
        self.axis, self.me, self.size, self.own, self.full = axis, me, size, own, full
        self.send, self.recv = send, recv

    def copy(self, k, slot):
        return pltpu.make_async_remote_copy(
            self.own, self.full.at[slot], self.send.at[k - 1], self.recv.at[k - 1],
            device_id={self.axis: (self.me + k) % self.size}, device_id_type=MESH)

    def start(self):
        for k in range(1, self.size):
            self.copy(k, self.me).start()

    def wait(self):
        for k in range(1, self.size):
            self.copy(k, (self.me + self.size - k) % self.size).wait_recv()
        for k in range(1, self.size):
            self.copy(k, self.me).wait_send()


class RingSum:
    def __init__(self, at, part, land, send, recv):
        self.at, self.part, self.land, self.send, self.recv = at, part, land, send, recv
        self.stages = at.ring // 2

    def rows_of(self, k, d):
        rows = self.part.shape[1]
        return pl.ds(d * (rows // 2), rows // 2) if k == 0 else pl.ds(0, rows)

    def target(self, k, d):
        return self.at.member((1 if d == 0 else -1) * (self.stages - k))

    def copy(self, k, d):
        r = self.rows_of(k, d)
        return pltpu.make_async_remote_copy(
            self.part.at[self.target(k, d), r], self.land.at[d, k, r],
            self.send.at[d, k], self.recv.at[d, k],
            device_id={"tensor": self.at.member(1 if d == 0 else -1)}, device_id_type=MESH)

    def start(self, k, d):
        self.copy(k, d).start()

    def add(self, k, d):
        self.copy(k, d).wait_recv()
        block = self.target(k + 1, d)
        rows = self.part.shape[1]
        half = rows // 2
        quarter = max(half // 4, 16)
        first = d * half if k == 0 else 0
        count = (half if k == 0 else rows) // quarter

        @pl.loop(0, count)
        def _(i):
            r = pl.ds(pl.multiple_of(first + i * quarter, quarter), quarter)
            self.part[block, r] = self.part[block, r] + self.land[d, k, r]

    def sent(self):
        for k in range(self.stages):
            for d in range(2):
                self.copy(k, d).wait_send()


def group_lanes(heads, width):
    return lax.broadcasted_iota(jnp.int32, (1, width), 1) // HEAD_DIM


def rope(values, cosine, sine, back=False):
    width = values.shape[-1]
    half = HEAD_DIM // 2
    first = lax.broadcasted_iota(jnp.int32, (1, width), 1) % HEAD_DIM < half
    ahead = pltpu.roll(values, width - half, 1)
    behind = pltpu.roll(values, half, 1)
    turned = jnp.where(first, -ahead, behind)
    return values * cosine - turned * sine if back else values * cosine + turned * sine


def inverse_rms(values):
    return lax.rsqrt(jnp.mean(values * values, axis=-1, keepdims=True) + norm_eps)


def causal_softmax(q_rows, keys, first_row):
    scores = dot_t(q_rows, keys) * HEAD_DIM ** (-0.5)
    row = first_row + lax.broadcasted_iota(jnp.int32, scores.shape, 0)
    column = lax.broadcasted_iota(jnp.int32, scores.shape, 1)
    scores = jnp.where(row >= column, scores, masked_score)
    exp_scores = jnp.exp(scores - jnp.max(scores, axis=-1, keepdims=True))
    return exp_scores * (1.0 / jnp.sum(exp_scores, axis=-1, keepdims=True))


def only(mask, values):
    return jnp.where(mask, values, jnp.zeros_like(values))


def forward_kernel(
    n, ring, pre, q_tile,
    tokens, cotangent, w_in, ff_in, cosine, sine,
    w_full, ff_full, normed_out, q_out, k_out, v_out, mixed_out, residual_out, x_full, dy_full,
    tok, wv, gains, q, k, v, mixed, acc, part, land, xrow, resid,
    a_send, a_recv, a_sib_send, a_sib_recv,
    f_send, f_recv, f_sib_send, f_sib_recv,
    t_send, t_recv, c_send, c_recv, x_send, x_recv, s_send, s_recv, io, load, gain_send, gain_recv,
):
    at = Place(n, ring)
    groups, _, _, _, bs = w_full.shape
    local, width = tokens.shape
    rows = local * ring
    heads = bs // HEAD_DIM
    att = LineGather(at, w_full, a_send, a_recv, a_sib_send, a_sib_recv)
    feed = LineGather(at, ff_full, f_send, f_recv, f_sib_send, f_sib_recv)
    tok_ring = RingGather(at, tokens, tok, t_send, t_recv)
    cot_ring = RingGather(at, cotangent, dy_full, c_send, c_recv)
    x_ring = RingGather(at, xrow, x_full, x_send, x_recv)
    sums = RingSum(at, part, land, s_send, s_recv)

    own_tok = pltpu.make_async_copy(tokens, tok.at[at.t], io.at[0])
    cot_in = pltpu.make_async_copy(cotangent, xrow, io.at[1])
    own_cot = pltpu.make_async_copy(xrow, dy_full.at[at.t], io.at[1])
    gain_in = pltpu.make_async_copy(
        w_full.at[0, at.z, at.c, pl.ds(4 * bs, 16)], gains.at[2 * at.z + at.c], io.at[2])
    own_tok.start()
    cot_in.start()
    gain_in.start()
    at.barrier(with_all=True)
    gain_all = SmallGather(
        "dp", 2 * at.z + at.c, 2 * n, gains.at[2 * at.z + at.c], gains, gain_send, gain_recv)

    first = (pre + 1) // 2
    batches = [[(att, g)] for g in range(groups)]
    for lot in (range(first), range(first, pre)):
        if len(lot):
            batches.append([(feed, a) for a in lot])

    def event(b, e):
        if b < len(batches):
            for line, a in batches[b]:
                line.event(a, e)

    def loads(g):
        return [
            pltpu.make_async_copy(w_full.at[g, :, :, pl.ds(i * bs, bs)], wv.at[i], load.at[i])
            for i in range(3)
        ]

    for g in range(groups):
        event(g, 0)
    tok_ring.start(1)
    gain_in.wait()
    gain_all.start()
    for g in range(groups):
        event(g, 1)
    cot_in.wait()
    own_cot.start()
    tok_ring.wait(1)
    tok_ring.start(2)
    event(0, 2)
    for h in range(3, ring // 2 + 1):
        tok_ring.wait(h - 1)
        tok_ring.start(h)
    tok_ring.wait(ring // 2)
    cot_ring.start(1)
    gain_all.wait()
    own_tok.wait()
    tok_ring.sent()

    def norm_into(values, scale, row, store):
        for i in range(2 * n):
            gain = gains[i, row : row + 1, :].astype(F32)
            cols = pl.ds(i * bs, bs)
            store(cols, (values(cols) * scale * gain).astype(BF16))

    norm_tile = min(64, local)

    @pl.loop(0, ring)
    def _(m):
        @pl.loop(0, local // norm_tile)
        def _(i):
            r = aligned(i, norm_tile)
            scale = inverse_rms(tok[m, r].astype(F32))

            def store(cols, value):
                tok[m, r, cols] = value

            norm_into(lambda cols: tok[m, r, cols].astype(F32), scale, 0, store)

    normed_store = pltpu.make_async_copy(tok, normed_out, io.at[2])
    normed_store.start()

    def project(g):
        cols = pl.ds(g * bs, bs)

        @pl.loop(0, ring)
        def _(m):
            r = aligned(m, local)
            x = tok[m]
            query = dot(x, wv[0].reshape(width, bs))
            key = dot(x, wv[1].reshape(width, bs))
            q[r, cols] = rope(query, cosine[r, :], sine[r, :]).astype(BF16)
            k[r, cols] = rope(key, cosine[r, :], sine[r, :]).astype(BF16)
            v[r, cols] = dot(x, wv[2].reshape(width, bs)).astype(BF16)

    def attend(g, between):
        cols = pl.ds(g * bs, bs)
        lanes = group_lanes(heads, bs)
        for i in range(rows // q_tile):
            r = pl.ds(i * q_tile, q_tile)
            keys = pl.ds(0, (i + 1) * q_tile)
            acc[...] = jnp.zeros_like(acc)

            @pl.loop(0, heads)
            def _(h):
                mask = lanes == h
                probs = causal_softmax(only(mask, q[r, cols]), k[keys, cols], i * q_tile)
                acc[...] += dot(probs.astype(BF16), only(mask, v[keys, cols]))

            mixed[r, cols] = acc[...].astype(BF16)
            between(i)

    for e in range(2, n - 1):
        for g in range(groups):
            if (g, e) != (0, 2):
                event(g, e)
    for b in range(groups, len(batches)):
        event(b, 0)
    def fetch(g):
        att.finish(g)
        for copy in loads(g):
            copy.start()

    event(0, n - 1)
    fetch(0)
    for g in range(groups):
        for copy in loads(g):
            copy.wait()
        project(g)
        if g == 0:
            cot_ring.wait(1)
            cot_ring.start(2)
        if g + 1 < groups:
            event(g + 1, n - 1)

        def between(i):
            if i == 1 and g + 1 < groups:
                fetch(g + 1)

        attend(g, between)
    for h in range(3, ring // 2 + 1):
        cot_ring.wait(h - 1)
        cot_ring.start(h)
    cot_ring.wait(ring // 2)
    stores = [
        pltpu.make_async_copy(ref, out, io.at[3 + i])
        for i, (ref, out) in enumerate(((q, q_out), (k, k_out), (v, v_out), (mixed, mixed_out)))
    ]
    for copy in stores:
        copy.start()
    out_loads = [
        pltpu.make_async_copy(w_full.at[g, :, :, pl.ds(3 * bs, bs)], wv.at[g], load.at[g])
        for g in range(groups)
    ]
    for copy in out_loads:
        copy.start()
    for copy in out_loads:
        copy.wait()

    def out_share(offset):
        m = at.member(offset)
        r = aligned(m, local)
        for b in range(n):
            block = sum(
                dot_t(mixed[r, g * bs : (g + 1) * bs], wv[g, b].reshape(2 * bs, bs))
                for g in range(groups)
            )
            part[m, :, b * 2 * bs : (b + 1) * 2 * bs] = block.astype(BF16)

    moves = [(b, e) for e in range(1, n) for b in range(groups, len(batches))]

    def move():
        if moves:
            event(*moves.pop(0))

    out_share(ring // 2)
    for d in range(2):
        sums.start(0, d)
    for kk in range(1, ring // 2):
        for d in range(2):
            out_share((1 if d == 0 else -1) * (ring // 2 - kk))
        move()
        for d in range(2):
            sums.add(kk - 1, d)
            sums.start(kk, d)
    out_share(0)
    move()
    own_cot.wait()
    own_again = pltpu.make_async_copy(tokens, xrow, io.at[7])
    own_again.start()
    own_again.wait()
    for d in range(2):
        sums.add(ring // 2 - 1, d)

    @pl.loop(0, local // norm_tile)
    def _(i):
        r = aligned(i, norm_tile)
        value = xrow[r].astype(F32) + part[at.t, r].astype(F32)
        resid[r] = value
        scale = inverse_rms(value)

        def store(cols, value):
            xrow[r, cols] = value

        norm_into(lambda cols: resid[r, cols], scale, 1, store)

    x_ring.start(1)
    own_x = pltpu.make_async_copy(xrow, x_full.at[at.t], io.at[0])
    resid_store = pltpu.make_async_copy(resid, residual_out, io.at[7])
    own_x.start()
    resid_store.start()
    move()
    for h in range(2, ring // 2 + 1):
        move()
        x_ring.wait(h - 1)
        x_ring.start(h)
    if len(moves) > len(batches) - groups:
        move()
    x_ring.wait(ring // 2)
    while moves:
        move()
    for line in (cot_ring, x_ring):
        line.sent()
    sums.sent()
    for a in range(pre):
        feed.finish(a)
    for copy in (normed_store, own_x, resid_store, *stores):
        copy.wait()


def forward_part(n, ring, pre, tokens, cotangent, w_full, ff_full, cosine, sine, q_tile=256):
    groups, bs = w_full.shape[0], w_full.shape[-1]
    chunks = ff_full.shape[0]
    local, width = tokens.shape
    rows = local * ring
    cols = groups * bs
    any_ = pl.BlockSpec(memory_space=pl.ANY)
    vmem = pl.BlockSpec(memory_space=pltpu.VMEM)
    dma = pltpu.SemaphoreType.DMA
    shape = jax.ShapeDtypeStruct
    half = ring // 2
    return pl.pallas_call(
        functools.partial(forward_kernel, n, ring, pre, min(q_tile, rows)),
        out_shape=[
            shape(w_full.shape, BF16),
            shape(ff_full.shape, BF16),
            shape((ring, local, width), BF16),
            shape((rows, cols), BF16),
            shape((rows, cols), BF16),
            shape((rows, cols), BF16),
            shape((rows, cols), BF16),
            shape((local, width), F32),
            shape((ring, local, width), BF16),
            shape((ring, local, width), BF16),
        ],
        in_specs=[any_] * 4 + [vmem] * 2,
        out_specs=[any_] * 10,
        input_output_aliases={2: 0, 3: 1},
        scratch_shapes=[
            pltpu.VMEM((ring, local, width), BF16),
            pltpu.VMEM((max(4, groups), n, 2, bs, bs), BF16),
            pltpu.VMEM((2 * n, 16, bs), BF16),
            pltpu.VMEM((rows, cols), BF16),
            pltpu.VMEM((rows, cols), BF16),
            pltpu.VMEM((rows, cols), BF16),
            pltpu.VMEM((rows, cols), BF16),
            pltpu.VMEM((min(q_tile, rows), bs), F32),
            pltpu.VMEM((ring, local, width), BF16),
            pltpu.VMEM((2, half, local, width), BF16),
            pltpu.VMEM((local, width), BF16),
            pltpu.VMEM((local, width), F32),
            dma((2, n - 1, groups)), dma((2, n - 1, groups)),
            dma((groups,)), dma((groups,)),
            dma((2, n - 1, chunks)), dma((2, n - 1, chunks)),
            dma((chunks,)), dma((chunks,)),
            dma((2, half)), dma((2, half)), dma((2, half)), dma((2, half)),
            dma((2, half)), dma((2, half)), dma((2, half)), dma((2, half)),
            dma((8,)), dma((5,)), dma((2 * n - 1,)), dma((2 * n - 1,)),
        ],
        compiler_params=pltpu.CompilerParams(
            collective_id=1, has_side_effects=True, vmem_limit_bytes=56 * 2**20),
    )(tokens, cotangent, w_full, ff_full, cosine, sine)


def layer_kernel(
    n, ring, pre, pace, plan, q_tile, tile,
    ff_in, x_hbm, dy_hbm, residual, cotangent, tokens, normed_in, q_in, k_in, v_in, mixed_in,
    w_full, cosine_in, sine_in,
    ff_full, output, grad_tokens, gain_grads, ff_result, ff_summed, ff_landed,
    att_result, att_summed, att_landed, out_hbm,
    part, land, dres_full, core_in, stage, got, total, gparts, gland, gsecond, gone, gtwo,
    w_send, w_recv, w_sib_send, w_sib_recv,
    f_send, f_recv, f_load, f_out, a_send, a_recv, a_load, a_out,
    core_send, core_recv, acore_send, acore_recv, store_sem,
    s1_send, s1_recv, s2_send, s2_recv, s3_send, s3_recv, x_send, x_recv, free_sem,
    g_send, g_recv, h_send, h_recv, io, load,
):
    at = Place(n, ring)
    c = at.c
    groups, _, _, _, bs = w_full.shape
    chunks, _, _, unit, _ = ff_full.shape
    local, width = tokens.shape
    rows = local * ring
    heads = bs // HEAD_DIM
    half = ring // 2
    weights = LineGather(at, ff_full, w_send, w_recv, w_sib_send, w_sib_recv)
    feed = LineSum(at, chunks, ff_summed, ff_landed, ff_result,
                   stage.at[:, :, :, pl.ds(0, unit)], got.at[:, pl.ds(0, unit)],
                   total.at[pl.ds(0, unit)],
                   f_send, f_recv, f_load, f_out)
    att = LineSum(at, groups, att_summed, att_landed, att_result, stage, got, total,
                  a_send, a_recv, a_load, a_out)
    sums1 = RingSum(at, part, land, s1_send, s1_recv)
    sums2 = RingSum(at, part, land, s2_send, s2_recv)
    sums3 = RingSum(at, part, land, s3_send, s3_recv)
    dres_ring = RingGather(at, dres_full.at[at.t], dres_full, x_send, x_recv)
    lag = max(0, n - pre)
    num, den, begin = pace

    def fetch(src, dst, i):
        return pltpu.make_async_copy(src, dst, io.at[i])

    x_in = fetch(x_hbm, part, 0)
    dy_in = fetch(dy_hbm, dres_full, 1)
    x_in.start()
    dy_in.start()
    at.barrier(with_all=True)

    def ticks_before(j):
        return (j >= begin) * ((num * (j - begin)) // den)

    def feed_phase(oacc, dacc, wv, pg, hid, dgate, dup, out_stage):
        x, dy = part, dres_full

        def loads(j):
            return [
                pltpu.make_async_copy(
                    ff_full.at[j, :, :, pl.ds(i * bs, bs)], wv.at[j % 3, i], load.at[j % 3, i])
                for i in range(3)
            ]

        def core_copy(j):
            return pltpu.make_async_remote_copy(
                pg.at[1 - c], core_in.at[j % 2, :, pl.ds(0, unit)],
                core_send.at[j % 2], core_recv.at[j % 2],
                device_id={"dp": at.sib}, device_id_type=MESH)

        def store(j):
            return pltpu.make_async_copy(pg.at[c], ff_summed.at[j], store_sem)

        for copy in loads(0):
            copy.start()

        @pl.loop(0, rows // 64)
        def _(i):
            r = aligned(i, 64)
            oacc[r] = jnp.zeros((64, width), F32)
            dacc[r] = jnp.zeros((64, width), F32)

        x_in.wait()
        dy_in.wait()
        per = max(1, min(tile // local, ring))

        def columns(ref, cols):
            return ref[:, :, cols].reshape(rows, bs)

        def weight_grads(cc, now):
            @pl.loop(0, n)
            def _(k):
                cols = aligned(2 * k + cc, bs)
                xt = columns(x, cols)
                pg[cc, k, pl.ds(0, bs)] = t_dot(xt, dgate[:, now]).astype(BF16)
                pg[cc, k, pl.ds(bs, bs)] = t_dot(xt, dup[:, now]).astype(BF16)
                pg[cc, k, pl.ds(2 * bs, bs)] = t_dot(columns(dy, cols), hid[:, now]).astype(BF16)

        def compute(j):
            slot = j % 3
            now = aligned(j % 2, bs)
            for copy in loads(j):
                copy.wait()

            @pl.when(j + 1 < pre)
            def _():
                for copy in loads(j + 1):
                    copy.start()

            @pl.loop(0, ring // per)
            def _(m):
                r = aligned(m, per * local)
                here = pl.ds(m * per, per)
                rows_x = x[here].reshape(per * local, width)
                gate = dot(rows_x, wv[slot, 0].reshape(width, bs))
                up = dot(rows_x, wv[slot, 1].reshape(width, bs))
                dh = dot(dy[here].reshape(per * local, width), wv[slot, 2].reshape(width, bs))
                s = jax.nn.sigmoid(gate)
                gs = gate * s
                hid[r, now] = (gs * up).astype(BF16)
                dup[r, now] = (dh * gs).astype(BF16)
                dgate[r, now] = (dh * up * (s + gs * (1 - s))).astype(BF16)

            weight_grads(1 - c, now)
            core_copy(j).start()

            @pl.when(j % 2 == 1)
            def _():
                one, two = (j + 2) % 3, slot

                @pl.loop(0, rows // tile)
                def _(m):
                    r = aligned(m, tile)
                    both = jnp.concatenate([dgate[r, :], dup[r, :]], axis=1)

                    @pl.loop(0, n)
                    def _(k):
                        def block(s, i):
                            return wv[s, i, k].reshape(2 * bs, bs)

                        cols = aligned(k, 2 * bs)
                        oacc[r, cols] += dot_t(
                            hid[r, :], jnp.concatenate([block(one, 2), block(two, 2)], axis=1))
                        dacc[r, cols] += dot_t(both, jnp.concatenate(
                            [block(one, 0), block(two, 0), block(one, 1), block(two, 1)], axis=1))

            weight_grads(c, now)
            core_copy(j).wait_recv()

            @pl.loop(0, n)
            def _(k):
                pg[c, k] = pg[c, k] + core_in[j % 2, k, pl.ds(0, unit)]

            store(j).start()
            core_copy(j).wait_send()

        def begin_step(i):
            return min(2 * i, i + max(pre - n, 0))

        @pl.loop(0, lag + chunks)
        def _(step):
            j = step - lag
            for i in range(chunks - pre):
                for e in range(n):
                    @pl.when(step == begin_step(i) + e)
                    def _():
                        weights.event(pre + i, e)

            @pl.when(j >= 1)
            def _():
                store(j - 1).wait()
                feed.event(j - 1, 0)

            for extra in range(2):
                tick = ticks_before(j) + extra
                for e in range(n - 1, 0, -1):
                    q = tick - (e - 1) + 2 * n
                    r = q // 2 - n

                    @pl.when((j >= 0) & (tick < ticks_before(j + 1)) & (q % 2 == 0)
                             & (r >= 0) & (r < chunks))
                    def _():
                        feed.event(r, e)

            @pl.when(j >= 0)
            def _():
                compute(j)

            for i in range(chunks - pre):
                @pl.when(step == begin_step(i) + n - 1)
                def _():
                    weights.finish(pre + i)

            @pl.when((j + 1 >= pre) & (j + 1 >= 1) & (j + 1 < chunks))
            def _():
                for copy in loads(j + 1):
                    copy.start()

        store(chunks - 1).wait()
        feed.event(chunks - 1, 0)

        @pl.loop(0, ring)
        def _(m):
            part[m] = dacc[aligned(m, local), :].astype(BF16)

        for d in range(2):
            sums1.start(0, d)

        piece = local // 2

        def put(m):
            return fetch(
                out_stage.at[m % 2], out_hbm.at[m // 2, pl.ds(m % 2 * piece, piece)], m % 2)

        for m in range(2 * ring):
            if m > 1:
                put(m - 2).wait()
            out_stage[m % 2] = oacc[m * piece : (m + 1) * piece, :].astype(BF16)
            put(m).start()
        for m in range(2 * ring - 2, 2 * ring):
            put(m).wait()

    pl.run_scoped(
        feed_phase,
        pltpu.VMEM((rows, width), F32),
        pltpu.VMEM((rows, width), F32),
        pltpu.VMEM((3, 3, n, 2, bs, bs), BF16),
        pltpu.VMEM((2, n, unit, bs), BF16),
        pltpu.VMEM((rows, 2 * bs), BF16),
        pltpu.VMEM((rows, 2 * bs), BF16),
        pltpu.VMEM((rows, 2 * bs), BF16),
        pltpu.VMEM((2, local // 2, width), BF16),
    )

    done = [0 if chunks < begin else (num * (chunks - begin)) // den]
    last = 2 * (chunks - 1) + n - 2

    planned = list(plan)
    moves = []

    def point():
        for _ in range(planned.pop(0) if planned else 1):
            if done[0] <= last:
                feed_tick()
                if done[0] > last:
                    feed.result(chunks - 1).wait()
            elif moves:
                att.event(*moves.pop(0))

    def feed_tick():
        tick = done[0]
        for e in range(n - 1, 0, -1):
            if (tick - e + 1) % 2 == 0 and 0 <= (tick - e + 1) // 2 < chunks:
                feed.event((tick - e + 1) // 2, e)
        done[0] += 1

    def attention_phase(
        normed, wv, gains, q, k, v, mixed, dmix, dq, dk, dv, dproj, resid, dres, small, lined,
        gsum, pg, cosine, sine,
    ):
        resid_in = fetch(residual, resid, 0)
        cot_in = fetch(cotangent, lined, 1)
        gains_in = fetch(w_full.at[0, :, :, pl.ds(4 * bs, 16)], gains, 2)
        saved = [
            fetch(src, dst, 3 + i)
            for i, (src, dst) in enumerate(
                ((normed_in, normed), (q_in, q), (k_in, k), (v_in, v), (mixed_in, mixed)))
        ]
        weight_loads = [
            pltpu.make_async_copy(
                w_full.at[g, :, :, pl.ds(i * bs, bs)], wv.at[i, g], load.at[i, g])
            for g in range(groups) for i in range(4)
        ]
        saved += [fetch(cosine_in, cosine, 8), fetch(sine_in, sine, 9)]
        for copy in (resid_in, cot_in, gains_in, *saved, *weight_loads):
            copy.start()

        def gain_of(row, i):
            return gains[i // 2, i % 2, row : row + 1, :].astype(F32)

        tile = min(64, local)

        def norm_back(value_of, grad_of, row, emit):
            gsum[row : row + 1, :] = jnp.zeros((1, width), F32)

            @pl.loop(0, local // tile)
            def _(i):
                r = aligned(i, tile)
                scale = inverse_rms(value_of(r, pl.ds(0, width)))
                inner = jnp.zeros((tile, 1), F32)
                for b in range(2 * n):
                    cols = pl.ds(b * bs, bs)
                    value = value_of(r, cols)
                    grad = grad_of(r, cols)
                    gsum[row : row + 1, cols] += jnp.sum(
                        grad * value * scale, axis=0, keepdims=True)
                    inner += jnp.sum(grad * gain_of(row, b) * value, axis=-1, keepdims=True)
                pull = scale * scale * scale * (inner / width)
                for b in range(2 * n):
                    cols = pl.ds(b * bs, bs)
                    emit(r, cols,
                         scale * grad_of(r, cols) * gain_of(row, b) - value_of(r, cols) * pull)

        for kk in range(half):
            point()
            for d in range(2):
                sums1.add(kk, d)
                if kk < half - 1:
                    sums1.start(kk + 1, d)
        for copy in (resid_in, cot_in, gains_in):
            copy.wait()

        def emit_residual(r, cols, value):
            total = lined[r, cols].astype(F32) + value
            dres[r, cols] = total
            dres_full[at.t, r, cols] = total.astype(BF16)

        norm_back(lambda r, cols: resid[r, cols],
                  lambda r, cols: part[at.t, r, cols].astype(F32), 1, emit_residual)
        dres_ring.start(1)
        sums1.sent()
        second_in = fetch(out_hbm, part, 0)
        second_in.start()
        for h in range(2, half + 1):
            point()
            dres_ring.wait(h - 1)
            dres_ring.start(h)
        point()
        second_in.wait()
        dres_ring.wait(half)
        for d in range(2):
            sums2.start(0, d)
        for copy in (*saved, *weight_loads):
            copy.wait()

        def core_copy(g):
            return pltpu.make_async_remote_copy(
                pg.at[1 - c], core_in.at[g], acore_send.at[g], acore_recv.at[g],
                device_id={"dp": at.sib}, device_id_type=MESH)

        def store(g):
            return pltpu.make_async_copy(pg.at[c], att_summed.at[g], store_sem)

        def attend_back(g, between):
            gcols = pl.ds(g * bs, bs)
            lanes = group_lanes(heads, bs)
            dk[...] = jnp.zeros_like(dk)
            dv[...] = jnp.zeros_like(dv)
            for i in range(rows // q_tile):
                r = pl.ds(i * q_tile, q_tile)
                keys = pl.ds(0, (i + 1) * q_tile)
                dq[r] = jnp.zeros((q_tile, bs), F32)

                @pl.loop(0, heads)
                def _(h):
                    mask = lanes == h
                    qh = only(mask, q[r, gcols])
                    dmh = only(mask, dmix[r])
                    probs = causal_softmax(qh, k[keys, gcols], i * q_tile)
                    d_probs = dot_t(dmh, v[keys, gcols])
                    inner = jnp.sum(d_probs * probs, axis=-1, keepdims=True)
                    d_scores = (probs * (d_probs - inner)).astype(BF16)
                    dq[r] += dot(d_scores, only(mask, k[keys, gcols]))
                    dk[keys] += t_dot(d_scores, qh)
                    dv[keys] += t_dot(probs.astype(BF16), dmh)

                between(i)

        def weight_grads(g, cc):
            gcols = pl.ds(g * bs, bs)

            @pl.loop(0, n)
            def _(b):
                cols = aligned(2 * b + cc, bs)
                x = normed[:, :, cols].reshape(rows, bs)
                for i in range(3):
                    pg[cc, b, pl.ds(i * bs, bs)] = t_dot(x, dproj[i, :, gcols]).astype(BF16)
                pg[cc, b, pl.ds(3 * bs, bs)] = t_dot(
                    dres_full[:, :, cols].reshape(rows, bs), mixed[:, gcols]).astype(BF16)

        second = [0]

        def second_sum():
            if second[0] < half:
                kk = second[0]
                for d in range(2):
                    sums2.add(kk, d)
                    if kk < half - 1:
                        sums2.start(kk + 1, d)
                second[0] += 1

        tiles = rows // q_tile

        def between(i):
            point()
            if i == tiles - 1:
                second_sum()

        for g in range(groups):
            gcols = pl.ds(g * bs, bs)

            @pl.loop(0, ring)
            def _(m):
                r = aligned(m, local)
                dmix[r] = dot(dres_full[m], wv[3, g].reshape(width, bs)).astype(BF16)

            attend_back(g, between)

            @pl.loop(0, ring)
            def _(m):
                r = aligned(m, local)
                for i, ref in enumerate((dq, dk)):
                    value = ref[r] * HEAD_DIM ** (-0.5)
                    dproj[i, r, gcols] = rope(
                        value, cosine[r, :], sine[r, :], back=True).astype(BF16)
                dproj[2, r, gcols] = dv[r].astype(BF16)

            weight_grads(g, 1 - c)
            core_copy(g).start()
            weight_grads(g, c)
            core_copy(g).wait_recv()

            @pl.loop(0, n)
            def _(b):
                pg[c, b] = pg[c, b] + core_in[g, b]

            store(g).start()
            core_copy(g).wait_send()
            store(g).wait()
            att.event(g, 0)
            moves.extend((g, e) for e in range(1, n))

        while second[0] < half:
            second_sum()
        sums2.sent()

        @pl.loop(0, local // tile)
        def _(i):
            r = aligned(i, tile)
            lined[r] = (resid[r] + part[at.t, r].astype(F32)).astype(BF16)

        out_store = fetch(lined, output, 0)
        out_store.start()
        for way in (1, -1):
            pl.semaphore_signal(
                free_sem, inc=1, device_id={"tensor": at.member(way)}, device_id_type=MESH)

        def share(offset):
            m = at.member(offset)
            r = aligned(m, local)
            for b in range(n):
                block = sum(
                    dot_t(dproj[i, r, g * bs : (g + 1) * bs], wv[i, g, b].reshape(2 * bs, bs))
                    for i in range(3) for g in range(groups)
                )
                part[m, :, b * 2 * bs : (b + 1) * 2 * bs] = block.astype(BF16)

        share(half)
        pl.semaphore_wait(free_sem, 2)
        for d in range(2):
            sums3.start(0, d)

        tok_in = fetch(tokens, small, 1)
        dres_ring.sent()
        tok_in.start()
        point()
        for kk in range(1, half):
            for d in range(2):
                share((1 if d == 0 else -1) * (half - kk))
            for d in range(2):
                sums3.add(kk - 1, d)
                sums3.start(kk, d)
            point()
        share(0)
        point()
        for d in range(2):
            sums3.add(half - 1, d)
        tok_in.wait()
        out_store.wait()

        def emit_tokens(r, cols, value):
            lined[r, cols] = (dres[r, cols] + value).astype(BF16)

        norm_back(lambda r, cols: small[r, cols].astype(F32),
                  lambda r, cols: part[at.t, r, cols].astype(F32), 0, emit_tokens)
        token_store = fetch(lined, grad_tokens, 0)
        token_store.start()
        for b in range(2 * n):
            gparts[b, 0:2] = gsum[0:2, b * bs : (b + 1) * bs]
            gparts[b, 2:8] = jnp.zeros((6, bs), F32)
        over_dp = SmallSum("dp", 2 * at.z + c, 2 * n, lambda i: gparts.at[i], gland, g_send, g_recv)
        gone[...] = over_dp.total()
        over_ring = SmallSum("tensor", at.t, ring, lambda i: gone, gsecond, h_send, h_recv)
        gtwo[...] = over_ring.total()
        gain_store = fetch(gtwo, gain_grads, 1)
        gain_store.start()
        while done[0] <= last or moves:
            point()
        att.result(groups - 1).wait()
        token_store.wait()
        gain_store.wait()
        sums3.sent()

    cols = groups * bs
    pl.run_scoped(
        attention_phase,
        pltpu.VMEM((ring, local, width), BF16),
        pltpu.VMEM((4, groups, n, 2, bs, bs), BF16),
        pltpu.VMEM((n, 2, 16, bs), BF16),
        pltpu.VMEM((rows, cols), BF16),
        pltpu.VMEM((rows, cols), BF16),
        pltpu.VMEM((rows, cols), BF16),
        pltpu.VMEM((rows, cols), BF16),
        pltpu.VMEM((rows, bs), BF16),
        pltpu.VMEM((rows, bs), F32),
        pltpu.VMEM((rows, bs), F32),
        pltpu.VMEM((rows, bs), F32),
        pltpu.VMEM((3, rows, cols), BF16),
        pltpu.VMEM((local, width), F32),
        pltpu.VMEM((local, width), F32),
        pltpu.VMEM((local, width), BF16),
        pltpu.VMEM((local, width), BF16),
        pltpu.VMEM((8, width), F32),
        pltpu.VMEM((2, n, 4 * bs, bs), BF16),
        pltpu.VMEM((rows, bs), F32),
        pltpu.VMEM((rows, bs), F32),
    )


def layer_part(
    n, ring, pre, pace, plan, ff_full, x, dy, residual, cotangent, tokens, normed, q, k, v, mixed,
    w_full, cosine, sine, q_tile=256, tile=512,
):
    groups, _, _, _, bs = w_full.shape
    chunks, _, _, unit, _ = ff_full.shape
    local, width = tokens.shape
    rows = local * ring
    half = ring // 2
    any_ = pl.BlockSpec(memory_space=pl.ANY)
    dma = pltpu.SemaphoreType.DMA
    shape = jax.ShapeDtypeStruct
    big = (ring, local, width)
    wide = 4 * bs
    return pl.pallas_call(
        functools.partial(
            layer_kernel, n, ring, pre, pace, plan, min(q_tile, rows), min(tile, rows)),
        out_shape=[
            shape(ff_full.shape, BF16),
            shape((local, width), BF16),
            shape((local, width), BF16),
            shape((8, bs), F32),
            shape((chunks, unit, bs), BF16),
            shape((chunks, n, unit, bs), BF16),
            shape((2, chunks, n - 1, unit, bs), BF16),
            shape((groups, wide, bs), BF16),
            shape((groups, n, wide, bs), BF16),
            shape((2, groups, n - 1, wide, bs), BF16),
            shape(big, BF16),
        ],
        in_specs=[any_] * 14,
        out_specs=[any_] * 11,
        input_output_aliases={0: 0},
        scratch_shapes=[
            pltpu.VMEM(big, BF16),
            pltpu.VMEM((2, half, local, width), BF16),
            pltpu.VMEM(big, BF16),
            pltpu.VMEM((max(2, groups), n, wide, bs), BF16),
            pltpu.VMEM((2, n - 2, n // 2, wide, bs), BF16),
            pltpu.VMEM((4, wide, bs), BF16),
            pltpu.VMEM((wide, bs), BF16),
            pltpu.VMEM((2 * n, 8, bs), F32),
            pltpu.VMEM((2 * n - 1, 8, bs), F32),
            pltpu.VMEM((ring - 1, 8, bs), F32),
            pltpu.VMEM((8, bs), F32),
            pltpu.VMEM((8, bs), F32),
            dma((2, n - 1, chunks)), dma((2, n - 1, chunks)), dma((chunks,)), dma((chunks,)),
            dma((2, n - 1, chunks)), dma((2, n - 1, chunks)), dma((4,)), dma,
            dma((2, n - 1, groups)), dma((2, n - 1, groups)), dma((4,)), dma,
            dma((2,)), dma((2,)), dma((groups,)), dma((groups,)), dma,
            dma((2, half)), dma((2, half)), dma((2, half)), dma((2, half)),
            dma((2, half)), dma((2, half)), dma((2, half)), dma((2, half)),
            pltpu.SemaphoreType.REGULAR,
            dma((2 * n - 1,)), dma((2 * n - 1,)), dma((ring - 1,)), dma((ring - 1,)),
            dma((10,)), dma((4, max(4, groups))),
        ],
        compiler_params=pltpu.CompilerParams(
            collective_id=2, has_side_effects=True, vmem_limit_bytes=63 * 2**20),
    )(ff_full, x, dy, residual, cotangent, tokens, normed, q, k, v, mixed, w_full, cosine, sine)


PREFETCH = 5
PACE = (1, 1, 3)
PLAN = (1, 2, 2, 2) + (0, 1, 1, 1) + (1, 1, 1, 1) + (1, 1, 1)


def pack_kernel(place, q, k, v, o, gain_attn, gain_mlp, gate, up, down, att, ff):
    bs = q.shape[0]
    for i, ref in enumerate((q, k, v)):
        att[i * bs : (i + 1) * bs] = ref[...]
    att[3 * bs : 4 * bs] = o[...].T
    row = lax.broadcasted_iota(jnp.int32, (16, bs), 0)
    first, second = (g[...].astype(F32) for g in (gain_attn, gain_mlp))
    gains = jnp.where(row == 0, first, jnp.where(row == 1, second, 0.0))
    att[4 * bs : 4 * bs + 16] = gains.astype(BF16)
    ff[0:bs] = gate[...]
    ff[bs : 2 * bs] = up[...]
    ff[2 * bs : 3 * bs] = down[...].T


def pack(w_query, w_key, w_value, w_out, gain_attn, gain_mlp, w_gate, w_up, w_down):
    bs = w_query.shape[0]
    n = lax.axis_size("dp") // 2
    groups, chunks = w_query.shape[1] // bs, w_gate.shape[1] // bs

    def at_group(j):
        return jnp.minimum(j, groups - 1)

    col = pl.BlockSpec((bs, bs), lambda j, p: (0, at_group(j)))
    row = pl.BlockSpec((bs, bs), lambda j, p: (at_group(j), 0))
    gain = pl.BlockSpec((1, bs), lambda j, p: (0, 0))
    wide = pl.BlockSpec((bs, bs), lambda j, p: (0, j))
    tall = pl.BlockSpec((bs, bs), lambda j, p: (j, 0))
    return pl.pallas_call(
        pack_kernel,
        out_shape=[
            jax.ShapeDtypeStruct((groups, n, 2, 4 * bs + 16, bs), BF16),
            jax.ShapeDtypeStruct((chunks, n, 2, 3 * bs, bs), BF16),
        ],
        grid_spec=pltpu.PrefetchScalarGridSpec(
            num_scalar_prefetch=1,
            grid=(chunks,),
            in_specs=[col, col, col, row, gain, gain, wide, wide, tall],
            out_specs=[
                pl.BlockSpec((None, None, None, 4 * bs + 16, bs),
                             lambda j, p: (at_group(j), p[0], p[1], 0, 0)),
                pl.BlockSpec((None, None, None, 3 * bs, bs), lambda j, p: (j, p[0], p[1], 0, 0)),
            ],
        ),
    )(jnp.stack([lax.axis_index("dp") // 2, lax.axis_index("dp") % 2]),
      w_query, w_key, w_value, w_out, gain_attn.reshape(1, bs), gain_mlp.reshape(1, bs),
      w_gate, w_up, w_down)


def unpack_kernel(att, ff, q, k, v, o, gate, up, down):
    bs = q.shape[0]
    for i, ref in enumerate((q, k, v)):
        ref[...] = att[0, i * bs : (i + 1) * bs].astype(F32)
    o[...] = att[0, 3 * bs : 4 * bs].astype(F32).T
    gate[...] = ff[0, 0:bs].astype(F32)
    up[...] = ff[0, bs : 2 * bs].astype(F32)
    down[...] = ff[0, 2 * bs : 3 * bs].astype(F32).T


def unpack(att, ff):
    groups, chunks, bs = att.shape[0], ff.shape[0], ff.shape[2]

    def at_group(j):
        return jnp.minimum(j, groups - 1)

    shape = jax.ShapeDtypeStruct
    col = pl.BlockSpec((bs, bs), lambda j: (0, at_group(j)))
    row = pl.BlockSpec((bs, bs), lambda j: (at_group(j), 0))
    wide = pl.BlockSpec((bs, bs), lambda j: (0, j))
    tall = pl.BlockSpec((bs, bs), lambda j: (j, 0))
    return pl.pallas_call(
        unpack_kernel,
        grid=(chunks,),
        out_shape=[shape((bs, groups * bs), F32)] * 3 + [shape((groups * bs, bs), F32)]
        + [shape((bs, chunks * bs), F32)] * 2 + [shape((chunks * bs, bs), F32)],
        in_specs=[
            pl.BlockSpec((1, 4 * bs, bs), lambda j: (at_group(j), 0, 0)),
            pl.BlockSpec((1, 3 * bs, bs), lambda j: (j, 0, 0)),
        ],
        out_specs=[col] * 3 + [row] + [wide] * 2 + [tall],
    )(att, ff)


def rotary_tables(row_count, width):
    frequency = rope_base ** (-np.arange(HEAD_DIM // 2) * 2.0 / HEAD_DIM)
    angles = (np.arange(row_count) % LEN)[:, None] * frequency[None, :]
    angles = np.tile(angles, (1, width // (HEAD_DIM // 2)))
    return np.cos(angles).astype(np.float32), np.sin(angles).astype(np.float32)


def shards(
    tokens, gain_attn, w_query, w_key, w_value, w_out, gain_mlp, w_gate, w_up, w_down, cotangent
):
    dp, ring = lax.axis_size("dp"), lax.axis_size("tensor")
    n = dp // 2
    local, width = tokens.shape
    rows = local * ring
    assert rows == LEN
    bs = w_query.shape[0]
    cosine, sine = rotary_tables(rows, bs)
    w_start, ff_start = pack(
        w_query, w_key, w_value, w_out, gain_attn, gain_mlp, w_gate, w_up, w_down
    )
    w_full, ff_full, normed, q, k, v, mixed, residual, x, dy = forward_part(
        n, ring, PREFETCH, tokens, cotangent, w_start, ff_start, cosine, sine
    )
    _, output, grad_tokens, gain_grads, ff_grads, _, _, att_grads, _, _, _ = layer_part(
        n, ring, PREFETCH, PACE, PLAN, ff_full, x, dy, residual, cotangent, tokens,
        normed, q, k, v, mixed, w_full, cosine, sine,
    )
    g_query, g_key, g_value, g_out, g_gate, g_up, g_down = unpack(att_grads, ff_grads)
    return (
        output,
        grad_tokens,
        gain_grads[0],
        g_query,
        g_key,
        g_value,
        g_out,
        gain_grads[1],
        g_gate,
        g_up,
        g_down,
    )


def solution(mesh):
    placed = (
        P(("dp", "tensor"), None),
        P("dp"),
        P("dp", "tensor"),
        P("dp", "tensor"),
        P("dp", "tensor"),
        P("tensor", "dp"),
        P("dp"),
        P("dp", "tensor"),
        P("dp", "tensor"),
        P("tensor", "dp"),
        P(("dp", "tensor"), None),
    )
    return jax.shard_map(
        shards,
        mesh=mesh,
        in_specs=placed,
        out_specs=(
            P(("dp", "tensor"), None),
            P(("dp", "tensor"), None),
            P("dp"),
            P("dp", "tensor"),
            P("dp", "tensor"),
            P("dp", "tensor"),
            P("tensor", "dp"),
            P("dp"),
            P("dp", "tensor"),
            P("dp", "tensor"),
            P("tensor", "dp"),
        ),
        check_vma=False,
    )
```

```python
import functools

import jax
import jax.numpy as jnp
import numpy as np
from jax import lax
from jax.experimental import pallas as pl
from jax.experimental.pallas import tpu as pltpu
from jax.sharding import PartitionSpec as P

HEAD_DIM = 64
LEN = 1024
MESH = pl.DeviceIdType.MESH
BF16 = jnp.bfloat16
F32 = jnp.float32

norm_eps = 1e-05
rope_base = 130000.0
masked_score = -1e30


def dot(a, b):
    return jnp.dot(a, b, preferred_element_type=F32)


def dot_t(a, b):
    return lax.dot_general(a, b, (((1,), (1,)), ((), ())), preferred_element_type=F32)


def t_dot(a, b):
    return lax.dot_general(a, b, (((0,), (0,)), ((), ())), preferred_element_type=F32)


def aligned(index, size):
    return pl.ds(pl.multiple_of(index * size, size), size)


class Place:
    def __init__(self, n, ring):
        me = lax.axis_index("dp")
        self.n, self.ring = n, ring
        self.z, self.c = me // 2, me % 2
        self.right, self.left = me + 2, me - 2
        self.sib = me + 1 - 2 * self.c
        self.has_r, self.has_l = self.z < n - 1, self.z > 0
        t = lax.axis_index("tensor")
        odd = t % 2
        self.t = t
        self.p = (1 - odd) * (t // 2) + odd * (ring - 1 - t // 2)

    def member(self, offset):
        p = (self.p + offset + self.ring) % self.ring
        back = (p >= self.ring // 2).astype(jnp.int32)
        return (1 - back) * (2 * p) + back * (2 * (self.ring - 1 - p) + 1)

    def barrier(self, with_ring=True, with_all=False):
        sem = pltpu.get_barrier_semaphore()

        def greet(peer):
            pl.semaphore_signal(sem, inc=1, device_id=peer, device_id_type=MESH)

        if with_all:
            for k in range(1, 2 * self.n):
                greet({"dp": (2 * self.z + self.c + k) % (2 * self.n)})
            for k in range(1, self.ring):
                greet({"tensor": (self.t + k) % self.ring})
            pl.semaphore_wait(sem, 2 * self.n - 1 + self.ring - 1)
            return

        greet({"dp": self.sib})
        if with_ring:
            greet({"tensor": self.member(1)})
            greet({"tensor": self.member(-1)})

        @pl.when(self.has_r)
        def _():
            greet({"dp": self.right})

        @pl.when(self.has_l)
        def _():
            greet({"dp": self.left})

        peers = self.has_r.astype(jnp.int32) + self.has_l.astype(jnp.int32)
        pl.semaphore_wait(sem, peers + (3 if with_ring else 1))

    def neighbour(self, d):
        return self.right if d == 0 else self.left

    def sends_to(self, d):
        return self.has_r if d == 0 else self.has_l

    def along(self, d, k):
        return self.z + k if d == 0 else self.z - k

    def depth(self, d):
        return self.z if d == 0 else self.n - 1 - self.z


class LineGather:
    def __init__(self, at, full, send, recv, sib_send, sib_recv):
        self.at, self.full = at, full
        self.send, self.recv = send, recv
        self.sib_send, self.sib_recv = sib_send, sib_recv

    def hop(self, a, h, d):
        at = self.at
        block = self.full.at[a, at.along(d, 1 - h), at.c]
        return pltpu.make_async_remote_copy(
            block, block, self.send.at[d, h - 1, a], self.recv.at[d, h - 1, a],
            device_id={"dp": at.neighbour(d)}, device_id_type=MESH)

    def sends(self, h, d):
        return self.at.sends_to(d) & (self.at.depth(d) >= h - 1)

    def arrives(self, h, d):
        return self.at.depth(d) >= h

    def to_sib(self, a):
        part = self.full.at[a, :, self.at.c]
        return pltpu.make_async_remote_copy(
            part, part, self.sib_send.at[a], self.sib_recv.at[a],
            device_id={"dp": self.at.sib}, device_id_type=MESH)

    def event(self, a, e):
        n = self.at.n
        for d in range(2):
            if e > 0:
                @pl.when(self.arrives(e, d))
                def _():
                    self.hop(a, e, d).wait_recv()

            if e < n - 1:
                @pl.when(self.sends(e + 1, d))
                def _():
                    self.hop(a, e + 1, d).start()

        if e == n - 1:
            self.to_sib(a).start()

    def finish(self, a):
        self.to_sib(a).wait_recv()
        self.to_sib(a).wait_send()
        for h in range(1, self.at.n):
            for d in range(2):
                @pl.when(self.sends(h, d))
                def _():
                    self.hop(a, h, d).wait_send()


class LineSum:
    def __init__(self, at, chunks, sums, land, out, stage, got, total, send, recv, load, out_sem):
        self.at, self.chunks = at, chunks
        self.sums, self.land, self.out = sums, land, out
        self.stage, self.got, self.total = stage, got, total
        self.send, self.recv, self.load, self.out_sem = send, recv, load, out_sem

    def valid(self, j):
        return (j >= 0) & (j < self.chunks)

    def copy(self, j, s, d, staged):
        at = self.at
        src = self.stage.at[d, s - 2, j % (at.n // 2)] if staged else self.sums.at[j, at.along(d, at.n - s)]
        return pltpu.make_async_remote_copy(
            src, self.land.at[d, j, s - 1], self.send.at[d, s - 1, j], self.recv.at[d, s - 1, j],
            device_id={"dp": at.neighbour(d)}, device_id_type=MESH)

    def arrival(self, j, s, d):
        return pltpu.make_async_remote_copy(
            self.land.at[d, j, s - 1], self.land.at[d, j, s - 1],
            self.send.at[d, s - 1, j], self.recv.at[d, s - 1, j],
            device_id={"dp": self.at.sib}, device_id_type=MESH)

    def arrives(self, s, d):
        depth = self.at.depth(d)
        return (depth > 0) & (depth <= s)

    def get(self, src, k):
        return pltpu.make_async_copy(src, self.got.at[k], self.load.at[k])

    def event(self, j, e):
        at, n = self.at, self.at.n
        if e == 0:
            for s in range(1, n):
                for d in range(2):
                    @pl.when(at.sends_to(d) & (at.depth(d) == 0))
                    def _():
                        self.copy(j, s, d, False).start()

        elif e < n - 1:
            s = e + 1
            here = [at.sends_to(d) & (at.depth(d) > 0) & (at.depth(d) < s) for d in range(2)]

            def own(d):
                return self.get(self.sums.at[j, at.along(d, n - s)], d)

            def came(d):
                return self.get(self.land.at[d, j, s - 2], 2 + d)

            for d in range(2):
                @pl.when(here[d])
                def _():
                    own(d).start()

            for d in range(2):
                @pl.when(here[d])
                def _():
                    self.arrival(j, s - 1, d).wait_recv()
                    came(d).start()

            for d in range(2):
                @pl.when(here[d])
                def _():
                    own(d).wait()
                    came(d).wait()
                    self.stage[d, s - 2, j % (n // 2)] = self.got[d] + self.got[2 + d]
                    self.copy(j, s, d, True).start()
        else:
            own = self.get(self.sums.at[j, at.z], 0)
            own.start()

            @pl.when(j > 0)
            def _():
                self.result(j - 1).wait()

            for d in range(2):
                @pl.when(at.depth(d) > 0)
                def _():
                    self.arrival(j, n - 1, d).wait_recv()
                    self.get(self.land.at[d, j, n - 2], 2 + d).start()

            own.wait()

            @pl.when(at.depth(0) == 0)
            def _():
                self.get(self.land.at[1, j, n - 2], 3).wait()
                self.total[...] = self.got[0] + self.got[3]

            @pl.when(at.depth(1) == 0)
            def _():
                self.get(self.land.at[0, j, n - 2], 2).wait()
                self.total[...] = self.got[0] + self.got[2]

            @pl.when((at.depth(0) > 0) & (at.depth(1) > 0))
            def _():
                for d in range(2):
                    self.get(self.land.at[d, j, n - 2], 2 + d).wait()
                self.total[...] = self.got[0] + self.got[2] + self.got[3]

            self.result(j).start()
            self.sent(j)

    def result(self, j):
        return pltpu.make_async_copy(self.total, self.out.at[j], self.out_sem)

    def sent(self, j):
        at, n = self.at, self.at.n
        for s in range(1, n):
            for d in range(2):
                @pl.when(at.sends_to(d) & (at.depth(d) == 0))
                def _():
                    self.copy(j, s, d, False).wait_send()

                if s >= 2:
                    @pl.when(at.sends_to(d) & (at.depth(d) > 0) & (at.depth(d) < s))
                    def _():
                        self.copy(j, s, d, True).wait_send()


class RingGather:
    def __init__(self, at, own, full, send, recv):
        self.at, self.own, self.full, self.send, self.recv = at, own, full, send, recv

    def copy(self, h, d):
        at = self.at
        way = 1 if d == 0 else -1
        owner = at.member(-way * (h - 1))
        rows = self.full.shape[1]
        part = pl.ds(0, rows)
        if h == at.ring // 2:
            part = pl.ds(d * (rows // 2), rows // 2)
        dst = self.full.at[owner, part]
        src = self.own.at[part] if h == 1 else dst
        return pltpu.make_async_remote_copy(
            src, dst, self.send.at[d, h - 1], self.recv.at[d, h - 1],
            device_id={"tensor": at.member(way)}, device_id_type=MESH)

    def start(self, h):
        for d in range(2):
            self.copy(h, d).start()

    def wait(self, h):
        for d in range(2):
            self.copy(h, d).wait_recv()

    def sent(self):
        for h in range(1, self.at.ring // 2 + 1):
            for d in range(2):
                self.copy(h, d).wait_send()


class SmallSum:
    def __init__(self, axis, me, size, part_of, land, send, recv):
        self.axis, self.me, self.size, self.part_of = axis, me, size, part_of
        self.land, self.send, self.recv = land, send, recv

    def copy(self, k):
        peer = (self.me + k) % self.size
        return pltpu.make_async_remote_copy(
            self.part_of(peer), self.land.at[k - 1], self.send.at[k - 1], self.recv.at[k - 1],
            device_id={self.axis: peer}, device_id_type=MESH)

    def total(self):
        for k in range(1, self.size):
            self.copy(k).start()
        result = self.part_of(self.me)[...]
        for k in range(1, self.size):
            self.copy(k).wait_recv()
            result = result + self.land[k - 1]
        for k in range(1, self.size):
            self.copy(k).wait_send()
        return result


class SmallGather:
    def __init__(self, axis, me, size, own, full, send, recv):
        self.axis, self.me, self.size, self.own, self.full = axis, me, size, own, full
        self.send, self.recv = send, recv

    def copy(self, k, slot):
        return pltpu.make_async_remote_copy(
            self.own, self.full.at[slot], self.send.at[k - 1], self.recv.at[k - 1],
            device_id={self.axis: (self.me + k) % self.size}, device_id_type=MESH)

    def start(self):
        for k in range(1, self.size):
            self.copy(k, self.me).start()

    def wait(self):
        for k in range(1, self.size):
            self.copy(k, (self.me + self.size - k) % self.size).wait_recv()
        for k in range(1, self.size):
            self.copy(k, self.me).wait_send()


class RingSum:
    def __init__(self, at, part, land, send, recv):
        self.at, self.part, self.land, self.send, self.recv = at, part, land, send, recv
        self.stages = at.ring // 2

    def rows_of(self, k, d):
        rows = self.part.shape[1]
        return pl.ds(d * (rows // 2), rows // 2) if k == 0 else pl.ds(0, rows)

    def target(self, k, d):
        return self.at.member((1 if d == 0 else -1) * (self.stages - k))

    def copy(self, k, d):
        r = self.rows_of(k, d)
        return pltpu.make_async_remote_copy(
            self.part.at[self.target(k, d), r], self.land.at[d, k, r],
            self.send.at[d, k], self.recv.at[d, k],
            device_id={"tensor": self.at.member(1 if d == 0 else -1)}, device_id_type=MESH)

    def start(self, k, d):
        self.copy(k, d).start()

    def add(self, k, d):
        self.copy(k, d).wait_recv()
        block = self.target(k + 1, d)
        rows = self.part.shape[1]
        half = rows // 2
        quarter = max(half // 4, 16)
        first = d * half if k == 0 else 0
        count = (half if k == 0 else rows) // quarter

        @pl.loop(0, count)
        def _(i):
            r = pl.ds(pl.multiple_of(first + i * quarter, quarter), quarter)
            self.part[block, r] = self.part[block, r] + self.land[d, k, r]

    def sent(self):
        for k in range(self.stages):
            for d in range(2):
                self.copy(k, d).wait_send()


def group_lanes(heads, width):
    return lax.broadcasted_iota(jnp.int32, (1, width), 1) // HEAD_DIM


def rope(values, cosine, sine, back=False):
    width = values.shape[-1]
    half = HEAD_DIM // 2
    first = lax.broadcasted_iota(jnp.int32, (1, width), 1) % HEAD_DIM < half
    ahead = pltpu.roll(values, width - half, 1)
    behind = pltpu.roll(values, half, 1)
    turned = jnp.where(first, -ahead, behind)
    return values * cosine - turned * sine if back else values * cosine + turned * sine


def inverse_rms(values):
    return lax.rsqrt(jnp.mean(values * values, axis=-1, keepdims=True) + norm_eps)


def score_parts(q_rows, k, cols, i, tile):
    diag = pl.ds(i * tile, tile)
    own = dot_t(q_rows, k[diag, cols])
    row = lax.broadcasted_iota(jnp.int32, own.shape, 0)
    column = lax.broadcasted_iota(jnp.int32, own.shape, 1)
    parts = [(diag, jnp.where(row >= column, own, masked_score))]
    if i > 0:
        past = pl.ds(0, i * tile)
        parts.append((past, dot_t(q_rows, k[past, cols])))
    return parts


def only(mask, values):
    return jnp.where(mask, values, jnp.zeros_like(values))


def forward_kernel(
    n, ring, pre, q_tile,
    tokens, cotangent, w_in, ff_in, cosine, sine,
    w_full, ff_full, normed_out, q_out, k_out, v_out, mixed_out, stats_out, residual_out, x_full, dy_full,
    tok, wv, gains, q, k, v, mixed, stats, acc, part, land, xrow, resid,
    a_send, a_recv, a_sib_send, a_sib_recv,
    f_send, f_recv, f_sib_send, f_sib_recv,
    t_send, t_recv, c_send, c_recv, x_send, x_recv, s_send, s_recv, io, load, gain_send, gain_recv,
):
    at = Place(n, ring)
    groups, _, _, _, bs = w_full.shape
    local, width = tokens.shape
    rows = local * ring
    heads = bs // HEAD_DIM
    att = LineGather(at, w_full, a_send, a_recv, a_sib_send, a_sib_recv)
    feed = LineGather(at, ff_full, f_send, f_recv, f_sib_send, f_sib_recv)
    tok_ring = RingGather(at, tokens, tok, t_send, t_recv)
    cot_ring = RingGather(at, cotangent, dy_full, c_send, c_recv)
    x_ring = RingGather(at, xrow, x_full, x_send, x_recv)
    sums = RingSum(at, part, land, s_send, s_recv)

    own_tok = pltpu.make_async_copy(tokens, tok.at[at.t], io.at[0])
    cot_in = pltpu.make_async_copy(cotangent, xrow, io.at[1])
    own_cot = pltpu.make_async_copy(xrow, dy_full.at[at.t], io.at[1])
    gain_in = pltpu.make_async_copy(
        w_full.at[0, at.z, at.c, pl.ds(4 * bs, 16)], gains.at[2 * at.z + at.c], io.at[2])
    own_tok.start()
    cot_in.start()
    gain_in.start()
    at.barrier(with_all=True)
    gain_all = SmallGather(
        "dp", 2 * at.z + at.c, 2 * n, gains.at[2 * at.z + at.c], gains, gain_send, gain_recv)

    first = (pre + 1) // 2
    batches = [[(att, g)] for g in range(groups)]
    for lot in (range(first), range(first, pre)):
        if len(lot):
            batches.append([(feed, a) for a in lot])

    def event(b, e):
        if b < len(batches):
            for line, a in batches[b]:
                line.event(a, e)

    def loads(g):
        return [
            pltpu.make_async_copy(w_full.at[g, :, :, pl.ds(i * bs, bs)], wv.at[i], load.at[i])
            for i in range(3)
        ]

    for g in range(groups):
        event(g, 0)
    tok_ring.start(1)
    stats[...] = jnp.zeros_like(stats)
    gain_in.wait()
    gain_all.start()
    for g in range(groups):
        event(g, 1)
    cot_in.wait()
    own_cot.start()
    tok_ring.wait(1)
    tok_ring.start(2)
    event(0, 2)
    for h in range(3, ring // 2 + 1):
        tok_ring.wait(h - 1)
        tok_ring.start(h)
    tok_ring.wait(ring // 2)
    cot_ring.start(1)
    gain_all.wait()
    own_tok.wait()
    tok_ring.sent()

    def norm_into(values, scale, row, store):
        for i in range(2 * n):
            gain = gains[i, row : row + 1, :].astype(F32)
            cols = pl.ds(i * bs, bs)
            store(cols, (values(cols) * scale * gain).astype(BF16))

    norm_tile = min(64, local)

    @pl.loop(0, ring)
    def _(m):
        @pl.loop(0, local // norm_tile)
        def _(i):
            r = aligned(i, norm_tile)
            scale = inverse_rms(tok[m, r].astype(F32))

            def store(cols, value):
                tok[m, r, cols] = value

            norm_into(lambda cols: tok[m, r, cols].astype(F32), scale, 0, store)

    normed_store = pltpu.make_async_copy(tok, normed_out, io.at[2])
    normed_store.start()

    def project(g):
        cols = pl.ds(g * bs, bs)

        @pl.loop(0, ring)
        def _(m):
            r = aligned(m, local)
            x = tok[m]
            query = dot(x, wv[0].reshape(width, bs))
            key = dot(x, wv[1].reshape(width, bs))
            q[r, cols] = rope(query, cosine[r, :], sine[r, :]).astype(BF16)
            k[r, cols] = rope(key, cosine[r, :], sine[r, :]).astype(BF16)
            v[r, cols] = dot(x, wv[2].reshape(width, bs)).astype(BF16)

    def attend(g, between):
        cols = pl.ds(g * bs, bs)
        lanes = group_lanes(heads, bs)
        columns = lax.broadcasted_iota(jnp.int32, (1, 128), 1)
        scale = jnp.asarray(HEAD_DIM ** (-0.5), BF16)
        for i in range(rows // q_tile):
            r = pl.ds(i * q_tile, q_tile)
            acc[...] = jnp.zeros_like(acc)

            @pl.loop(0, heads)
            def _(h):
                mask = lanes == h
                scaled = only(mask, q[r, cols]) * scale
                parts = score_parts(scaled, k, cols, i, q_tile)
                most = functools.reduce(
                    jnp.maximum, [jnp.max(s, axis=-1, keepdims=True) for _, s in parts])
                total, mix = 0.0, 0.0
                for keys, scores in parts:
                    exp_scores = jnp.exp(scores - most)
                    total += jnp.sum(exp_scores, axis=-1, keepdims=True)
                    mix += dot(exp_scores.astype(BF16), only(mask, v[keys, cols]))
                acc[...] += mix * (1.0 / total)
                stats[r] = jnp.where(columns == g * heads + h, most + jnp.log(total), stats[r])

            mixed[r, cols] = acc[...].astype(BF16)
            between(i)

    for e in range(2, n - 1):
        for g in range(groups):
            if (g, e) != (0, 2):
                event(g, e)
    for b in range(groups, len(batches)):
        event(b, 0)
    def fetch(g):
        att.finish(g)
        for copy in loads(g):
            copy.start()

    event(0, n - 1)
    fetch(0)
    for g in range(groups):
        for copy in loads(g):
            copy.wait()
        project(g)
        if g == 0:
            cot_ring.wait(1)
            cot_ring.start(2)
        if g + 1 < groups:
            event(g + 1, n - 1)

        def between(i):
            if i == 1 and g + 1 < groups:
                fetch(g + 1)

        attend(g, between)
    for h in range(3, ring // 2 + 1):
        cot_ring.wait(h - 1)
        cot_ring.start(h)
    cot_ring.wait(ring // 2)
    stores = [
        pltpu.make_async_copy(ref, out, io.at[3 + i])
        for i, (ref, out) in enumerate(((q, q_out), (k, k_out), (v, v_out), (mixed, mixed_out), (stats, stats_out)))
    ]
    for copy in stores:
        copy.start()
    out_loads = [
        pltpu.make_async_copy(w_full.at[g, :, :, pl.ds(3 * bs, bs)], wv.at[g], load.at[g])
        for g in range(groups)
    ]
    for copy in out_loads:
        copy.start()
    for copy in out_loads:
        copy.wait()

    def out_share(offset):
        m = at.member(offset)
        r = aligned(m, local)
        for b in range(n):
            block = sum(
                dot_t(mixed[r, g * bs : (g + 1) * bs], wv[g, b].reshape(2 * bs, bs))
                for g in range(groups)
            )
            part[m, :, b * 2 * bs : (b + 1) * 2 * bs] = block.astype(BF16)

    moves = [(b, e) for e in range(1, n) for b in range(groups, len(batches))]

    def move():
        if moves:
            event(*moves.pop(0))

    out_share(ring // 2)
    for d in range(2):
        sums.start(0, d)
    for kk in range(1, ring // 2):
        for d in range(2):
            out_share((1 if d == 0 else -1) * (ring // 2 - kk))
        move()
        for d in range(2):
            sums.add(kk - 1, d)
            sums.start(kk, d)
    out_share(0)
    move()
    own_cot.wait()
    own_again = pltpu.make_async_copy(tokens, xrow, io.at[8])
    own_again.start()
    own_again.wait()
    for d in range(2):
        sums.add(ring // 2 - 1, d)

    @pl.loop(0, local // norm_tile)
    def _(i):
        r = aligned(i, norm_tile)
        value = xrow[r].astype(F32) + part[at.t, r].astype(F32)
        resid[r] = value
        scale = inverse_rms(value)

        def store(cols, value):
            xrow[r, cols] = value

        norm_into(lambda cols: resid[r, cols], scale, 1, store)

    x_ring.start(1)
    own_x = pltpu.make_async_copy(xrow, x_full.at[at.t], io.at[0])
    resid_store = pltpu.make_async_copy(resid, residual_out, io.at[8])
    own_x.start()
    resid_store.start()
    move()
    for h in range(2, ring // 2 + 1):
        move()
        x_ring.wait(h - 1)
        x_ring.start(h)
    if len(moves) > len(batches) - groups:
        move()
    x_ring.wait(ring // 2)
    while moves:
        move()
    for line in (cot_ring, x_ring):
        line.sent()
    sums.sent()
    for a in range(pre):
        feed.finish(a)
    for copy in (normed_store, own_x, resid_store, *stores):
        copy.wait()


def forward_part(n, ring, pre, tokens, cotangent, w_full, ff_full, cosine, sine, q_tile=256):
    groups, bs = w_full.shape[0], w_full.shape[-1]
    chunks = ff_full.shape[0]
    local, width = tokens.shape
    rows = local * ring
    cols = groups * bs
    any_ = pl.BlockSpec(memory_space=pl.ANY)
    vmem = pl.BlockSpec(memory_space=pltpu.VMEM)
    dma = pltpu.SemaphoreType.DMA
    shape = jax.ShapeDtypeStruct
    half = ring // 2
    return pl.pallas_call(
        functools.partial(forward_kernel, n, ring, pre, min(q_tile, rows)),
        out_shape=[
            shape(w_full.shape, BF16),
            shape(ff_full.shape, BF16),
            shape((ring, local, width), BF16),
            shape((rows, cols), BF16),
            shape((rows, cols), BF16),
            shape((rows, cols), BF16),
            shape((rows, cols), BF16),
            shape((rows, 128), F32),
            shape((local, width), F32),
            shape((ring, local, width), BF16),
            shape((ring, local, width), BF16),
        ],
        in_specs=[any_] * 4 + [vmem] * 2,
        out_specs=[any_] * 11,
        input_output_aliases={2: 0, 3: 1},
        scratch_shapes=[
            pltpu.VMEM((ring, local, width), BF16),
            pltpu.VMEM((max(4, groups), n, 2, bs, bs), BF16),
            pltpu.VMEM((2 * n, 16, bs), BF16),
            pltpu.VMEM((rows, cols), BF16),
            pltpu.VMEM((rows, cols), BF16),
            pltpu.VMEM((rows, cols), BF16),
            pltpu.VMEM((rows, cols), BF16),
            pltpu.VMEM((rows, 128), F32),
            pltpu.VMEM((min(q_tile, rows), bs), F32),
            pltpu.VMEM((ring, local, width), BF16),
            pltpu.VMEM((2, half, local, width), BF16),
            pltpu.VMEM((local, width), BF16),
            pltpu.VMEM((local, width), F32),
            dma((2, n - 1, groups)), dma((2, n - 1, groups)),
            dma((groups,)), dma((groups,)),
            dma((2, n - 1, chunks)), dma((2, n - 1, chunks)),
            dma((chunks,)), dma((chunks,)),
            dma((2, half)), dma((2, half)), dma((2, half)), dma((2, half)),
            dma((2, half)), dma((2, half)), dma((2, half)), dma((2, half)),
            dma((9,)), dma((5,)), dma((2 * n - 1,)), dma((2 * n - 1,)),
        ],
        compiler_params=pltpu.CompilerParams(
            collective_id=1, has_side_effects=True, vmem_limit_bytes=56 * 2**20),
    )(tokens, cotangent, w_full, ff_full, cosine, sine)


def layer_kernel(
    n, ring, pre, pace, plan, q_tile, tile,
    ff_in, x_hbm, dy_hbm, residual, cotangent, tokens, normed_in, q_in, k_in, v_in, mixed_in, stats_in,
    w_full, cosine_in, sine_in,
    ff_full, output, grad_tokens, gain_grads, ff_result, ff_summed, ff_landed,
    att_result, att_summed, att_landed, out_hbm,
    part, land, dres_full, core_in, stage, got, total, gparts, gland, gsecond, gone, gtwo,
    w_send, w_recv, w_sib_send, w_sib_recv,
    f_send, f_recv, f_load, f_out, a_send, a_recv, a_load, a_out,
    core_send, core_recv, acore_send, acore_recv, store_sem,
    s1_send, s1_recv, s2_send, s2_recv, s3_send, s3_recv, x_send, x_recv, free_sem,
    g_send, g_recv, h_send, h_recv, io, load,
):
    at = Place(n, ring)
    c = at.c
    groups, _, _, _, bs = w_full.shape
    chunks, _, _, unit, _ = ff_full.shape
    local, width = tokens.shape
    rows = local * ring
    heads = bs // HEAD_DIM
    half = ring // 2
    weights = LineGather(at, ff_full, w_send, w_recv, w_sib_send, w_sib_recv)
    feed = LineSum(at, chunks, ff_summed, ff_landed, ff_result,
                   stage.at[:, :, :, pl.ds(0, unit)], got.at[:, pl.ds(0, unit)],
                   total.at[pl.ds(0, unit)],
                   f_send, f_recv, f_load, f_out)
    att = LineSum(at, groups, att_summed, att_landed, att_result, stage, got, total,
                  a_send, a_recv, a_load, a_out)
    sums1 = RingSum(at, part, land, s1_send, s1_recv)
    sums2 = RingSum(at, part, land, s2_send, s2_recv)
    sums3 = RingSum(at, part, land, s3_send, s3_recv)
    dres_ring = RingGather(at, dres_full.at[at.t], dres_full, x_send, x_recv)
    lag = max(0, n - pre)
    num, den, begin = pace

    def fetch(src, dst, i):
        return pltpu.make_async_copy(src, dst, io.at[i])

    x_in = fetch(x_hbm, part, 0)
    dy_in = fetch(dy_hbm, dres_full, 1)
    x_in.start()
    dy_in.start()
    at.barrier(with_all=True)

    def ticks_before(j):
        return (j >= begin) * ((num * (j - begin)) // den)

    def feed_phase(oacc, dacc, wv, pg, hid, dgate, dup, out_stage):
        x, dy = part, dres_full

        def loads(j):
            return [
                pltpu.make_async_copy(
                    ff_full.at[j, :, :, pl.ds(i * bs, bs)], wv.at[j % 3, i], load.at[j % 3, i])
                for i in range(3)
            ]

        def core_copy(j):
            return pltpu.make_async_remote_copy(
                pg.at[1 - c], core_in.at[j % 2, :, pl.ds(0, unit)],
                core_send.at[j % 2], core_recv.at[j % 2],
                device_id={"dp": at.sib}, device_id_type=MESH)

        def store(j):
            return pltpu.make_async_copy(pg.at[c], ff_summed.at[j], store_sem)

        for copy in loads(0):
            copy.start()

        @pl.loop(0, rows // 64)
        def _(i):
            r = aligned(i, 64)
            oacc[r] = jnp.zeros((64, width), F32)
            dacc[r] = jnp.zeros((64, width), F32)

        x_in.wait()
        dy_in.wait()
        per = max(1, min(tile // local, ring))

        def columns(ref, cols):
            return ref[:, :, cols].reshape(rows, bs)

        def weight_grads(cc, now):
            @pl.loop(0, n)
            def _(k):
                cols = aligned(2 * k + cc, bs)
                xt = columns(x, cols)
                pg[cc, k, pl.ds(0, bs)] = t_dot(xt, dgate[:, now]).astype(BF16)
                pg[cc, k, pl.ds(bs, bs)] = t_dot(xt, dup[:, now]).astype(BF16)
                pg[cc, k, pl.ds(2 * bs, bs)] = t_dot(columns(dy, cols), hid[:, now]).astype(BF16)

        def compute(j):
            slot = j % 3
            now = aligned(j % 2, bs)
            for copy in loads(j):
                copy.wait()

            @pl.when(j + 1 < pre)
            def _():
                for copy in loads(j + 1):
                    copy.start()

            @pl.loop(0, ring // per)
            def _(m):
                r = aligned(m, per * local)
                here = pl.ds(m * per, per)
                rows_x = x[here].reshape(per * local, width)
                gate = dot(rows_x, wv[slot, 0].reshape(width, bs))
                up = dot(rows_x, wv[slot, 1].reshape(width, bs))
                dh = dot(dy[here].reshape(per * local, width), wv[slot, 2].reshape(width, bs))
                s = jax.nn.sigmoid(gate)
                gs = gate * s
                hid[r, now] = (gs * up).astype(BF16)
                dup[r, now] = (dh * gs).astype(BF16)
                dgate[r, now] = (dh * up * (s + gs * (1 - s))).astype(BF16)

            weight_grads(1 - c, now)
            core_copy(j).start()

            @pl.when(j % 2 == 1)
            def _():
                one, two = (j + 2) % 3, slot

                @pl.loop(0, rows // tile)
                def _(m):
                    r = aligned(m, tile)
                    both = jnp.concatenate([dgate[r, :], dup[r, :]], axis=1)

                    @pl.loop(0, n)
                    def _(k):
                        def block(s, i):
                            return wv[s, i, k].reshape(2 * bs, bs)

                        cols = aligned(k, 2 * bs)
                        oacc[r, cols] += dot_t(
                            hid[r, :], jnp.concatenate([block(one, 2), block(two, 2)], axis=1))
                        dacc[r, cols] += dot_t(both, jnp.concatenate(
                            [block(one, 0), block(two, 0), block(one, 1), block(two, 1)], axis=1))

            weight_grads(c, now)
            core_copy(j).wait_recv()

            @pl.loop(0, n)
            def _(k):
                pg[c, k] = pg[c, k] + core_in[j % 2, k, pl.ds(0, unit)]

            store(j).start()
            core_copy(j).wait_send()

        def begin_step(i):
            return min(2 * i, i + max(pre - n, 0))

        @pl.loop(0, lag + chunks)
        def _(step):
            j = step - lag
            for i in range(chunks - pre):
                for e in range(n):
                    @pl.when(step == begin_step(i) + e)
                    def _():
                        weights.event(pre + i, e)

            @pl.when(j >= 1)
            def _():
                store(j - 1).wait()
                feed.event(j - 1, 0)

            for extra in range(2):
                tick = ticks_before(j) + extra
                for e in range(n - 1, 0, -1):
                    q = tick - (e - 1) + 2 * n
                    r = q // 2 - n

                    @pl.when((j >= 0) & (tick < ticks_before(j + 1)) & (q % 2 == 0)
                             & (r >= 0) & (r < chunks))
                    def _():
                        feed.event(r, e)

            @pl.when(j >= 0)
            def _():
                compute(j)

            for i in range(chunks - pre):
                @pl.when(step == begin_step(i) + n - 1)
                def _():
                    weights.finish(pre + i)

            @pl.when((j + 1 >= pre) & (j + 1 >= 1) & (j + 1 < chunks))
            def _():
                for copy in loads(j + 1):
                    copy.start()

        store(chunks - 1).wait()
        feed.event(chunks - 1, 0)

        @pl.loop(0, ring)
        def _(m):
            part[m] = dacc[aligned(m, local), :].astype(BF16)

        for d in range(2):
            sums1.start(0, d)

        piece = local // 2

        def put(m):
            return fetch(
                out_stage.at[m % 2], out_hbm.at[m // 2, pl.ds(m % 2 * piece, piece)], m % 2)

        for m in range(2 * ring):
            if m > 1:
                put(m - 2).wait()
            out_stage[m % 2] = oacc[m * piece : (m + 1) * piece, :].astype(BF16)
            put(m).start()
        for m in range(2 * ring - 2, 2 * ring):
            put(m).wait()

    pl.run_scoped(
        feed_phase,
        pltpu.VMEM((rows, width), F32),
        pltpu.VMEM((rows, width), F32),
        pltpu.VMEM((3, 3, n, 2, bs, bs), BF16),
        pltpu.VMEM((2, n, unit, bs), BF16),
        pltpu.VMEM((rows, 2 * bs), BF16),
        pltpu.VMEM((rows, 2 * bs), BF16),
        pltpu.VMEM((rows, 2 * bs), BF16),
        pltpu.VMEM((2, local // 2, width), BF16),
    )

    done = [0 if chunks < begin else (num * (chunks - begin)) // den]
    last = 2 * (chunks - 1) + n - 2

    planned = list(plan)
    moves = []

    def point():
        for _ in range(planned.pop(0) if planned else 1):
            if done[0] <= last:
                feed_tick()
                if done[0] > last:
                    feed.result(chunks - 1).wait()
            elif moves:
                att.event(*moves.pop(0))

    def feed_tick():
        tick = done[0]
        for e in range(n - 1, 0, -1):
            if (tick - e + 1) % 2 == 0 and 0 <= (tick - e + 1) // 2 < chunks:
                feed.event((tick - e + 1) // 2, e)
        done[0] += 1

    def attention_phase(
        normed, wv, gains, q, k, v, mixed, stats, dmix, dq, dk, dv, dproj, resid, dres, small, lined,
        gsum, pg, cosine, sine,
    ):
        resid_in = fetch(residual, resid, 0)
        cot_in = fetch(cotangent, lined, 1)
        gains_in = fetch(w_full.at[0, :, :, pl.ds(4 * bs, 16)], gains, 2)
        saved = [
            fetch(src, dst, 3 + i)
            for i, (src, dst) in enumerate(
                ((normed_in, normed), (q_in, q), (k_in, k), (v_in, v), (mixed_in, mixed)))
        ]
        weight_loads = [
            pltpu.make_async_copy(
                w_full.at[g, :, :, pl.ds(i * bs, bs)], wv.at[i, g], load.at[i, g])
            for g in range(groups) for i in range(4)
        ]
        saved += [fetch(cosine_in, cosine, 8), fetch(sine_in, sine, 9), fetch(stats_in, stats, 10)]
        for copy in (resid_in, cot_in, gains_in, *saved, *weight_loads):
            copy.start()

        def gain_of(row, i):
            return gains[i // 2, i % 2, row : row + 1, :].astype(F32)

        tile = min(64, local)

        def norm_back(value_of, grad_of, row, emit):
            gsum[row : row + 1, :] = jnp.zeros((1, width), F32)

            @pl.loop(0, local // tile)
            def _(i):
                r = aligned(i, tile)
                scale = inverse_rms(value_of(r, pl.ds(0, width)))
                inner = jnp.zeros((tile, 1), F32)
                for b in range(2 * n):
                    cols = pl.ds(b * bs, bs)
                    value = value_of(r, cols)
                    grad = grad_of(r, cols)
                    gsum[row : row + 1, cols] += jnp.sum(
                        grad * value * scale, axis=0, keepdims=True)
                    inner += jnp.sum(grad * gain_of(row, b) * value, axis=-1, keepdims=True)
                pull = scale * scale * scale * (inner / width)
                for b in range(2 * n):
                    cols = pl.ds(b * bs, bs)
                    emit(r, cols,
                         scale * grad_of(r, cols) * gain_of(row, b) - value_of(r, cols) * pull)

        for kk in range(half):
            point()
            for d in range(2):
                sums1.add(kk, d)
                if kk < half - 1:
                    sums1.start(kk + 1, d)
        for copy in (resid_in, cot_in, gains_in):
            copy.wait()

        def emit_residual(r, cols, value):
            total = lined[r, cols].astype(F32) + value
            dres[r, cols] = total
            dres_full[at.t, r, cols] = total.astype(BF16)

        norm_back(lambda r, cols: resid[r, cols],
                  lambda r, cols: part[at.t, r, cols].astype(F32), 1, emit_residual)
        dres_ring.start(1)
        sums1.sent()
        second_in = fetch(out_hbm, part, 0)
        second_in.start()
        for h in range(2, half + 1):
            point()
            dres_ring.wait(h - 1)
            dres_ring.start(h)
        point()
        second_in.wait()
        dres_ring.wait(half)
        for d in range(2):
            sums2.start(0, d)
        for copy in (*saved, *weight_loads):
            copy.wait()

        def core_copy(g):
            return pltpu.make_async_remote_copy(
                pg.at[1 - c], core_in.at[g], acore_send.at[g], acore_recv.at[g],
                device_id={"dp": at.sib}, device_id_type=MESH)

        def store(g):
            return pltpu.make_async_copy(pg.at[c], att_summed.at[g], store_sem)

        def attend_back(g, between):
            gcols = pl.ds(g * bs, bs)
            lanes = group_lanes(heads, bs)
            columns = lax.broadcasted_iota(jnp.int32, (1, 128), 1)
            scale = jnp.asarray(HEAD_DIM ** (-0.5), BF16)
            dk[...] = jnp.zeros_like(dk)
            dv[...] = jnp.zeros_like(dv)
            for i in range(rows // q_tile):
                r = pl.ds(i * q_tile, q_tile)
                dq[r] = jnp.zeros((q_tile, bs), F32)

                @pl.loop(0, heads)
                def _(h):
                    mask = lanes == h
                    scaled = only(mask, q[r, gcols]) * scale
                    dmh = only(mask, dmix[r])
                    log_total = jnp.sum(
                        jnp.where(columns == g * heads + h, stats[r], 0.0), axis=-1, keepdims=True)
                    inner = jnp.sum(
                        dmh.astype(F32) * mixed[r, gcols].astype(F32), axis=-1, keepdims=True)
                    d_query = 0.0
                    for keys, scores in score_parts(scaled, k, gcols, i, q_tile):
                        probs = jnp.exp(scores - log_total)
                        d_probs = dot_t(dmh, v[keys, gcols])
                        d_scores = (probs * (d_probs - inner)).astype(BF16)
                        d_query += dot(d_scores, only(mask, k[keys, gcols]))
                        dk[keys] += t_dot(d_scores, scaled)
                        dv[keys] += t_dot(probs.astype(BF16), dmh)
                    dq[r] += d_query

                between(i)

        def weight_grads(g, cc):
            gcols = pl.ds(g * bs, bs)

            @pl.loop(0, n)
            def _(b):
                cols = aligned(2 * b + cc, bs)
                x = normed[:, :, cols].reshape(rows, bs)
                for i in range(3):
                    pg[cc, b, pl.ds(i * bs, bs)] = t_dot(x, dproj[i, :, gcols]).astype(BF16)
                pg[cc, b, pl.ds(3 * bs, bs)] = t_dot(
                    dres_full[:, :, cols].reshape(rows, bs), mixed[:, gcols]).astype(BF16)

        second = [0]

        def second_sum():
            if second[0] < half:
                kk = second[0]
                for d in range(2):
                    sums2.add(kk, d)
                    if kk < half - 1:
                        sums2.start(kk + 1, d)
                second[0] += 1

        tiles = rows // q_tile

        def between(i):
            point()
            if i == tiles - 1:
                second_sum()

        for g in range(groups):
            gcols = pl.ds(g * bs, bs)

            @pl.loop(0, ring)
            def _(m):
                r = aligned(m, local)
                dmix[r] = dot(dres_full[m], wv[3, g].reshape(width, bs)).astype(BF16)

            attend_back(g, between)

            @pl.loop(0, ring)
            def _(m):
                r = aligned(m, local)
                for i, value in enumerate((dq[r] * HEAD_DIM ** (-0.5), dk[r])):
                    dproj[i, r, gcols] = rope(
                        value, cosine[r, :], sine[r, :], back=True).astype(BF16)
                dproj[2, r, gcols] = dv[r].astype(BF16)

            weight_grads(g, 1 - c)
            core_copy(g).start()
            weight_grads(g, c)
            core_copy(g).wait_recv()

            @pl.loop(0, n)
            def _(b):
                pg[c, b] = pg[c, b] + core_in[g, b]

            store(g).start()
            core_copy(g).wait_send()
            store(g).wait()
            att.event(g, 0)
            moves.extend((g, e) for e in range(1, n))

        while second[0] < half:
            second_sum()
        sums2.sent()

        @pl.loop(0, local // tile)
        def _(i):
            r = aligned(i, tile)
            lined[r] = (resid[r] + part[at.t, r].astype(F32)).astype(BF16)

        out_store = fetch(lined, output, 0)
        out_store.start()
        for way in (1, -1):
            pl.semaphore_signal(
                free_sem, inc=1, device_id={"tensor": at.member(way)}, device_id_type=MESH)

        def share(offset):
            m = at.member(offset)
            r = aligned(m, local)
            for b in range(n):
                block = sum(
                    dot_t(dproj[i, r, g * bs : (g + 1) * bs], wv[i, g, b].reshape(2 * bs, bs))
                    for i in range(3) for g in range(groups)
                )
                part[m, :, b * 2 * bs : (b + 1) * 2 * bs] = block.astype(BF16)

        share(half)
        pl.semaphore_wait(free_sem, 2)
        for d in range(2):
            sums3.start(0, d)

        tok_in = fetch(tokens, small, 1)
        dres_ring.sent()
        tok_in.start()
        point()
        for kk in range(1, half):
            for d in range(2):
                share((1 if d == 0 else -1) * (half - kk))
            for d in range(2):
                sums3.add(kk - 1, d)
                sums3.start(kk, d)
            point()
        share(0)
        point()
        for d in range(2):
            sums3.add(half - 1, d)
        tok_in.wait()
        out_store.wait()

        def emit_tokens(r, cols, value):
            lined[r, cols] = (dres[r, cols] + value).astype(BF16)

        norm_back(lambda r, cols: small[r, cols].astype(F32),
                  lambda r, cols: part[at.t, r, cols].astype(F32), 0, emit_tokens)
        token_store = fetch(lined, grad_tokens, 0)
        token_store.start()
        for b in range(2 * n):
            gparts[b, 0:2] = gsum[0:2, b * bs : (b + 1) * bs]
            gparts[b, 2:8] = jnp.zeros((6, bs), F32)
        over_dp = SmallSum("dp", 2 * at.z + c, 2 * n, lambda i: gparts.at[i], gland, g_send, g_recv)
        gone[...] = over_dp.total()
        over_ring = SmallSum("tensor", at.t, ring, lambda i: gone, gsecond, h_send, h_recv)
        gtwo[...] = over_ring.total()
        gain_store = fetch(gtwo, gain_grads, 1)
        gain_store.start()
        while done[0] <= last or moves:
            point()
        att.result(groups - 1).wait()
        token_store.wait()
        gain_store.wait()
        sums3.sent()

    cols = groups * bs
    pl.run_scoped(
        attention_phase,
        pltpu.VMEM((ring, local, width), BF16),
        pltpu.VMEM((4, groups, n, 2, bs, bs), BF16),
        pltpu.VMEM((n, 2, 16, bs), BF16),
        pltpu.VMEM((rows, cols), BF16),
        pltpu.VMEM((rows, cols), BF16),
        pltpu.VMEM((rows, cols), BF16),
        pltpu.VMEM((rows, cols), BF16),
        pltpu.VMEM((rows, 128), F32),
        pltpu.VMEM((rows, bs), BF16),
        pltpu.VMEM((rows, bs), F32),
        pltpu.VMEM((rows, bs), F32),
        pltpu.VMEM((rows, bs), F32),
        pltpu.VMEM((3, rows, cols), BF16),
        pltpu.VMEM((local, width), F32),
        pltpu.VMEM((local, width), F32),
        pltpu.VMEM((local, width), BF16),
        pltpu.VMEM((local, width), BF16),
        pltpu.VMEM((8, width), F32),
        pltpu.VMEM((2, n, 4 * bs, bs), BF16),
        pltpu.VMEM((rows, bs), F32),
        pltpu.VMEM((rows, bs), F32),
    )


def layer_part(
    n, ring, pre, pace, plan, ff_full, x, dy, residual, cotangent, tokens, normed, q, k, v, mixed, stats,
    w_full, cosine, sine, q_tile=256, tile=512,
):
    groups, _, _, _, bs = w_full.shape
    chunks, _, _, unit, _ = ff_full.shape
    local, width = tokens.shape
    rows = local * ring
    half = ring // 2
    any_ = pl.BlockSpec(memory_space=pl.ANY)
    dma = pltpu.SemaphoreType.DMA
    shape = jax.ShapeDtypeStruct
    big = (ring, local, width)
    wide = 4 * bs
    return pl.pallas_call(
        functools.partial(
            layer_kernel, n, ring, pre, pace, plan, min(q_tile, rows), min(tile, rows)),
        out_shape=[
            shape(ff_full.shape, BF16),
            shape((local, width), BF16),
            shape((local, width), BF16),
            shape((8, bs), F32),
            shape((chunks, unit, bs), BF16),
            shape((chunks, n, unit, bs), BF16),
            shape((2, chunks, n - 1, unit, bs), BF16),
            shape((groups, wide, bs), BF16),
            shape((groups, n, wide, bs), BF16),
            shape((2, groups, n - 1, wide, bs), BF16),
            shape(big, BF16),
        ],
        in_specs=[any_] * 15,
        out_specs=[any_] * 11,
        input_output_aliases={0: 0},
        scratch_shapes=[
            pltpu.VMEM(big, BF16),
            pltpu.VMEM((2, half, local, width), BF16),
            pltpu.VMEM(big, BF16),
            pltpu.VMEM((max(2, groups), n, wide, bs), BF16),
            pltpu.VMEM((2, n - 2, n // 2, wide, bs), BF16),
            pltpu.VMEM((4, wide, bs), BF16),
            pltpu.VMEM((wide, bs), BF16),
            pltpu.VMEM((2 * n, 8, bs), F32),
            pltpu.VMEM((2 * n - 1, 8, bs), F32),
            pltpu.VMEM((ring - 1, 8, bs), F32),
            pltpu.VMEM((8, bs), F32),
            pltpu.VMEM((8, bs), F32),
            dma((2, n - 1, chunks)), dma((2, n - 1, chunks)), dma((chunks,)), dma((chunks,)),
            dma((2, n - 1, chunks)), dma((2, n - 1, chunks)), dma((4,)), dma,
            dma((2, n - 1, groups)), dma((2, n - 1, groups)), dma((4,)), dma,
            dma((2,)), dma((2,)), dma((groups,)), dma((groups,)), dma,
            dma((2, half)), dma((2, half)), dma((2, half)), dma((2, half)),
            dma((2, half)), dma((2, half)), dma((2, half)), dma((2, half)),
            pltpu.SemaphoreType.REGULAR,
            dma((2 * n - 1,)), dma((2 * n - 1,)), dma((ring - 1,)), dma((ring - 1,)),
            dma((11,)), dma((4, max(4, groups))),
        ],
        compiler_params=pltpu.CompilerParams(
            collective_id=2, has_side_effects=True, vmem_limit_bytes=63 * 2**20),
    )(ff_full, x, dy, residual, cotangent, tokens, normed, q, k, v, mixed, stats,
      w_full, cosine, sine)


PREFETCH = 6
PACE = (1, 1, 2)
PLAN = (1, 2, 2, 2) + (1, 0, 1, 0) + (1, 1, 0, 1) + (1, 2, 1)


def pack_kernel(place, q, k, v, o, gain_attn, gain_mlp, gate, up, down, att, ff):
    bs = q.shape[0]
    for i, ref in enumerate((q, k, v)):
        att[i * bs : (i + 1) * bs] = ref[...]
    att[3 * bs : 4 * bs] = o[...].T
    row = lax.broadcasted_iota(jnp.int32, (16, bs), 0)
    first, second = (g[...].astype(F32) for g in (gain_attn, gain_mlp))
    gains = jnp.where(row == 0, first, jnp.where(row == 1, second, 0.0))
    att[4 * bs : 4 * bs + 16] = gains.astype(BF16)
    ff[0:bs] = gate[...]
    ff[bs : 2 * bs] = up[...]
    ff[2 * bs : 3 * bs] = down[...].T


def pack(w_query, w_key, w_value, w_out, gain_attn, gain_mlp, w_gate, w_up, w_down):
    bs = w_query.shape[0]
    n = lax.axis_size("dp") // 2
    groups, chunks = w_query.shape[1] // bs, w_gate.shape[1] // bs

    def at_group(j):
        return jnp.minimum(j, groups - 1)

    col = pl.BlockSpec((bs, bs), lambda j, p: (0, at_group(j)))
    row = pl.BlockSpec((bs, bs), lambda j, p: (at_group(j), 0))
    gain = pl.BlockSpec((1, bs), lambda j, p: (0, 0))
    wide = pl.BlockSpec((bs, bs), lambda j, p: (0, j))
    tall = pl.BlockSpec((bs, bs), lambda j, p: (j, 0))
    return pl.pallas_call(
        pack_kernel,
        out_shape=[
            jax.ShapeDtypeStruct((groups, n, 2, 4 * bs + 16, bs), BF16),
            jax.ShapeDtypeStruct((chunks, n, 2, 3 * bs, bs), BF16),
        ],
        grid_spec=pltpu.PrefetchScalarGridSpec(
            num_scalar_prefetch=1,
            grid=(chunks,),
            in_specs=[col, col, col, row, gain, gain, wide, wide, tall],
            out_specs=[
                pl.BlockSpec((None, None, None, 4 * bs + 16, bs),
                             lambda j, p: (at_group(j), p[0], p[1], 0, 0)),
                pl.BlockSpec((None, None, None, 3 * bs, bs), lambda j, p: (j, p[0], p[1], 0, 0)),
            ],
        ),
    )(jnp.stack([lax.axis_index("dp") // 2, lax.axis_index("dp") % 2]),
      w_query, w_key, w_value, w_out, gain_attn.reshape(1, bs), gain_mlp.reshape(1, bs),
      w_gate, w_up, w_down)


def unpack_kernel(att, ff, q, k, v, o, gate, up, down):
    bs = q.shape[0]
    for i, ref in enumerate((q, k, v)):
        ref[...] = att[0, i * bs : (i + 1) * bs].astype(F32)
    o[...] = att[0, 3 * bs : 4 * bs].astype(F32).T
    gate[...] = ff[0, 0:bs].astype(F32)
    up[...] = ff[0, bs : 2 * bs].astype(F32)
    down[...] = ff[0, 2 * bs : 3 * bs].astype(F32).T


def unpack(att, ff):
    groups, chunks, bs = att.shape[0], ff.shape[0], ff.shape[2]

    def at_group(j):
        return jnp.minimum(j, groups - 1)

    shape = jax.ShapeDtypeStruct
    col = pl.BlockSpec((bs, bs), lambda j: (0, at_group(j)))
    row = pl.BlockSpec((bs, bs), lambda j: (at_group(j), 0))
    wide = pl.BlockSpec((bs, bs), lambda j: (0, j))
    tall = pl.BlockSpec((bs, bs), lambda j: (j, 0))
    return pl.pallas_call(
        unpack_kernel,
        grid=(chunks,),
        out_shape=[shape((bs, groups * bs), F32)] * 3 + [shape((groups * bs, bs), F32)]
        + [shape((bs, chunks * bs), F32)] * 2 + [shape((chunks * bs, bs), F32)],
        in_specs=[
            pl.BlockSpec((1, 4 * bs, bs), lambda j: (at_group(j), 0, 0)),
            pl.BlockSpec((1, 3 * bs, bs), lambda j: (j, 0, 0)),
        ],
        out_specs=[col] * 3 + [row] + [wide] * 2 + [tall],
    )(att, ff)


def rotary_tables(row_count, width):
    frequency = rope_base ** (-np.arange(HEAD_DIM // 2) * 2.0 / HEAD_DIM)
    angles = (np.arange(row_count) % LEN)[:, None] * frequency[None, :]
    angles = np.tile(angles, (1, width // (HEAD_DIM // 2)))
    return np.cos(angles).astype(np.float32), np.sin(angles).astype(np.float32)


def shards(
    tokens, gain_attn, w_query, w_key, w_value, w_out, gain_mlp, w_gate, w_up, w_down, cotangent
):
    dp, ring = lax.axis_size("dp"), lax.axis_size("tensor")
    n = dp // 2
    local, width = tokens.shape
    rows = local * ring
    assert rows == LEN
    bs = w_query.shape[0]
    cosine, sine = rotary_tables(rows, bs)
    w_start, ff_start = pack(
        w_query, w_key, w_value, w_out, gain_attn, gain_mlp, w_gate, w_up, w_down
    )
    w_full, ff_full, normed, q, k, v, mixed, stats, residual, x, dy = forward_part(
        n, ring, PREFETCH, tokens, cotangent, w_start, ff_start, cosine, sine
    )
    _, output, grad_tokens, gain_grads, ff_grads, _, _, att_grads, _, _, _ = layer_part(
        n, ring, PREFETCH, PACE, PLAN, ff_full, x, dy, residual, cotangent, tokens,
        normed, q, k, v, mixed, stats, w_full, cosine, sine,
    )
    g_query, g_key, g_value, g_out, g_gate, g_up, g_down = unpack(att_grads, ff_grads)
    return (
        output,
        grad_tokens,
        gain_grads[0],
        g_query,
        g_key,
        g_value,
        g_out,
        gain_grads[1],
        g_gate,
        g_up,
        g_down,
    )


def solution(mesh):
    placed = (
        P(("dp", "tensor"), None),
        P("dp"),
        P("dp", "tensor"),
        P("dp", "tensor"),
        P("dp", "tensor"),
        P("tensor", "dp"),
        P("dp"),
        P("dp", "tensor"),
        P("dp", "tensor"),
        P("tensor", "dp"),
        P(("dp", "tensor"), None),
    )
    return jax.shard_map(
        shards,
        mesh=mesh,
        in_specs=placed,
        out_specs=(
            P(("dp", "tensor"), None),
            P(("dp", "tensor"), None),
            P("dp"),
            P("dp", "tensor"),
            P("dp", "tensor"),
            P("dp", "tensor"),
            P("tensor", "dp"),
            P("dp"),
            P("dp", "tensor"),
            P("dp", "tensor"),
            P("tensor", "dp"),
        ),
        check_vma=False,
    )
```

```python
import functools

import jax
import jax.numpy as jnp
import numpy as np
from jax import lax
from jax.experimental import pallas as pl
from jax.experimental.pallas import tpu as pltpu
from jax.sharding import PartitionSpec as P

HEAD_DIM = 64
LEN = 1024
MESH = pl.DeviceIdType.MESH
BF16 = jnp.bfloat16
F32 = jnp.float32

norm_eps = 1e-05
rope_base = 130000.0
masked_score = -1e30


def dot(a, b):
    return jnp.dot(a, b, preferred_element_type=F32)


def dot_t(a, b):
    return lax.dot_general(a, b, (((1,), (1,)), ((), ())), preferred_element_type=F32)


def t_dot(a, b):
    return lax.dot_general(a, b, (((0,), (0,)), ((), ())), preferred_element_type=F32)


def aligned(index, size):
    return pl.ds(pl.multiple_of(index * size, size), size)


class Place:
    def __init__(self, n, ring):
        me = lax.axis_index("dp")
        self.n, self.ring = n, ring
        self.z, self.c = me // 2, me % 2
        self.right, self.left = me + 2, me - 2
        self.sib = me + 1 - 2 * self.c
        self.has_r, self.has_l = self.z < n - 1, self.z > 0
        t = lax.axis_index("tensor")
        odd = t % 2
        self.t = t
        self.p = (1 - odd) * (t // 2) + odd * (ring - 1 - t // 2)

    def member(self, offset):
        p = (self.p + offset + self.ring) % self.ring
        back = (p >= self.ring // 2).astype(jnp.int32)
        return (1 - back) * (2 * p) + back * (2 * (self.ring - 1 - p) + 1)

    def barrier(self, with_ring=True, with_all=False):
        sem = pltpu.get_barrier_semaphore()

        def greet(peer):
            pl.semaphore_signal(sem, inc=1, device_id=peer, device_id_type=MESH)

        if with_all:
            for k in range(1, 2 * self.n):
                greet({"dp": (2 * self.z + self.c + k) % (2 * self.n)})
            for k in range(1, self.ring):
                greet({"tensor": (self.t + k) % self.ring})
            pl.semaphore_wait(sem, 2 * self.n - 1 + self.ring - 1)
            return

        greet({"dp": self.sib})
        if with_ring:
            greet({"tensor": self.member(1)})
            greet({"tensor": self.member(-1)})

        @pl.when(self.has_r)
        def _():
            greet({"dp": self.right})

        @pl.when(self.has_l)
        def _():
            greet({"dp": self.left})

        peers = self.has_r.astype(jnp.int32) + self.has_l.astype(jnp.int32)
        pl.semaphore_wait(sem, peers + (3 if with_ring else 1))

    def neighbour(self, d):
        return self.right if d == 0 else self.left

    def sends_to(self, d):
        return self.has_r if d == 0 else self.has_l

    def along(self, d, k):
        return self.z + k if d == 0 else self.z - k

    def depth(self, d):
        return self.z if d == 0 else self.n - 1 - self.z


class LineGather:
    def __init__(self, at, full, send, recv, sib_send, sib_recv):
        self.at, self.full = at, full
        self.send, self.recv = send, recv
        self.sib_send, self.sib_recv = sib_send, sib_recv

    def hop(self, a, h, d):
        at = self.at
        block = self.full.at[a, at.along(d, 1 - h), at.c]
        return pltpu.make_async_remote_copy(
            block, block, self.send.at[d, h - 1, a], self.recv.at[d, h - 1, a],
            device_id={"dp": at.neighbour(d)}, device_id_type=MESH)

    def sends(self, h, d):
        return self.at.sends_to(d) & (self.at.depth(d) >= h - 1)

    def arrives(self, h, d):
        return self.at.depth(d) >= h

    def to_sib(self, a):
        part = self.full.at[a, :, self.at.c]
        return pltpu.make_async_remote_copy(
            part, part, self.sib_send.at[a], self.sib_recv.at[a],
            device_id={"dp": self.at.sib}, device_id_type=MESH)

    def take(self, a, h):
        for d in range(2):
            @pl.when(self.arrives(h, d))
            def _():
                self.hop(a, h, d).wait_recv()

    def give(self, a, h):
        for d in range(2):
            @pl.when(self.sends(h, d))
            def _():
                self.hop(a, h, d).start()

    def event(self, a, e):
        n = self.at.n
        if e > 0:
            self.take(a, e)
        if e < n - 1:
            self.give(a, e + 1)
        else:
            self.to_sib(a).start()

    def given(self, a):
        self.to_sib(a).wait_recv()
        self.to_sib(a).wait_send()

    def finish(self, a):
        self.given(a)
        self.sent(a)

    def sent(self, a, hops=None):
        for h in hops or range(1, self.at.n):
            for d in range(2):
                @pl.when(self.sends(h, d))
                def _():
                    self.hop(a, h, d).wait_send()


class LineSum:
    def __init__(self, at, chunks, sums, land, out, stage, got, total, send, recv, load, out_sem):
        self.at, self.chunks = at, chunks
        self.sums, self.land, self.out = sums, land, out
        self.stage, self.got, self.total = stage, got, total
        self.send, self.recv, self.load, self.out_sem = send, recv, load, out_sem

    def valid(self, j):
        return (j >= 0) & (j < self.chunks)

    def copy(self, j, s, d, staged):
        at = self.at
        src = self.stage.at[d, s - 2, j % (at.n // 2)] if staged else self.sums.at[j, at.along(d, at.n - s)]
        return pltpu.make_async_remote_copy(
            src, self.land.at[d, j, s - 1], self.send.at[d, s - 1, j], self.recv.at[d, s - 1, j],
            device_id={"dp": at.neighbour(d)}, device_id_type=MESH)

    def arrival(self, j, s, d):
        return pltpu.make_async_remote_copy(
            self.land.at[d, j, s - 1], self.land.at[d, j, s - 1],
            self.send.at[d, s - 1, j], self.recv.at[d, s - 1, j],
            device_id={"dp": self.at.sib}, device_id_type=MESH)

    def arrives(self, s, d):
        depth = self.at.depth(d)
        return (depth > 0) & (depth <= s)

    def get(self, src, k):
        return pltpu.make_async_copy(src, self.got.at[k], self.load.at[k])

    def event(self, j, e):
        at, n = self.at, self.at.n
        if e == 0:
            for s in range(1, n):
                for d in range(2):
                    @pl.when(at.sends_to(d) & (at.depth(d) == 0))
                    def _():
                        self.copy(j, s, d, False).start()

        elif e < n - 1:
            s = e + 1
            here = [at.sends_to(d) & (at.depth(d) > 0) & (at.depth(d) < s) for d in range(2)]

            def own(d):
                return self.get(self.sums.at[j, at.along(d, n - s)], d)

            def came(d):
                return self.get(self.land.at[d, j, s - 2], 2 + d)

            for d in range(2):
                @pl.when(here[d])
                def _():
                    own(d).start()

            for d in range(2):
                @pl.when(here[d])
                def _():
                    self.arrival(j, s - 1, d).wait_recv()
                    came(d).start()

            for d in range(2):
                @pl.when(here[d])
                def _():
                    own(d).wait()
                    came(d).wait()
                    self.stage[d, s - 2, j % (n // 2)] = self.got[d] + self.got[2 + d]
                    self.copy(j, s, d, True).start()
        else:
            own = self.get(self.sums.at[j, at.z], 0)
            own.start()

            @pl.when(j > 0)
            def _():
                self.result(j - 1).wait()

            for d in range(2):
                @pl.when(at.depth(d) > 0)
                def _():
                    self.arrival(j, n - 1, d).wait_recv()
                    self.get(self.land.at[d, j, n - 2], 2 + d).start()

            own.wait()

            @pl.when(at.depth(0) == 0)
            def _():
                self.get(self.land.at[1, j, n - 2], 3).wait()
                self.total[...] = self.got[0] + self.got[3]

            @pl.when(at.depth(1) == 0)
            def _():
                self.get(self.land.at[0, j, n - 2], 2).wait()
                self.total[...] = self.got[0] + self.got[2]

            @pl.when((at.depth(0) > 0) & (at.depth(1) > 0))
            def _():
                for d in range(2):
                    self.get(self.land.at[d, j, n - 2], 2 + d).wait()
                self.total[...] = self.got[0] + self.got[2] + self.got[3]

            self.result(j).start()
            self.sent(j)

    def result(self, j):
        return pltpu.make_async_copy(self.total, self.out.at[j], self.out_sem)

    def sent(self, j):
        at, n = self.at, self.at.n
        for s in range(1, n):
            for d in range(2):
                @pl.when(at.sends_to(d) & (at.depth(d) == 0))
                def _():
                    self.copy(j, s, d, False).wait_send()

                if s >= 2:
                    @pl.when(at.sends_to(d) & (at.depth(d) > 0) & (at.depth(d) < s))
                    def _():
                        self.copy(j, s, d, True).wait_send()


class RingGather:
    def __init__(self, at, own, full, send, recv):
        self.at, self.own, self.full, self.send, self.recv = at, own, full, send, recv

    def copy(self, h, d):
        at = self.at
        way = 1 if d == 0 else -1
        owner = at.member(-way * (h - 1))
        rows = self.full.shape[1]
        part = pl.ds(0, rows)
        if h == at.ring // 2:
            part = pl.ds(d * (rows // 2), rows // 2)
        dst = self.full.at[owner, part]
        src = self.own.at[part] if h == 1 else dst
        return pltpu.make_async_remote_copy(
            src, dst, self.send.at[d, h - 1], self.recv.at[d, h - 1],
            device_id={"tensor": at.member(way)}, device_id_type=MESH)

    def start(self, h):
        for d in range(2):
            self.copy(h, d).start()

    def wait(self, h):
        for d in range(2):
            self.copy(h, d).wait_recv()

    def sent(self):
        for h in range(1, self.at.ring // 2 + 1):
            for d in range(2):
                self.copy(h, d).wait_send()


class SmallSum:
    def __init__(self, axis, me, size, part_of, land, send, recv):
        self.axis, self.me, self.size, self.part_of = axis, me, size, part_of
        self.land, self.send, self.recv = land, send, recv

    def copy(self, k):
        peer = (self.me + k) % self.size
        return pltpu.make_async_remote_copy(
            self.part_of(peer), self.land.at[k - 1], self.send.at[k - 1], self.recv.at[k - 1],
            device_id={self.axis: peer}, device_id_type=MESH)

    def total(self):
        for k in range(1, self.size):
            self.copy(k).start()
        result = self.part_of(self.me)[...]
        for k in range(1, self.size):
            self.copy(k).wait_recv()
            result = result + self.land[k - 1]
        for k in range(1, self.size):
            self.copy(k).wait_send()
        return result


class SmallGather:
    def __init__(self, axis, me, size, own, full, send, recv):
        self.axis, self.me, self.size, self.own, self.full = axis, me, size, own, full
        self.send, self.recv = send, recv

    def copy(self, k, slot):
        return pltpu.make_async_remote_copy(
            self.own, self.full.at[slot], self.send.at[k - 1], self.recv.at[k - 1],
            device_id={self.axis: (self.me + k) % self.size}, device_id_type=MESH)

    def start(self):
        for k in range(1, self.size):
            self.copy(k, self.me).start()

    def wait(self):
        for k in range(1, self.size):
            self.copy(k, (self.me + self.size - k) % self.size).wait_recv()
        for k in range(1, self.size):
            self.copy(k, self.me).wait_send()


class RingSum:
    def __init__(self, at, part, land, send, recv):
        self.at, self.part, self.land, self.send, self.recv = at, part, land, send, recv
        self.stages = at.ring // 2

    def rows_of(self, k, d):
        rows = self.part.shape[1]
        return pl.ds(d * (rows // 2), rows // 2) if k == 0 else pl.ds(0, rows)

    def target(self, k, d):
        return self.at.member((1 if d == 0 else -1) * (self.stages - k))

    def copy(self, k, d):
        r = self.rows_of(k, d)
        return pltpu.make_async_remote_copy(
            self.part.at[self.target(k, d), r], self.land.at[d, k, r],
            self.send.at[d, k], self.recv.at[d, k],
            device_id={"tensor": self.at.member(1 if d == 0 else -1)}, device_id_type=MESH)

    def start(self, k, d):
        self.copy(k, d).start()

    def add(self, k, d):
        self.copy(k, d).wait_recv()
        block = self.target(k + 1, d)
        rows = self.part.shape[1]
        half = rows // 2
        quarter = max(half // 4, 16)
        first = d * half if k == 0 else 0
        count = (half if k == 0 else rows) // quarter

        @pl.loop(0, count)
        def _(i):
            r = pl.ds(pl.multiple_of(first + i * quarter, quarter), quarter)
            self.part[block, r] = self.part[block, r] + self.land[d, k, r]

    def sent(self):
        for k in range(self.stages):
            for d in range(2):
                self.copy(k, d).wait_send()


def group_lanes(heads, width):
    return lax.broadcasted_iota(jnp.int32, (1, width), 1) // HEAD_DIM


def rope(values, cosine, sine, back=False):
    width = values.shape[-1]
    half = HEAD_DIM // 2
    first = lax.broadcasted_iota(jnp.int32, (1, width), 1) % HEAD_DIM < half
    ahead = pltpu.roll(values, width - half, 1)
    behind = pltpu.roll(values, half, 1)
    turned = jnp.where(first, -ahead, behind)
    return values * cosine - turned * sine if back else values * cosine + turned * sine


def inverse_rms(values):
    return lax.rsqrt(jnp.mean(values * values, axis=-1, keepdims=True) + norm_eps)


def score_parts(q_rows, k, cols, i, tile):
    diag = pl.ds(i * tile, tile)
    own = dot_t(q_rows, k[diag, cols])
    row = lax.broadcasted_iota(jnp.int32, own.shape, 0)
    column = lax.broadcasted_iota(jnp.int32, own.shape, 1)
    parts = [(diag, jnp.where(row >= column, own, masked_score))]
    if i > 0:
        past = pl.ds(0, i * tile)
        parts.append((past, dot_t(q_rows, k[past, cols])))
    return parts


def only(mask, values):
    return jnp.where(mask, values, jnp.zeros_like(values))


def forward_kernel(
    n, ring, pre, q_tile,
    tokens, cotangent, w_in, ff_in, cosine, sine,
    w_full, ff_full, normed_out, q_out, k_out, v_out, mixed_out, stats_out, residual_out, x_full, dy_full,
    tok, wv, gains, q, k, v, mixed, stats, acc, part, land, xrow, resid,
    a_send, a_recv, a_sib_send, a_sib_recv,
    f_send, f_recv, f_sib_send, f_sib_recv,
    t_send, t_recv, c_send, c_recv, x_send, x_recv, s_send, s_recv, io, load, gain_send, gain_recv,
):
    at = Place(n, ring)
    groups, _, _, _, bs = w_full.shape
    local, width = tokens.shape
    rows = local * ring
    heads = bs // HEAD_DIM
    att = LineGather(at, w_full, a_send, a_recv, a_sib_send, a_sib_recv)
    feed = LineGather(at, ff_full, f_send, f_recv, f_sib_send, f_sib_recv)
    tok_ring = RingGather(at, tokens, tok, t_send, t_recv)
    cot_ring = RingGather(at, cotangent, dy_full, c_send, c_recv)
    x_ring = RingGather(at, xrow, x_full, x_send, x_recv)
    sums = RingSum(at, part, land, s_send, s_recv)

    own_tok = pltpu.make_async_copy(tokens, tok.at[at.t], io.at[0])
    cot_in = pltpu.make_async_copy(cotangent, xrow, io.at[1])
    own_cot = pltpu.make_async_copy(xrow, dy_full.at[at.t], io.at[1])
    gain_in = pltpu.make_async_copy(
        w_full.at[0, at.z, at.c, pl.ds(4 * bs, 16)], gains.at[2 * at.z + at.c], io.at[2])
    own_tok.start()
    cot_in.start()
    gain_in.start()
    at.barrier(with_all=True)
    gain_all = SmallGather(
        "dp", 2 * at.z + at.c, 2 * n, gains.at[2 * at.z + at.c], gains, gain_send, gain_recv)

    first = (pre + 1) // 2
    batches = [[(att, g)] for g in range(groups)]
    for lot in (range(first), range(first, pre)):
        if len(lot):
            batches.append([(feed, a) for a in lot])

    def event(b, e):
        if b < len(batches):
            for line, a in batches[b]:
                if line is att or a < first or e < n - 2:
                    line.event(a, e)
                elif e == n - 2:
                    line.take(a, e)

    def loads(g):
        return [
            pltpu.make_async_copy(w_full.at[g, :, :, pl.ds(i * bs, bs)], wv.at[i], load.at[i])
            for i in range(3)
        ]

    for g in range(groups):
        event(g, 0)
    tok_ring.start(1)
    stats[...] = jnp.zeros_like(stats)
    gain_in.wait()
    gain_all.start()
    for g in range(groups):
        event(g, 1)
    cot_in.wait()
    own_cot.start()
    tok_ring.wait(1)
    tok_ring.start(2)
    event(0, 2)
    for h in range(3, ring // 2 + 1):
        tok_ring.wait(h - 1)
        tok_ring.start(h)
    tok_ring.wait(ring // 2)
    cot_ring.start(1)
    gain_all.wait()
    own_tok.wait()
    tok_ring.sent()

    def norm_into(values, scale, row, store):
        for i in range(2 * n):
            gain = gains[i, row : row + 1, :].astype(F32)
            cols = pl.ds(i * bs, bs)
            store(cols, (values(cols) * scale * gain).astype(BF16))

    norm_tile = min(64, local)

    @pl.loop(0, ring)
    def _(m):
        @pl.loop(0, local // norm_tile)
        def _(i):
            r = aligned(i, norm_tile)
            scale = inverse_rms(tok[m, r].astype(F32))

            def store(cols, value):
                tok[m, r, cols] = value

            norm_into(lambda cols: tok[m, r, cols].astype(F32), scale, 0, store)

    normed_store = pltpu.make_async_copy(tok, normed_out, io.at[2])
    normed_store.start()

    def project(g):
        cols = pl.ds(g * bs, bs)

        @pl.loop(0, ring)
        def _(m):
            r = aligned(m, local)
            x = tok[m]
            query = dot(x, wv[0].reshape(width, bs))
            key = dot(x, wv[1].reshape(width, bs))
            q[r, cols] = rope(query, cosine[r, :], sine[r, :]).astype(BF16)
            k[r, cols] = rope(key, cosine[r, :], sine[r, :]).astype(BF16)
            v[r, cols] = dot(x, wv[2].reshape(width, bs)).astype(BF16)

    def attend(g, between):
        cols = pl.ds(g * bs, bs)
        lanes = group_lanes(heads, bs)
        columns = lax.broadcasted_iota(jnp.int32, (1, 128), 1)
        scale = jnp.asarray(HEAD_DIM ** (-0.5), BF16)
        for i in range(rows // q_tile):
            r = pl.ds(i * q_tile, q_tile)
            acc[...] = jnp.zeros_like(acc)

            @pl.loop(0, heads)
            def _(h):
                mask = lanes == h
                scaled = only(mask, q[r, cols]) * scale
                parts = score_parts(scaled, k, cols, i, q_tile)
                most = functools.reduce(
                    jnp.maximum, [jnp.max(s, axis=-1, keepdims=True) for _, s in parts])
                total, mix = 0.0, 0.0
                for keys, scores in parts:
                    exp_scores = jnp.exp(scores - most)
                    total += jnp.sum(exp_scores, axis=-1, keepdims=True)
                    mix += dot(exp_scores.astype(BF16), only(mask, v[keys, cols]))
                acc[...] += mix * (1.0 / total)
                stats[r] = jnp.where(columns == g * heads + h, most + jnp.log(total), stats[r])

            mixed[r, cols] = acc[...].astype(BF16)
            between(i)

    for e in range(2, n - 1):
        for g in range(groups):
            if (g, e) != (0, 2):
                event(g, e)
    for b in range(groups, len(batches)):
        event(b, 0)
    def fetch(g):
        att.finish(g)
        for copy in loads(g):
            copy.start()

    event(0, n - 1)
    fetch(0)
    for g in range(groups):
        for copy in loads(g):
            copy.wait()
        project(g)
        if g == 0:
            cot_ring.wait(1)
            cot_ring.start(2)
        if g + 1 < groups:
            event(g + 1, n - 1)

        def between(i):
            if i == 1 and g + 1 < groups:
                fetch(g + 1)

        attend(g, between)
    for h in range(3, ring // 2 + 1):
        cot_ring.wait(h - 1)
        cot_ring.start(h)
    cot_ring.wait(ring // 2)
    stores = [
        pltpu.make_async_copy(ref, out, io.at[3 + i])
        for i, (ref, out) in enumerate(((q, q_out), (k, k_out), (v, v_out), (mixed, mixed_out), (stats, stats_out)))
    ]
    for copy in stores:
        copy.start()
    out_loads = [
        pltpu.make_async_copy(w_full.at[g, :, :, pl.ds(3 * bs, bs)], wv.at[g], load.at[g])
        for g in range(groups)
    ]
    for copy in out_loads:
        copy.start()
    for copy in out_loads:
        copy.wait()

    def out_share(offset):
        m = at.member(offset)
        r = aligned(m, local)
        for b in range(n):
            block = sum(
                dot_t(mixed[r, g * bs : (g + 1) * bs], wv[g, b].reshape(2 * bs, bs))
                for g in range(groups)
            )
            part[m, :, b * 2 * bs : (b + 1) * 2 * bs] = block.astype(BF16)

    moves = [(b, e) for e in range(1, n) for b in range(groups, len(batches))]

    def move():
        if moves:
            event(*moves.pop(0))

    out_share(ring // 2)
    for d in range(2):
        sums.start(0, d)
    for kk in range(1, ring // 2):
        for d in range(2):
            out_share((1 if d == 0 else -1) * (ring // 2 - kk))
        move()
        for d in range(2):
            sums.add(kk - 1, d)
            sums.start(kk, d)
    out_share(0)
    move()
    own_cot.wait()
    own_again = pltpu.make_async_copy(tokens, xrow, io.at[8])
    own_again.start()
    own_again.wait()
    for d in range(2):
        sums.add(ring // 2 - 1, d)

    @pl.loop(0, local // norm_tile)
    def _(i):
        r = aligned(i, norm_tile)
        value = xrow[r].astype(F32) + part[at.t, r].astype(F32)
        resid[r] = value
        scale = inverse_rms(value)

        def store(cols, value):
            xrow[r, cols] = value

        norm_into(lambda cols: resid[r, cols], scale, 1, store)

    x_ring.start(1)
    own_x = pltpu.make_async_copy(xrow, x_full.at[at.t], io.at[0])
    resid_store = pltpu.make_async_copy(resid, residual_out, io.at[8])
    own_x.start()
    resid_store.start()
    move()
    for h in range(2, ring // 2 + 1):
        move()
        x_ring.wait(h - 1)
        x_ring.start(h)
    if len(moves) > len(batches) - groups:
        move()
    x_ring.wait(ring // 2)
    while moves:
        move()
    for line in (cot_ring, x_ring):
        line.sent()
    sums.sent()
    for a in range(pre):
        if a < first:
            feed.finish(a)
        else:
            feed.sent(a, range(1, n - 1))
    for copy in (normed_store, own_x, resid_store, *stores):
        copy.wait()


def forward_part(n, ring, pre, tokens, cotangent, w_full, ff_full, cosine, sine, q_tile=256):
    groups, bs = w_full.shape[0], w_full.shape[-1]
    chunks = ff_full.shape[0]
    local, width = tokens.shape
    rows = local * ring
    cols = groups * bs
    any_ = pl.BlockSpec(memory_space=pl.ANY)
    vmem = pl.BlockSpec(memory_space=pltpu.VMEM)
    dma = pltpu.SemaphoreType.DMA
    shape = jax.ShapeDtypeStruct
    half = ring // 2
    return pl.pallas_call(
        functools.partial(forward_kernel, n, ring, pre, min(q_tile, rows)),
        out_shape=[
            shape(w_full.shape, BF16),
            shape(ff_full.shape, BF16),
            shape((ring, local, width), BF16),
            shape((rows, cols), BF16),
            shape((rows, cols), BF16),
            shape((rows, cols), BF16),
            shape((rows, cols), BF16),
            shape((rows, 128), F32),
            shape((local, width), F32),
            shape((ring, local, width), BF16),
            shape((ring, local, width), BF16),
        ],
        in_specs=[any_] * 4 + [vmem] * 2,
        out_specs=[any_] * 11,
        input_output_aliases={2: 0, 3: 1},
        scratch_shapes=[
            pltpu.VMEM((ring, local, width), BF16),
            pltpu.VMEM((max(4, groups), n, 2, bs, bs), BF16),
            pltpu.VMEM((2 * n, 16, bs), BF16),
            pltpu.VMEM((rows, cols), BF16),
            pltpu.VMEM((rows, cols), BF16),
            pltpu.VMEM((rows, cols), BF16),
            pltpu.VMEM((rows, cols), BF16),
            pltpu.VMEM((rows, 128), F32),
            pltpu.VMEM((min(q_tile, rows), bs), F32),
            pltpu.VMEM((ring, local, width), BF16),
            pltpu.VMEM((2, half, local, width), BF16),
            pltpu.VMEM((local, width), BF16),
            pltpu.VMEM((local, width), F32),
            dma((2, n - 1, groups)), dma((2, n - 1, groups)),
            dma((groups,)), dma((groups,)),
            dma((2, n - 1, chunks)), dma((2, n - 1, chunks)),
            dma((chunks,)), dma((chunks,)),
            dma((2, half)), dma((2, half)), dma((2, half)), dma((2, half)),
            dma((2, half)), dma((2, half)), dma((2, half)), dma((2, half)),
            dma((9,)), dma((5,)), dma((2 * n - 1,)), dma((2 * n - 1,)),
        ],
        compiler_params=pltpu.CompilerParams(
            collective_id=1, has_side_effects=True, vmem_limit_bytes=56 * 2**20),
    )(tokens, cotangent, w_full, ff_full, cosine, sine)


def layer_kernel(
    n, ring, pre, pace, plan, q_tile, tile,
    ff_in, x_hbm, dy_hbm, residual, cotangent, tokens, normed_in, q_in, k_in, v_in, mixed_in, stats_in,
    w_full, cosine_in, sine_in,
    ff_full, output, grad_tokens, gain_grads, ff_result, ff_summed, ff_landed,
    att_result, att_summed, att_landed, out_hbm,
    part, land, dres_full, core_in, stage, got, total, gparts, gland, gsecond, gone, gtwo,
    w_send, w_recv, w_sib_send, w_sib_recv,
    f_send, f_recv, f_load, f_out, a_send, a_recv, a_load, a_out,
    core_send, core_recv, acore_send, acore_recv, store_sem,
    s1_send, s1_recv, s2_send, s2_recv, s3_send, s3_recv, x_send, x_recv, free_sem,
    g_send, g_recv, h_send, h_recv, io, load,
):
    at = Place(n, ring)
    c = at.c
    groups, _, _, _, bs = w_full.shape
    chunks, _, _, unit, _ = ff_full.shape
    local, width = tokens.shape
    rows = local * ring
    heads = bs // HEAD_DIM
    half = ring // 2
    weights = LineGather(at, ff_full, w_send, w_recv, w_sib_send, w_sib_recv)
    feed = LineSum(at, chunks, ff_summed, ff_landed, ff_result,
                   stage.at[:, :, :, pl.ds(0, unit)], got.at[:, pl.ds(0, unit)],
                   total.at[pl.ds(0, unit)],
                   f_send, f_recv, f_load, f_out)
    att = LineSum(at, groups, att_summed, att_landed, att_result, stage, got, total,
                  a_send, a_recv, a_load, a_out)
    sums1 = RingSum(at, part, land, s1_send, s1_recv)
    sums2 = RingSum(at, part, land, s2_send, s2_recv)
    sums3 = RingSum(at, part, land, s3_send, s3_recv)
    dres_ring = RingGather(at, dres_full.at[at.t], dres_full, x_send, x_recv)
    lag = max(0, n - pre)
    num, den, begin = pace

    def fetch(src, dst, i):
        return pltpu.make_async_copy(src, dst, io.at[i])

    x_in = fetch(x_hbm, part, 0)
    dy_in = fetch(dy_hbm, dres_full, 1)
    x_in.start()
    dy_in.start()
    at.barrier(with_all=True)
    first = (pre + 1) // 2
    for a in range(first, pre):
        weights.give(a, n - 1)

    def ticks_before(j):
        return (j >= begin) * ((num * (j - begin)) // den)

    def feed_phase(oacc, dacc, wv, pg, hid, dgate, dup, out_stage):
        x, dy = part, dres_full

        def loads(j):
            return [
                pltpu.make_async_copy(
                    ff_full.at[j, :, :, pl.ds(i * bs, bs)], wv.at[j % 3, i], load.at[j % 3, i])
                for i in range(3)
            ]

        def core_copy(j):
            return pltpu.make_async_remote_copy(
                pg.at[1 - c], core_in.at[j % 2, :, pl.ds(0, unit)],
                core_send.at[j % 2], core_recv.at[j % 2],
                device_id={"dp": at.sib}, device_id_type=MESH)

        def store(j):
            return pltpu.make_async_copy(pg.at[c], ff_summed.at[j], store_sem)

        for copy in loads(0):
            copy.start()

        @pl.loop(0, rows // 64)
        def _(i):
            r = aligned(i, 64)
            oacc[r] = jnp.zeros((64, width), F32)
            dacc[r] = jnp.zeros((64, width), F32)

        x_in.wait()
        dy_in.wait()
        per = max(1, min(tile // local, ring))

        def columns(ref, cols):
            return ref[:, :, cols].reshape(rows, bs)

        def weight_grads(cc, now):
            @pl.loop(0, n)
            def _(k):
                cols = aligned(2 * k + cc, bs)
                xt = columns(x, cols)
                pg[cc, k, pl.ds(0, bs)] = t_dot(xt, dgate[:, now]).astype(BF16)
                pg[cc, k, pl.ds(bs, bs)] = t_dot(xt, dup[:, now]).astype(BF16)
                pg[cc, k, pl.ds(2 * bs, bs)] = t_dot(columns(dy, cols), hid[:, now]).astype(BF16)

        def compute(j):
            slot = j % 3
            now = aligned(j % 2, bs)
            for copy in loads(j):
                copy.wait()

            @pl.when((j + 1 >= first) & (j + 1 < pre))
            def _():
                weights.given(j + 1)
                weights.sent(j + 1, (n - 1,))

            @pl.when(j + 1 < pre)
            def _():
                for copy in loads(j + 1):
                    copy.start()

            @pl.loop(0, ring // per)
            def _(m):
                r = aligned(m, per * local)
                here = pl.ds(m * per, per)
                rows_x = x[here].reshape(per * local, width)
                gate = dot(rows_x, wv[slot, 0].reshape(width, bs))
                up = dot(rows_x, wv[slot, 1].reshape(width, bs))
                dh = dot(dy[here].reshape(per * local, width), wv[slot, 2].reshape(width, bs))
                s = jax.nn.sigmoid(gate)
                gs = gate * s
                hid[r, now] = (gs * up).astype(BF16)
                dup[r, now] = (dh * gs).astype(BF16)
                dgate[r, now] = (dh * up * (s + gs * (1 - s))).astype(BF16)

            weight_grads(1 - c, now)
            core_copy(j).start()

            @pl.when(j % 2 == 1)
            def _():
                one, two = (j + 2) % 3, slot

                @pl.loop(0, rows // tile)
                def _(m):
                    r = aligned(m, tile)
                    both = jnp.concatenate([dgate[r, :], dup[r, :]], axis=1)

                    @pl.loop(0, n)
                    def _(k):
                        def block(s, i):
                            return wv[s, i, k].reshape(2 * bs, bs)

                        cols = aligned(k, 2 * bs)
                        oacc[r, cols] += dot_t(
                            hid[r, :], jnp.concatenate([block(one, 2), block(two, 2)], axis=1))
                        dacc[r, cols] += dot_t(both, jnp.concatenate(
                            [block(one, 0), block(two, 0), block(one, 1), block(two, 1)], axis=1))

            weight_grads(c, now)
            core_copy(j).wait_recv()

            @pl.loop(0, n)
            def _(k):
                pg[c, k] = pg[c, k] + core_in[j % 2, k, pl.ds(0, unit)]

            store(j).start()
            core_copy(j).wait_send()

        def begin_step(i):
            return min(2 * i + 1, i + max(pre - n, 0))

        @pl.loop(0, lag + chunks)
        def _(step):
            j = step - lag
            for a in range(first, pre):
                @pl.when(j == a - 2)
                def _():
                    weights.event(a, n - 1)

            for i in range(chunks - pre):
                for e in range(n):
                    @pl.when(step == begin_step(i) + e)
                    def _():
                        weights.event(pre + i, e)

            @pl.when(j >= 1)
            def _():
                store(j - 1).wait()
                feed.event(j - 1, 0)

            for extra in range(2):
                tick = ticks_before(j) + extra
                for e in range(n - 1, 0, -1):
                    q = tick - (e - 1) + 2 * n
                    r = q // 2 - n

                    @pl.when((j >= 0) & (tick < ticks_before(j + 1)) & (q % 2 == 0)
                             & (r >= 0) & (r < chunks))
                    def _():
                        feed.event(r, e)

            @pl.when(j >= 0)
            def _():
                compute(j)

            for i in range(chunks - pre):
                @pl.when(step == begin_step(i) + n - 1)
                def _():
                    weights.finish(pre + i)

            @pl.when((j + 1 >= pre) & (j + 1 >= 1) & (j + 1 < chunks))
            def _():
                for copy in loads(j + 1):
                    copy.start()

        store(chunks - 1).wait()
        feed.event(chunks - 1, 0)

        @pl.loop(0, ring)
        def _(m):
            part[m] = dacc[aligned(m, local), :].astype(BF16)

        for d in range(2):
            sums1.start(0, d)

        piece = local // 2

        def put(m):
            return fetch(
                out_stage.at[m % 2], out_hbm.at[m // 2, pl.ds(m % 2 * piece, piece)], m % 2)

        for m in range(2 * ring):
            if m > 1:
                put(m - 2).wait()
            out_stage[m % 2] = oacc[m * piece : (m + 1) * piece, :].astype(BF16)
            put(m).start()
        for m in range(2 * ring - 2, 2 * ring):
            put(m).wait()

    pl.run_scoped(
        feed_phase,
        pltpu.VMEM((rows, width), F32),
        pltpu.VMEM((rows, width), F32),
        pltpu.VMEM((3, 3, n, 2, bs, bs), BF16),
        pltpu.VMEM((2, n, unit, bs), BF16),
        pltpu.VMEM((rows, 2 * bs), BF16),
        pltpu.VMEM((rows, 2 * bs), BF16),
        pltpu.VMEM((rows, 2 * bs), BF16),
        pltpu.VMEM((2, local // 2, width), BF16),
    )

    done = [0 if chunks < begin else (num * (chunks - begin)) // den]
    last = 2 * (chunks - 1) + n - 2

    planned = list(plan)
    moves = []

    def point():
        for _ in range(planned.pop(0) if planned else 1):
            if done[0] <= last:
                feed_tick()
                if done[0] > last:
                    feed.result(chunks - 1).wait()
            elif moves:
                att.event(*moves.pop(0))

    def feed_tick():
        tick = done[0]
        for e in range(n - 1, 0, -1):
            if (tick - e + 1) % 2 == 0 and 0 <= (tick - e + 1) // 2 < chunks:
                feed.event((tick - e + 1) // 2, e)
        done[0] += 1

    def attention_phase(
        normed, wv, gains, q, k, v, mixed, stats, dmix, dq, dk, dv, dproj, resid, dres, small, lined,
        gsum, pg, cosine, sine,
    ):
        resid_in = fetch(residual, resid, 0)
        cot_in = fetch(cotangent, lined, 1)
        gains_in = fetch(w_full.at[0, :, :, pl.ds(4 * bs, 16)], gains, 2)
        saved = [
            fetch(src, dst, 3 + i)
            for i, (src, dst) in enumerate(
                ((normed_in, normed), (q_in, q), (k_in, k), (v_in, v), (mixed_in, mixed)))
        ]
        weight_loads = [
            pltpu.make_async_copy(
                w_full.at[g, :, :, pl.ds(i * bs, bs)], wv.at[i, g], load.at[i, g])
            for g in range(groups) for i in range(4)
        ]
        saved += [fetch(cosine_in, cosine, 8), fetch(sine_in, sine, 9), fetch(stats_in, stats, 10)]
        for copy in (resid_in, cot_in, gains_in, *saved, *weight_loads):
            copy.start()

        def gain_of(row, i):
            return gains[i // 2, i % 2, row : row + 1, :].astype(F32)

        tile = min(64, local)

        def norm_back(value_of, grad_of, row, emit):
            gsum[row : row + 1, :] = jnp.zeros((1, width), F32)

            @pl.loop(0, local // tile)
            def _(i):
                r = aligned(i, tile)
                scale = inverse_rms(value_of(r, pl.ds(0, width)))
                inner = jnp.zeros((tile, 1), F32)
                for b in range(2 * n):
                    cols = pl.ds(b * bs, bs)
                    value = value_of(r, cols)
                    grad = grad_of(r, cols)
                    gsum[row : row + 1, cols] += jnp.sum(
                        grad * value * scale, axis=0, keepdims=True)
                    inner += jnp.sum(grad * gain_of(row, b) * value, axis=-1, keepdims=True)
                pull = scale * scale * scale * (inner / width)
                for b in range(2 * n):
                    cols = pl.ds(b * bs, bs)
                    emit(r, cols,
                         scale * grad_of(r, cols) * gain_of(row, b) - value_of(r, cols) * pull)

        for kk in range(half):
            point()
            for d in range(2):
                sums1.add(kk, d)
                if kk < half - 1:
                    sums1.start(kk + 1, d)
        for copy in (resid_in, cot_in, gains_in):
            copy.wait()

        def emit_residual(r, cols, value):
            total = lined[r, cols].astype(F32) + value
            dres[r, cols] = total
            dres_full[at.t, r, cols] = total.astype(BF16)

        norm_back(lambda r, cols: resid[r, cols],
                  lambda r, cols: part[at.t, r, cols].astype(F32), 1, emit_residual)
        dres_ring.start(1)
        sums1.sent()
        second_in = fetch(out_hbm, part, 0)
        second_in.start()
        for h in range(2, half + 1):
            point()
            dres_ring.wait(h - 1)
            dres_ring.start(h)
        point()
        second_in.wait()
        dres_ring.wait(half)
        for d in range(2):
            sums2.start(0, d)
        for copy in (*saved, *weight_loads):
            copy.wait()

        def core_copy(g):
            return pltpu.make_async_remote_copy(
                pg.at[1 - c], core_in.at[g], acore_send.at[g], acore_recv.at[g],
                device_id={"dp": at.sib}, device_id_type=MESH)

        def store(g):
            return pltpu.make_async_copy(pg.at[c], att_summed.at[g], store_sem)

        def attend_back(g, between):
            gcols = pl.ds(g * bs, bs)
            lanes = group_lanes(heads, bs)
            columns = lax.broadcasted_iota(jnp.int32, (1, 128), 1)
            scale = jnp.asarray(HEAD_DIM ** (-0.5), BF16)
            dk[...] = jnp.zeros_like(dk)
            dv[...] = jnp.zeros_like(dv)
            for i in range(rows // q_tile):
                r = pl.ds(i * q_tile, q_tile)
                dq[r] = jnp.zeros((q_tile, bs), F32)

                @pl.loop(0, heads)
                def _(h):
                    mask = lanes == h
                    scaled = only(mask, q[r, gcols]) * scale
                    dmh = only(mask, dmix[r])
                    log_total = jnp.sum(
                        jnp.where(columns == g * heads + h, stats[r], 0.0), axis=-1, keepdims=True)
                    inner = jnp.sum(
                        dmh.astype(F32) * mixed[r, gcols].astype(F32), axis=-1, keepdims=True)
                    d_query = 0.0
                    for keys, scores in score_parts(scaled, k, gcols, i, q_tile):
                        probs = jnp.exp(scores - log_total)
                        d_probs = dot_t(dmh, v[keys, gcols])
                        d_scores = (probs * (d_probs - inner)).astype(BF16)
                        d_query += dot(d_scores, only(mask, k[keys, gcols]))
                        dk[keys] += t_dot(d_scores, scaled)
                        dv[keys] += t_dot(probs.astype(BF16), dmh)
                    dq[r] += d_query

                between(i)

        def weight_grads(g, cc):
            gcols = pl.ds(g * bs, bs)

            @pl.loop(0, n)
            def _(b):
                cols = aligned(2 * b + cc, bs)
                x = normed[:, :, cols].reshape(rows, bs)
                for i in range(3):
                    pg[cc, b, pl.ds(i * bs, bs)] = t_dot(x, dproj[i, :, gcols]).astype(BF16)
                pg[cc, b, pl.ds(3 * bs, bs)] = t_dot(
                    dres_full[:, :, cols].reshape(rows, bs), mixed[:, gcols]).astype(BF16)

        second = [0]

        def second_sum():
            if second[0] < half:
                kk = second[0]
                for d in range(2):
                    sums2.add(kk, d)
                    if kk < half - 1:
                        sums2.start(kk + 1, d)
                second[0] += 1

        tiles = rows // q_tile

        def between(i):
            point()
            if i == tiles - 1:
                second_sum()

        for g in range(groups):
            gcols = pl.ds(g * bs, bs)

            @pl.loop(0, ring)
            def _(m):
                r = aligned(m, local)
                dmix[r] = dot(dres_full[m], wv[3, g].reshape(width, bs)).astype(BF16)

            attend_back(g, between)

            @pl.loop(0, ring)
            def _(m):
                r = aligned(m, local)
                for i, value in enumerate((dq[r] * HEAD_DIM ** (-0.5), dk[r])):
                    dproj[i, r, gcols] = rope(
                        value, cosine[r, :], sine[r, :], back=True).astype(BF16)
                dproj[2, r, gcols] = dv[r].astype(BF16)

            weight_grads(g, 1 - c)
            core_copy(g).start()
            weight_grads(g, c)
            core_copy(g).wait_recv()

            @pl.loop(0, n)
            def _(b):
                pg[c, b] = pg[c, b] + core_in[g, b]

            store(g).start()
            core_copy(g).wait_send()
            store(g).wait()
            att.event(g, 0)
            moves.extend((g, e) for e in range(1, n))

        while second[0] < half:
            second_sum()
        sums2.sent()

        @pl.loop(0, local // tile)
        def _(i):
            r = aligned(i, tile)
            lined[r] = (resid[r] + part[at.t, r].astype(F32)).astype(BF16)

        out_store = fetch(lined, output, 0)
        out_store.start()
        for way in (1, -1):
            pl.semaphore_signal(
                free_sem, inc=1, device_id={"tensor": at.member(way)}, device_id_type=MESH)

        def share(offset):
            m = at.member(offset)
            r = aligned(m, local)
            for b in range(n):
                block = sum(
                    dot_t(dproj[i, r, g * bs : (g + 1) * bs], wv[i, g, b].reshape(2 * bs, bs))
                    for i in range(3) for g in range(groups)
                )
                part[m, :, b * 2 * bs : (b + 1) * 2 * bs] = block.astype(BF16)

        share(half)
        pl.semaphore_wait(free_sem, 2)
        for d in range(2):
            sums3.start(0, d)

        tok_in = fetch(tokens, small, 1)
        dres_ring.sent()
        tok_in.start()
        point()
        for kk in range(1, half):
            for d in range(2):
                share((1 if d == 0 else -1) * (half - kk))
            for d in range(2):
                sums3.add(kk - 1, d)
                sums3.start(kk, d)
            point()
        share(0)
        point()
        for d in range(2):
            sums3.add(half - 1, d)
        tok_in.wait()
        out_store.wait()

        def emit_tokens(r, cols, value):
            lined[r, cols] = (dres[r, cols] + value).astype(BF16)

        norm_back(lambda r, cols: small[r, cols].astype(F32),
                  lambda r, cols: part[at.t, r, cols].astype(F32), 0, emit_tokens)
        token_store = fetch(lined, grad_tokens, 0)
        token_store.start()
        for b in range(2 * n):
            gparts[b, 0:2] = gsum[0:2, b * bs : (b + 1) * bs]
            gparts[b, 2:8] = jnp.zeros((6, bs), F32)
        over_dp = SmallSum("dp", 2 * at.z + c, 2 * n, lambda i: gparts.at[i], gland, g_send, g_recv)
        gone[...] = over_dp.total()
        over_ring = SmallSum("tensor", at.t, ring, lambda i: gone, gsecond, h_send, h_recv)
        gtwo[...] = over_ring.total()
        gain_store = fetch(gtwo, gain_grads, 1)
        gain_store.start()
        while done[0] <= last or moves:
            point()
        att.result(groups - 1).wait()
        token_store.wait()
        gain_store.wait()
        sums3.sent()

    cols = groups * bs
    pl.run_scoped(
        attention_phase,
        pltpu.VMEM((ring, local, width), BF16),
        pltpu.VMEM((4, groups, n, 2, bs, bs), BF16),
        pltpu.VMEM((n, 2, 16, bs), BF16),
        pltpu.VMEM((rows, cols), BF16),
        pltpu.VMEM((rows, cols), BF16),
        pltpu.VMEM((rows, cols), BF16),
        pltpu.VMEM((rows, cols), BF16),
        pltpu.VMEM((rows, 128), F32),
        pltpu.VMEM((rows, bs), BF16),
        pltpu.VMEM((rows, bs), F32),
        pltpu.VMEM((rows, bs), F32),
        pltpu.VMEM((rows, bs), F32),
        pltpu.VMEM((3, rows, cols), BF16),
        pltpu.VMEM((local, width), F32),
        pltpu.VMEM((local, width), F32),
        pltpu.VMEM((local, width), BF16),
        pltpu.VMEM((local, width), BF16),
        pltpu.VMEM((8, width), F32),
        pltpu.VMEM((2, n, 4 * bs, bs), BF16),
        pltpu.VMEM((rows, bs), F32),
        pltpu.VMEM((rows, bs), F32),
    )


def layer_part(
    n, ring, pre, pace, plan, ff_full, x, dy, residual, cotangent, tokens, normed, q, k, v, mixed, stats,
    w_full, cosine, sine, q_tile=256, tile=512,
):
    groups, _, _, _, bs = w_full.shape
    chunks, _, _, unit, _ = ff_full.shape
    local, width = tokens.shape
    rows = local * ring
    half = ring // 2
    any_ = pl.BlockSpec(memory_space=pl.ANY)
    dma = pltpu.SemaphoreType.DMA
    shape = jax.ShapeDtypeStruct
    big = (ring, local, width)
    wide = 4 * bs
    return pl.pallas_call(
        functools.partial(
            layer_kernel, n, ring, pre, pace, plan, min(q_tile, rows), min(tile, rows)),
        out_shape=[
            shape(ff_full.shape, BF16),
            shape((local, width), BF16),
            shape((local, width), BF16),
            shape((8, bs), F32),
            shape((chunks, unit, bs), BF16),
            shape((chunks, n, unit, bs), BF16),
            shape((2, chunks, n - 1, unit, bs), BF16),
            shape((groups, wide, bs), BF16),
            shape((groups, n, wide, bs), BF16),
            shape((2, groups, n - 1, wide, bs), BF16),
            shape(big, BF16),
        ],
        in_specs=[any_] * 15,
        out_specs=[any_] * 11,
        input_output_aliases={0: 0},
        scratch_shapes=[
            pltpu.VMEM(big, BF16),
            pltpu.VMEM((2, half, local, width), BF16),
            pltpu.VMEM(big, BF16),
            pltpu.VMEM((max(2, groups), n, wide, bs), BF16),
            pltpu.VMEM((2, n - 2, n // 2, wide, bs), BF16),
            pltpu.VMEM((4, wide, bs), BF16),
            pltpu.VMEM((wide, bs), BF16),
            pltpu.VMEM((2 * n, 8, bs), F32),
            pltpu.VMEM((2 * n - 1, 8, bs), F32),
            pltpu.VMEM((ring - 1, 8, bs), F32),
            pltpu.VMEM((8, bs), F32),
            pltpu.VMEM((8, bs), F32),
            dma((2, n - 1, chunks)), dma((2, n - 1, chunks)), dma((chunks,)), dma((chunks,)),
            dma((2, n - 1, chunks)), dma((2, n - 1, chunks)), dma((4,)), dma,
            dma((2, n - 1, groups)), dma((2, n - 1, groups)), dma((4,)), dma,
            dma((2,)), dma((2,)), dma((groups,)), dma((groups,)), dma,
            dma((2, half)), dma((2, half)), dma((2, half)), dma((2, half)),
            dma((2, half)), dma((2, half)), dma((2, half)), dma((2, half)),
            pltpu.SemaphoreType.REGULAR,
            dma((2 * n - 1,)), dma((2 * n - 1,)), dma((ring - 1,)), dma((ring - 1,)),
            dma((11,)), dma((4, max(4, groups))),
        ],
        compiler_params=pltpu.CompilerParams(
            collective_id=2, has_side_effects=True, vmem_limit_bytes=63 * 2**20),
    )(ff_full, x, dy, residual, cotangent, tokens, normed, q, k, v, mixed, stats,
      w_full, cosine, sine)


PREFETCH = 6
PACE = (5, 4, 2)
PLAN = (1, 2, 2, 2) + (1, 0, 1, 0) + (1, 0, 0, 1) + (1, 2, 1)


def pack_kernel(place, q, k, v, o, gain_attn, gain_mlp, gate, up, down, att, ff):
    bs = q.shape[0]

    @pl.when(pl.program_id(0) == 0)
    def _():
        row = lax.broadcasted_iota(jnp.int32, (16, bs), 0)
        first, second = (g[...].astype(F32) for g in (gain_attn, gain_mlp))
        gains = jnp.where(row == 0, first, jnp.where(row == 1, second, 0.0)).astype(BF16)
        for g in range(att.shape[0]):
            here = slice(g * bs, (g + 1) * bs)
            for i, ref in enumerate((q, k, v)):
                att[g, i * bs : (i + 1) * bs] = ref[:, here]
            att[g, 3 * bs : 4 * bs] = o[here].T
            att[g, 4 * bs : 4 * bs + 16] = gains

    for j in range(ff.shape[0]):
        here = slice(j * bs, (j + 1) * bs)
        ff[j, 0:bs] = gate[:, here]
        ff[j, bs : 2 * bs] = up[:, here]
        ff[j, 2 * bs : 3 * bs] = down[here].T


def chunks_at_once(chunks):
    return 4 if chunks % 4 == 0 else 1


def pack(w_query, w_key, w_value, w_out, gain_attn, gain_mlp, w_gate, w_up, w_down):
    bs = w_query.shape[0]
    n = lax.axis_size("dp") // 2
    groups, chunks = w_query.shape[1] // bs, w_gate.shape[1] // bs
    some = chunks_at_once(chunks)
    col = pl.BlockSpec((bs, groups * bs), lambda j, p: (0, 0))
    row = pl.BlockSpec((groups * bs, bs), lambda j, p: (0, 0))
    gain = pl.BlockSpec((1, bs), lambda j, p: (0, 0))
    wide = pl.BlockSpec((bs, some * bs), lambda j, p: (0, j))
    tall = pl.BlockSpec((some * bs, bs), lambda j, p: (j, 0))
    return pl.pallas_call(
        pack_kernel,
        out_shape=[
            jax.ShapeDtypeStruct((groups, n, 2, 4 * bs + 16, bs), BF16),
            jax.ShapeDtypeStruct((chunks, n, 2, 3 * bs, bs), BF16),
        ],
        grid_spec=pltpu.PrefetchScalarGridSpec(
            num_scalar_prefetch=1,
            grid=(chunks // some,),
            in_specs=[col, col, col, row, gain, gain, wide, wide, tall],
            out_specs=[
                pl.BlockSpec((groups, None, None, 4 * bs + 16, bs),
                             lambda j, p: (0, p[0], p[1], 0, 0)),
                pl.BlockSpec((some, None, None, 3 * bs, bs),
                             lambda j, p: (j, p[0], p[1], 0, 0)),
            ],
        ),
        compiler_params=pltpu.CompilerParams(vmem_limit_bytes=63 * 2**20),
    )(jnp.stack([lax.axis_index("dp") // 2, lax.axis_index("dp") % 2]),
      w_query, w_key, w_value, w_out, gain_attn.reshape(1, bs), gain_mlp.reshape(1, bs),
      w_gate, w_up, w_down)


def unpack_kernel(att, ff, q, k, v, o, gate, up, down):
    bs = q.shape[0]

    @pl.when(pl.program_id(0) == 0)
    def _():
        for g in range(att.shape[0]):
            here = slice(g * bs, (g + 1) * bs)
            for i, ref in enumerate((q, k, v)):
                ref[:, here] = att[g, i * bs : (i + 1) * bs].astype(F32)
            o[here] = att[g, 3 * bs : 4 * bs].astype(F32).T

    for j in range(ff.shape[0]):
        here = slice(j * bs, (j + 1) * bs)
        gate[:, here] = ff[j, 0:bs].astype(F32)
        up[:, here] = ff[j, bs : 2 * bs].astype(F32)
        down[here] = ff[j, 2 * bs : 3 * bs].astype(F32).T


def unpack(att, ff):
    groups, chunks, bs = att.shape[0], ff.shape[0], ff.shape[2]
    some = chunks_at_once(chunks)
    shape = jax.ShapeDtypeStruct
    col = pl.BlockSpec((bs, groups * bs), lambda j: (0, 0))
    row = pl.BlockSpec((groups * bs, bs), lambda j: (0, 0))
    wide = pl.BlockSpec((bs, some * bs), lambda j: (0, j))
    tall = pl.BlockSpec((some * bs, bs), lambda j: (j, 0))
    return pl.pallas_call(
        unpack_kernel,
        grid=(chunks // some,),
        out_shape=[shape((bs, groups * bs), F32)] * 3 + [shape((groups * bs, bs), F32)]
        + [shape((bs, chunks * bs), F32)] * 2 + [shape((chunks * bs, bs), F32)],
        in_specs=[
            pl.BlockSpec((groups, 4 * bs, bs), lambda j: (0, 0, 0)),
            pl.BlockSpec((some, 3 * bs, bs), lambda j: (j, 0, 0)),
        ],
        out_specs=[col] * 3 + [row] + [wide] * 2 + [tall],
        compiler_params=pltpu.CompilerParams(vmem_limit_bytes=63 * 2**20),
    )(att, ff)


def rotary_tables(row_count, width):
    frequency = rope_base ** (-np.arange(HEAD_DIM // 2) * 2.0 / HEAD_DIM)
    angles = (np.arange(row_count) % LEN)[:, None] * frequency[None, :]
    angles = np.tile(angles, (1, width // (HEAD_DIM // 2)))
    return np.cos(angles).astype(np.float32), np.sin(angles).astype(np.float32)


def shards(
    tokens, gain_attn, w_query, w_key, w_value, w_out, gain_mlp, w_gate, w_up, w_down, cotangent
):
    dp, ring = lax.axis_size("dp"), lax.axis_size("tensor")
    n = dp // 2
    local, width = tokens.shape
    rows = local * ring
    assert rows == LEN
    bs = w_query.shape[0]
    cosine, sine = rotary_tables(rows, bs)
    w_start, ff_start = pack(
        w_query, w_key, w_value, w_out, gain_attn, gain_mlp, w_gate, w_up, w_down
    )
    w_full, ff_full, normed, q, k, v, mixed, stats, residual, x, dy = forward_part(
        n, ring, PREFETCH, tokens, cotangent, w_start, ff_start, cosine, sine
    )
    _, output, grad_tokens, gain_grads, ff_grads, _, _, att_grads, _, _, _ = layer_part(
        n, ring, PREFETCH, PACE, PLAN, ff_full, x, dy, residual, cotangent, tokens,
        normed, q, k, v, mixed, stats, w_full, cosine, sine,
    )
    g_query, g_key, g_value, g_out, g_gate, g_up, g_down = unpack(att_grads, ff_grads)
    return (
        output,
        grad_tokens,
        gain_grads[0],
        g_query,
        g_key,
        g_value,
        g_out,
        gain_grads[1],
        g_gate,
        g_up,
        g_down,
    )


def solution(mesh):
    placed = (
        P(("dp", "tensor"), None),
        P("dp"),
        P("dp", "tensor"),
        P("dp", "tensor"),
        P("dp", "tensor"),
        P("tensor", "dp"),
        P("dp"),
        P("dp", "tensor"),
        P("dp", "tensor"),
        P("tensor", "dp"),
        P(("dp", "tensor"), None),
    )
    return jax.shard_map(
        shards,
        mesh=mesh,
        in_specs=placed,
        out_specs=(
            P(("dp", "tensor"), None),
            P(("dp", "tensor"), None),
            P("dp"),
            P("dp", "tensor"),
            P("dp", "tensor"),
            P("dp", "tensor"),
            P("tensor", "dp"),
            P("dp"),
            P("dp", "tensor"),
            P("dp", "tensor"),
            P("tensor", "dp"),
        ),
        check_vma=False,
    )
```

```python
import functools

import jax
import jax.numpy as jnp
import numpy as np
from jax import lax
from jax.experimental import pallas as pl
from jax.experimental.pallas import tpu as pltpu
from jax.sharding import PartitionSpec as P

HEAD_DIM = 64
LEN = 1024
MESH = pl.DeviceIdType.MESH
BF16 = jnp.bfloat16
F32 = jnp.float32

norm_eps = 1e-05
rope_base = 130000.0
masked_score = -1e30


def dot(a, b):
    return jnp.dot(a, b, preferred_element_type=F32)


def dot_t(a, b):
    return lax.dot_general(a, b, (((1,), (1,)), ((), ())), preferred_element_type=F32)


def t_dot(a, b):
    return lax.dot_general(a, b, (((0,), (0,)), ((), ())), preferred_element_type=F32)


def aligned(index, size):
    return pl.ds(pl.multiple_of(index * size, size), size)


class Place:
    def __init__(self, n, ring):
        me = lax.axis_index("dp")
        self.n, self.ring = n, ring
        self.z, self.c = me // 2, me % 2
        self.right, self.left = me + 2, me - 2
        self.sib = me + 1 - 2 * self.c
        self.has_r, self.has_l = self.z < n - 1, self.z > 0
        t = lax.axis_index("tensor")
        odd = t % 2
        self.t = t
        self.p = (1 - odd) * (t // 2) + odd * (ring - 1 - t // 2)

    def member(self, offset):
        p = (self.p + offset + self.ring) % self.ring
        back = (p >= self.ring // 2).astype(jnp.int32)
        return (1 - back) * (2 * p) + back * (2 * (self.ring - 1 - p) + 1)

    def barrier(self, with_ring=True, with_all=False):
        sem = pltpu.get_barrier_semaphore()

        def greet(peer):
            pl.semaphore_signal(sem, inc=1, device_id=peer, device_id_type=MESH)

        if with_all:
            for k in range(1, 2 * self.n):
                greet({"dp": (2 * self.z + self.c + k) % (2 * self.n)})
            for k in range(1, self.ring):
                greet({"tensor": (self.t + k) % self.ring})
            pl.semaphore_wait(sem, 2 * self.n - 1 + self.ring - 1)
            return

        greet({"dp": self.sib})
        if with_ring:
            greet({"tensor": self.member(1)})
            greet({"tensor": self.member(-1)})

        @pl.when(self.has_r)
        def _():
            greet({"dp": self.right})

        @pl.when(self.has_l)
        def _():
            greet({"dp": self.left})

        peers = self.has_r.astype(jnp.int32) + self.has_l.astype(jnp.int32)
        pl.semaphore_wait(sem, peers + (3 if with_ring else 1))

    def neighbour(self, d):
        return self.right if d == 0 else self.left

    def sends_to(self, d):
        return self.has_r if d == 0 else self.has_l

    def along(self, d, k):
        return self.z + k if d == 0 else self.z - k

    def depth(self, d):
        return self.z if d == 0 else self.n - 1 - self.z


class LineGather:
    def __init__(self, at, full, send, recv, sib_send, sib_recv):
        self.at, self.full = at, full
        self.send, self.recv = send, recv
        self.sib_send, self.sib_recv = sib_send, sib_recv

    def hop(self, a, h, d):
        at = self.at
        block = self.full.at[a, at.along(d, 1 - h), at.c]
        return pltpu.make_async_remote_copy(
            block, block, self.send.at[d, h - 1, a], self.recv.at[d, h - 1, a],
            device_id={"dp": at.neighbour(d)}, device_id_type=MESH)

    def sends(self, h, d):
        return self.at.sends_to(d) & (self.at.depth(d) >= h - 1)

    def arrives(self, h, d):
        return self.at.depth(d) >= h

    def to_sib(self, a):
        part = self.full.at[a, :, self.at.c]
        return pltpu.make_async_remote_copy(
            part, part, self.sib_send.at[a], self.sib_recv.at[a],
            device_id={"dp": self.at.sib}, device_id_type=MESH)

    def take(self, a, h):
        for d in range(2):
            @pl.when(self.arrives(h, d))
            def _():
                self.hop(a, h, d).wait_recv()

    def give(self, a, h):
        for d in range(2):
            @pl.when(self.sends(h, d))
            def _():
                self.hop(a, h, d).start()

    def event(self, a, e):
        n = self.at.n
        if e > 0:
            self.take(a, e)
        if e < n - 1:
            self.give(a, e + 1)
        else:
            self.to_sib(a).start()

    def given(self, a):
        self.to_sib(a).wait_recv()
        self.to_sib(a).wait_send()

    def finish(self, a):
        self.given(a)
        self.sent(a)

    def sent(self, a, hops=None):
        for h in hops or range(1, self.at.n):
            for d in range(2):
                @pl.when(self.sends(h, d))
                def _():
                    self.hop(a, h, d).wait_send()


def blocks_at_once(n):
    return 4 * ((n - 1) // 2) + 3


class LineSum:
    def __init__(self, at, chunks, sums, land, out, stage, got, total, send, recv, load, out_sem):
        self.at, self.chunks = at, chunks
        self.sums, self.land, self.out = sums, land, out
        self.stage, self.got, self.total = stage, got, total
        self.send, self.recv, self.load, self.out_sem = send, recv, load, out_sem
        self.slots = blocks_at_once(at.n)

    def valid(self, j):
        return (j >= 0) & (j < self.chunks)

    def copy(self, j, s, d, staged):
        at = self.at
        src = self.stage.at[d, s - 2, j % (at.n // 2)] if staged else self.sums.at[j, at.along(d, at.n - s)]
        return pltpu.make_async_remote_copy(
            src, self.land.at[d, j, s - 1], self.send.at[d, s - 1, j], self.recv.at[d, s - 1, j],
            device_id={"dp": at.neighbour(d)}, device_id_type=MESH)

    def arrival(self, j, s, d):
        return pltpu.make_async_remote_copy(
            self.land.at[d, j, s - 1], self.land.at[d, j, s - 1],
            self.send.at[d, s - 1, j], self.recv.at[d, s - 1, j],
            device_id={"dp": self.at.sib}, device_id_type=MESH)

    def arrives(self, s, d):
        depth = self.at.depth(d)
        return (depth > 0) & (depth <= s)

    def get(self, src, k):
        return pltpu.make_async_copy(src, self.got.at[k], self.load.at[k])

    def event(self, j, e):
        self.open(j, e)
        self.close(j, e)

    def slot(self, s):
        return 4 * ((s - 2) // 2)

    def passes(self, s, d):
        at = self.at
        return at.sends_to(d) & (at.depth(d) > 0) & (at.depth(d) < s)

    def own(self, j, s, d):
        return self.get(self.sums.at[j, self.at.along(d, self.at.n - s)], self.slot(s) + d)

    def came(self, j, s, d):
        return self.get(self.land.at[d, j, s - 2], self.slot(s) + 2 + d)

    def own_last(self, j):
        return self.get(self.sums.at[j, self.at.z], self.slots - 3)

    def came_last(self, j, d):
        return self.get(self.land.at[d, j, self.at.n - 2], self.slots - 2 + d)

    def open(self, j, e):
        at, n = self.at, self.at.n
        if e == 0:
            for s in range(1, n):
                for d in range(2):
                    @pl.when(at.sends_to(d) & (at.depth(d) == 0))
                    def _():
                        self.copy(j, s, d, False).start()

        elif e < n - 1:
            for d in range(2):
                @pl.when(self.passes(e + 1, d))
                def _():
                    self.own(j, e + 1, d).start()

            for d in range(2):
                @pl.when(self.passes(e + 1, d))
                def _():
                    self.arrival(j, e, d).wait_recv()
                    self.came(j, e + 1, d).start()
        else:
            self.own_last(j).start()
            for d in range(2):
                @pl.when(at.depth(d) > 0)
                def _():
                    self.arrival(j, n - 1, d).wait_recv()
                    self.came_last(j, d).start()

    def close(self, j, e):
        at, n = self.at, self.at.n
        if e == 0:
            return
        if e < n - 1:
            s = e + 1
            for d in range(2):
                @pl.when(self.passes(s, d))
                def _():
                    self.own(j, s, d).wait()
                    self.came(j, s, d).wait()
                    self.stage[d, s - 2, j % (n // 2)] = (
                        self.got[self.slot(s) + d] + self.got[self.slot(s) + 2 + d])
                    self.copy(j, s, d, True).start()

            return

        @pl.when(j > 0)
        def _():
            self.result(j - 1).wait()

        self.own_last(j).wait()
        for d in range(2):
            @pl.when(at.depth(d) > 0)
            def _():
                self.came_last(j, d).wait()

        @pl.when(at.depth(0) == 0)
        def _():
            self.total[...] = self.got[self.slots - 3] + self.got[self.slots - 1]

        @pl.when(at.depth(1) == 0)
        def _():
            self.total[...] = self.got[self.slots - 3] + self.got[self.slots - 2]

        @pl.when((at.depth(0) > 0) & (at.depth(1) > 0))
        def _():
            self.total[...] = (
                self.got[self.slots - 3] + self.got[self.slots - 2] + self.got[self.slots - 1])

        self.result(j).start()
        self.sent(j)

    def result(self, j):
        return pltpu.make_async_copy(self.total, self.out.at[j], self.out_sem)

    def sent(self, j):
        at, n = self.at, self.at.n
        for s in range(1, n):
            for d in range(2):
                @pl.when(at.sends_to(d) & (at.depth(d) == 0))
                def _():
                    self.copy(j, s, d, False).wait_send()

                if s >= 2:
                    @pl.when(at.sends_to(d) & (at.depth(d) > 0) & (at.depth(d) < s))
                    def _():
                        self.copy(j, s, d, True).wait_send()


class RingGather:
    def __init__(self, at, own, full, send, recv):
        self.at, self.own, self.full, self.send, self.recv = at, own, full, send, recv

    def copy(self, h, d):
        at = self.at
        way = 1 if d == 0 else -1
        owner = at.member(-way * (h - 1))
        rows = self.full.shape[1]
        part = pl.ds(0, rows)
        if h == at.ring // 2:
            part = pl.ds(d * (rows // 2), rows // 2)
        dst = self.full.at[owner, part]
        src = self.own.at[part] if h == 1 else dst
        return pltpu.make_async_remote_copy(
            src, dst, self.send.at[d, h - 1], self.recv.at[d, h - 1],
            device_id={"tensor": at.member(way)}, device_id_type=MESH)

    def start(self, h):
        for d in range(2):
            self.copy(h, d).start()

    def wait(self, h):
        for d in range(2):
            self.copy(h, d).wait_recv()

    def sent(self):
        for h in range(1, self.at.ring // 2 + 1):
            for d in range(2):
                self.copy(h, d).wait_send()


class SmallSum:
    def __init__(self, axis, me, size, part_of, land, send, recv):
        self.axis, self.me, self.size, self.part_of = axis, me, size, part_of
        self.land, self.send, self.recv = land, send, recv

    def copy(self, k):
        peer = (self.me + k) % self.size
        return pltpu.make_async_remote_copy(
            self.part_of(peer), self.land.at[k - 1], self.send.at[k - 1], self.recv.at[k - 1],
            device_id={self.axis: peer}, device_id_type=MESH)

    def total(self):
        for k in range(1, self.size):
            self.copy(k).start()
        result = self.part_of(self.me)[...]
        for k in range(1, self.size):
            self.copy(k).wait_recv()
            result = result + self.land[k - 1]
        for k in range(1, self.size):
            self.copy(k).wait_send()
        return result


class SmallGather:
    def __init__(self, axis, me, size, own, full, send, recv):
        self.axis, self.me, self.size, self.own, self.full = axis, me, size, own, full
        self.send, self.recv = send, recv

    def copy(self, k, slot):
        return pltpu.make_async_remote_copy(
            self.own, self.full.at[slot], self.send.at[k - 1], self.recv.at[k - 1],
            device_id={self.axis: (self.me + k) % self.size}, device_id_type=MESH)

    def start(self):
        for k in range(1, self.size):
            self.copy(k, self.me).start()

    def wait(self):
        for k in range(1, self.size):
            self.copy(k, (self.me + self.size - k) % self.size).wait_recv()
        for k in range(1, self.size):
            self.copy(k, self.me).wait_send()


class RingSum:
    def __init__(self, at, part, land, send, recv):
        self.at, self.part, self.land, self.send, self.recv = at, part, land, send, recv
        self.stages = at.ring // 2

    def rows_of(self, k, d):
        rows = self.part.shape[1]
        return pl.ds(d * (rows // 2), rows // 2) if k == 0 else pl.ds(0, rows)

    def target(self, k, d):
        return self.at.member((1 if d == 0 else -1) * (self.stages - k))

    def copy(self, k, d):
        r = self.rows_of(k, d)
        return pltpu.make_async_remote_copy(
            self.part.at[self.target(k, d), r], self.land.at[d, k, r],
            self.send.at[d, k], self.recv.at[d, k],
            device_id={"tensor": self.at.member(1 if d == 0 else -1)}, device_id_type=MESH)

    def start(self, k, d):
        self.copy(k, d).start()

    def add(self, k, d):
        self.copy(k, d).wait_recv()
        block = self.target(k + 1, d)
        rows = self.part.shape[1]
        half = rows // 2
        quarter = max(half // 4, 16)
        first = d * half if k == 0 else 0
        count = (half if k == 0 else rows) // quarter

        @pl.loop(0, count)
        def _(i):
            r = pl.ds(pl.multiple_of(first + i * quarter, quarter), quarter)
            self.part[block, r] = self.part[block, r] + self.land[d, k, r]

    def sent(self):
        for k in range(self.stages):
            for d in range(2):
                self.copy(k, d).wait_send()


def group_lanes(heads, width):
    return lax.broadcasted_iota(jnp.int32, (1, width), 1) // HEAD_DIM


def rope(values, cosine, sine, back=False):
    width = values.shape[-1]
    half = HEAD_DIM // 2
    first = lax.broadcasted_iota(jnp.int32, (1, width), 1) % HEAD_DIM < half
    ahead = pltpu.roll(values, width - half, 1)
    behind = pltpu.roll(values, half, 1)
    turned = jnp.where(first, -ahead, behind)
    return values * cosine - turned * sine if back else values * cosine + turned * sine


def inverse_rms(values):
    return lax.rsqrt(jnp.mean(values * values, axis=-1, keepdims=True) + norm_eps)


def score_parts(q_rows, k, cols, i, tile):
    diag = pl.ds(i * tile, tile)
    own = dot_t(q_rows, k[diag, cols])
    row = lax.broadcasted_iota(jnp.int32, own.shape, 0)
    column = lax.broadcasted_iota(jnp.int32, own.shape, 1)
    parts = [(diag, jnp.where(row >= column, own, masked_score))]
    if i > 0:
        past = pl.ds(0, i * tile)
        parts.append((past, dot_t(q_rows, k[past, cols])))
    return parts


def only(mask, values):
    return jnp.where(mask, values, jnp.zeros_like(values))


def forward_kernel(
    n, ring, pre, q_tile,
    tokens, cotangent, w_in, ff_in, cosine, sine,
    w_full, ff_full, normed_out, q_out, k_out, v_out, mixed_out, stats_out, residual_out, x_full, dy_full,
    tok, wv, gains, q, k, v, mixed, stats, acc, part, land, xrow, resid,
    a_send, a_recv, a_sib_send, a_sib_recv,
    f_send, f_recv, f_sib_send, f_sib_recv,
    t_send, t_recv, c_send, c_recv, x_send, x_recv, s_send, s_recv, io, load, gain_send, gain_recv,
):
    at = Place(n, ring)
    groups, _, _, _, bs = w_full.shape
    local, width = tokens.shape
    rows = local * ring
    heads = bs // HEAD_DIM
    att = LineGather(at, w_full, a_send, a_recv, a_sib_send, a_sib_recv)
    feed = LineGather(at, ff_full, f_send, f_recv, f_sib_send, f_sib_recv)
    tok_ring = RingGather(at, tokens, tok, t_send, t_recv)
    cot_ring = RingGather(at, cotangent, dy_full, c_send, c_recv)
    x_ring = RingGather(at, xrow, x_full, x_send, x_recv)
    sums = RingSum(at, part, land, s_send, s_recv)

    own_tok = pltpu.make_async_copy(tokens, tok.at[at.t], io.at[0])
    cot_in = pltpu.make_async_copy(cotangent, xrow, io.at[1])
    own_cot = pltpu.make_async_copy(xrow, dy_full.at[at.t], io.at[1])
    gain_in = pltpu.make_async_copy(
        w_full.at[0, at.z, at.c, pl.ds(4 * bs, 16)], gains.at[2 * at.z + at.c], io.at[2])
    own_tok.start()
    cot_in.start()
    gain_in.start()
    at.barrier(with_all=True)
    gain_all = SmallGather(
        "dp", 2 * at.z + at.c, 2 * n, gains.at[2 * at.z + at.c], gains, gain_send, gain_recv)

    first = (pre + 1) // 2
    batches = [[(att, g)] for g in range(groups)]
    for lot in (range(first), range(first, pre)):
        if len(lot):
            batches.append([(feed, a) for a in lot])

    def event(b, e):
        if b < len(batches):
            for line, a in batches[b]:
                if line is att or a < first or e < n - 2:
                    line.event(a, e)
                elif e == n - 2:
                    line.take(a, e)

    def loads(g):
        return [
            pltpu.make_async_copy(w_full.at[g, :, :, pl.ds(i * bs, bs)], wv.at[i], load.at[i])
            for i in range(3)
        ]

    for g in range(groups):
        event(g, 0)
    tok_ring.start(1)
    stats[...] = jnp.zeros_like(stats)
    gain_in.wait()
    gain_all.start()
    for g in range(groups):
        event(g, 1)
    cot_in.wait()
    own_cot.start()
    tok_ring.wait(1)
    tok_ring.start(2)
    event(0, 2)
    for h in range(3, ring // 2 + 1):
        tok_ring.wait(h - 1)
        tok_ring.start(h)
    tok_ring.wait(ring // 2)
    cot_ring.start(1)
    gain_all.wait()
    own_tok.wait()
    tok_ring.sent()

    def norm_into(values, scale, row, store):
        for i in range(2 * n):
            gain = gains[i, row : row + 1, :].astype(F32)
            cols = pl.ds(i * bs, bs)
            store(cols, (values(cols) * scale * gain).astype(BF16))

    norm_tile = min(64, local)

    @pl.loop(0, ring)
    def _(m):
        @pl.loop(0, local // norm_tile)
        def _(i):
            r = aligned(i, norm_tile)
            scale = inverse_rms(tok[m, r].astype(F32))

            def store(cols, value):
                tok[m, r, cols] = value

            norm_into(lambda cols: tok[m, r, cols].astype(F32), scale, 0, store)

    normed_store = pltpu.make_async_copy(tok, normed_out, io.at[2])
    normed_store.start()

    def project(g):
        cols = pl.ds(g * bs, bs)

        @pl.loop(0, ring)
        def _(m):
            r = aligned(m, local)
            x = tok[m]
            query = dot(x, wv[0].reshape(width, bs))
            key = dot(x, wv[1].reshape(width, bs))
            q[r, cols] = rope(query, cosine[r, :], sine[r, :]).astype(BF16)
            k[r, cols] = rope(key, cosine[r, :], sine[r, :]).astype(BF16)
            v[r, cols] = dot(x, wv[2].reshape(width, bs)).astype(BF16)

    def attend(g, between):
        cols = pl.ds(g * bs, bs)
        lanes = group_lanes(heads, bs)
        columns = lax.broadcasted_iota(jnp.int32, (1, 128), 1)
        scale = jnp.asarray(HEAD_DIM ** (-0.5), BF16)
        for i in range(rows // q_tile):
            r = pl.ds(i * q_tile, q_tile)
            acc[...] = jnp.zeros_like(acc)

            @pl.loop(0, heads)
            def _(h):
                mask = lanes == h
                scaled = only(mask, q[r, cols]) * scale
                parts = score_parts(scaled, k, cols, i, q_tile)
                most = functools.reduce(
                    jnp.maximum, [jnp.max(s, axis=-1, keepdims=True) for _, s in parts])
                total, mix = 0.0, 0.0
                for keys, scores in parts:
                    exp_scores = jnp.exp(scores - most)
                    total += jnp.sum(exp_scores, axis=-1, keepdims=True)
                    mix += dot(exp_scores.astype(BF16), only(mask, v[keys, cols]))
                acc[...] += mix * (1.0 / total)
                stats[r] = jnp.where(columns == g * heads + h, most + jnp.log(total), stats[r])

            mixed[r, cols] = acc[...].astype(BF16)
            between(i)

    for e in range(2, n - 1):
        for g in range(groups):
            if (g, e) != (0, 2):
                event(g, e)
    for b in range(groups, len(batches)):
        event(b, 0)
    def fetch(g):
        att.finish(g)
        for copy in loads(g):
            copy.start()

    event(0, n - 1)
    fetch(0)
    for g in range(groups):
        for copy in loads(g):
            copy.wait()
        project(g)
        if g == 0:
            cot_ring.wait(1)
            cot_ring.start(2)
        if g + 1 < groups:
            event(g + 1, n - 1)

        def between(i):
            if i == 1 and g + 1 < groups:
                fetch(g + 1)

        attend(g, between)
    for h in range(3, ring // 2 + 1):
        cot_ring.wait(h - 1)
        cot_ring.start(h)
    cot_ring.wait(ring // 2)
    stores = [
        pltpu.make_async_copy(ref, out, io.at[3 + i])
        for i, (ref, out) in enumerate(((q, q_out), (k, k_out), (v, v_out), (mixed, mixed_out), (stats, stats_out)))
    ]
    for copy in stores:
        copy.start()
    out_loads = [
        pltpu.make_async_copy(w_full.at[g, :, :, pl.ds(3 * bs, bs)], wv.at[g], load.at[g])
        for g in range(groups)
    ]
    for copy in out_loads:
        copy.start()
    for copy in out_loads:
        copy.wait()

    def out_share(offset):
        m = at.member(offset)
        r = aligned(m, local)
        for b in range(n):
            block = sum(
                dot_t(mixed[r, g * bs : (g + 1) * bs], wv[g, b].reshape(2 * bs, bs))
                for g in range(groups)
            )
            part[m, :, b * 2 * bs : (b + 1) * 2 * bs] = block.astype(BF16)

    moves = [(b, e) for e in range(1, n) for b in range(groups, len(batches))]

    def move():
        if moves:
            event(*moves.pop(0))

    out_share(ring // 2)
    for d in range(2):
        sums.start(0, d)
    for kk in range(1, ring // 2):
        for d in range(2):
            out_share((1 if d == 0 else -1) * (ring // 2 - kk))
        move()
        for d in range(2):
            sums.add(kk - 1, d)
            sums.start(kk, d)
    out_share(0)
    move()
    own_cot.wait()
    own_again = pltpu.make_async_copy(tokens, xrow, io.at[8])
    own_again.start()
    own_again.wait()
    for d in range(2):
        sums.add(ring // 2 - 1, d)

    @pl.loop(0, local // norm_tile)
    def _(i):
        r = aligned(i, norm_tile)
        value = xrow[r].astype(F32) + part[at.t, r].astype(F32)
        resid[r] = value
        scale = inverse_rms(value)

        def store(cols, value):
            xrow[r, cols] = value

        norm_into(lambda cols: resid[r, cols], scale, 1, store)

    x_ring.start(1)
    own_x = pltpu.make_async_copy(xrow, x_full.at[at.t], io.at[0])
    resid_store = pltpu.make_async_copy(resid, residual_out, io.at[8])
    own_x.start()
    resid_store.start()
    move()
    for h in range(2, ring // 2 + 1):
        move()
        x_ring.wait(h - 1)
        x_ring.start(h)
    if len(moves) > len(batches) - groups:
        move()
    x_ring.wait(ring // 2)
    while moves:
        move()
    for line in (cot_ring, x_ring):
        line.sent()
    sums.sent()
    for a in range(pre):
        if a < first:
            feed.finish(a)
        else:
            feed.sent(a, range(1, n - 1))
    for copy in (normed_store, own_x, resid_store, *stores):
        copy.wait()


def forward_part(n, ring, pre, tokens, cotangent, w_full, ff_full, cosine, sine, q_tile=256):
    groups, bs = w_full.shape[0], w_full.shape[-1]
    chunks = ff_full.shape[0]
    local, width = tokens.shape
    rows = local * ring
    cols = groups * bs
    any_ = pl.BlockSpec(memory_space=pl.ANY)
    vmem = pl.BlockSpec(memory_space=pltpu.VMEM)
    dma = pltpu.SemaphoreType.DMA
    shape = jax.ShapeDtypeStruct
    half = ring // 2
    return pl.pallas_call(
        functools.partial(forward_kernel, n, ring, pre, min(q_tile, rows)),
        out_shape=[
            shape(w_full.shape, BF16),
            shape(ff_full.shape, BF16),
            shape((ring, local, width), BF16),
            shape((rows, cols), BF16),
            shape((rows, cols), BF16),
            shape((rows, cols), BF16),
            shape((rows, cols), BF16),
            shape((rows, 128), F32),
            shape((local, width), F32),
            shape((ring, local, width), BF16),
            shape((ring, local, width), BF16),
        ],
        in_specs=[any_] * 4 + [vmem] * 2,
        out_specs=[any_] * 11,
        input_output_aliases={2: 0, 3: 1},
        scratch_shapes=[
            pltpu.VMEM((ring, local, width), BF16),
            pltpu.VMEM((max(4, groups), n, 2, bs, bs), BF16),
            pltpu.VMEM((2 * n, 16, bs), BF16),
            pltpu.VMEM((rows, cols), BF16),
            pltpu.VMEM((rows, cols), BF16),
            pltpu.VMEM((rows, cols), BF16),
            pltpu.VMEM((rows, cols), BF16),
            pltpu.VMEM((rows, 128), F32),
            pltpu.VMEM((min(q_tile, rows), bs), F32),
            pltpu.VMEM((ring, local, width), BF16),
            pltpu.VMEM((2, half, local, width), BF16),
            pltpu.VMEM((local, width), BF16),
            pltpu.VMEM((local, width), F32),
            dma((2, n - 1, groups)), dma((2, n - 1, groups)),
            dma((groups,)), dma((groups,)),
            dma((2, n - 1, chunks)), dma((2, n - 1, chunks)),
            dma((chunks,)), dma((chunks,)),
            dma((2, half)), dma((2, half)), dma((2, half)), dma((2, half)),
            dma((2, half)), dma((2, half)), dma((2, half)), dma((2, half)),
            dma((9,)), dma((5,)), dma((2 * n - 1,)), dma((2 * n - 1,)),
        ],
        compiler_params=pltpu.CompilerParams(
            collective_id=1, has_side_effects=True, vmem_limit_bytes=56 * 2**20),
    )(tokens, cotangent, w_full, ff_full, cosine, sine)


def layer_kernel(
    n, ring, pre, pace, plan, q_tile, tile,
    ff_in, x_hbm, dy_hbm, residual, cotangent, tokens, normed_in, q_in, k_in, v_in, mixed_in, stats_in,
    w_full, cosine_in, sine_in,
    ff_full, output, grad_tokens, gain_grads, ff_result, ff_summed, ff_landed,
    att_result, att_summed, att_landed, out_hbm,
    part, land, dres_full, core_in, stage, got, total, gparts, gland, gsecond, gone, gtwo,
    w_send, w_recv, w_sib_send, w_sib_recv,
    f_send, f_recv, f_load, f_out, a_send, a_recv, a_load, a_out,
    core_send, core_recv, acore_send, acore_recv, store_sem,
    s1_send, s1_recv, s2_send, s2_recv, s3_send, s3_recv, x_send, x_recv, free_sem,
    g_send, g_recv, h_send, h_recv, io, load,
):
    at = Place(n, ring)
    c = at.c
    groups, _, _, _, bs = w_full.shape
    chunks, _, _, unit, _ = ff_full.shape
    local, width = tokens.shape
    rows = local * ring
    heads = bs // HEAD_DIM
    half = ring // 2
    weights = LineGather(at, ff_full, w_send, w_recv, w_sib_send, w_sib_recv)
    feed = LineSum(at, chunks, ff_summed, ff_landed, ff_result,
                   stage.at[:, :, :, pl.ds(0, unit)], got.at[:, pl.ds(0, unit)],
                   total.at[pl.ds(0, unit)],
                   f_send, f_recv, f_load, f_out)
    att = LineSum(at, groups, att_summed, att_landed, att_result, stage, got, total,
                  a_send, a_recv, a_load, a_out)
    sums1 = RingSum(at, part, land, s1_send, s1_recv)
    sums2 = RingSum(at, part, land, s2_send, s2_recv)
    sums3 = RingSum(at, part, land, s3_send, s3_recv)
    dres_ring = RingGather(at, dres_full.at[at.t], dres_full, x_send, x_recv)
    lag = max(0, n - pre)
    num, den, begin = pace

    def fetch(src, dst, i):
        return pltpu.make_async_copy(src, dst, io.at[i])

    x_in = fetch(x_hbm, part, 0)
    dy_in = fetch(dy_hbm, dres_full, 1)
    x_in.start()
    dy_in.start()
    at.barrier(with_all=True)
    first = (pre + 1) // 2
    for a in range(first, pre):
        weights.give(a, n - 1)

    def ticks_before(j):
        return (j >= begin) * ((num * (j - begin)) // den)

    def feed_phase(oacc, dacc, wv, pg, hid, dgate, dup, out_stage):
        x, dy = part, dres_full

        def loads(j):
            return [
                pltpu.make_async_copy(
                    ff_full.at[j, :, :, pl.ds(i * bs, bs)], wv.at[j % 3, i], load.at[j % 3, i])
                for i in range(3)
            ]

        def core_copy(j):
            return pltpu.make_async_remote_copy(
                pg.at[1 - c], core_in.at[j % 2, :, pl.ds(0, unit)],
                core_send.at[j % 2], core_recv.at[j % 2],
                device_id={"dp": at.sib}, device_id_type=MESH)

        def store(j):
            return pltpu.make_async_copy(pg.at[c], ff_summed.at[j], store_sem)

        for copy in loads(0):
            copy.start()

        @pl.loop(0, rows // 64)
        def _(i):
            r = aligned(i, 64)
            oacc[r] = jnp.zeros((64, width), F32)
            dacc[r] = jnp.zeros((64, width), F32)

        x_in.wait()
        dy_in.wait()
        per = max(1, min(tile // local, ring))

        def columns(ref, cols):
            return ref[:, :, cols].reshape(rows, bs)

        def weight_grads(cc, now):
            @pl.loop(0, n)
            def _(k):
                cols = aligned(2 * k + cc, bs)
                xt = columns(x, cols)
                pg[cc, k, pl.ds(0, bs)] = t_dot(xt, dgate[:, now]).astype(BF16)
                pg[cc, k, pl.ds(bs, bs)] = t_dot(xt, dup[:, now]).astype(BF16)
                pg[cc, k, pl.ds(2 * bs, bs)] = t_dot(columns(dy, cols), hid[:, now]).astype(BF16)

        def turn(j, half_event):
            tick = ticks_before(j)
            for e in range(n - 1, 0, -1):
                q = tick - (e - 1) + 2 * n
                r = q // 2 - n

                @pl.when((j >= 0) & (tick < ticks_before(j + 1)) & (q % 2 == 0)
                         & (r >= 0) & (r < chunks))
                def _():
                    half_event(r, e)

        def compute(j):
            slot = j % 3
            now = aligned(j % 2, bs)
            for copy in loads(j):
                copy.wait()

            @pl.when((j + 1 >= first) & (j + 1 < pre))
            def _():
                weights.given(j + 1)
                weights.sent(j + 1, (n - 1,))

            @pl.when(j + 1 < pre)
            def _():
                for copy in loads(j + 1):
                    copy.start()

            @pl.loop(0, ring // per)
            def _(m):
                r = aligned(m, per * local)
                here = pl.ds(m * per, per)
                rows_x = x[here].reshape(per * local, width)
                gate = dot(rows_x, wv[slot, 0].reshape(width, bs))
                up = dot(rows_x, wv[slot, 1].reshape(width, bs))
                dh = dot(dy[here].reshape(per * local, width), wv[slot, 2].reshape(width, bs))
                s = jax.nn.sigmoid(gate)
                gs = gate * s
                hid[r, now] = (gs * up).astype(BF16)
                dup[r, now] = (dh * gs).astype(BF16)
                dgate[r, now] = (dh * up * (s + gs * (1 - s))).astype(BF16)

            turn(j, feed.close)
            weight_grads(1 - c, now)
            core_copy(j).start()

            @pl.when(j % 2 == 1)
            def _():
                one, two = (j + 2) % 3, slot

                @pl.loop(0, rows // tile)
                def _(m):
                    r = aligned(m, tile)
                    both = jnp.concatenate([dgate[r, :], dup[r, :]], axis=1)

                    @pl.loop(0, n)
                    def _(k):
                        def block(s, i):
                            return wv[s, i, k].reshape(2 * bs, bs)

                        cols = aligned(k, 2 * bs)
                        oacc[r, cols] += dot_t(
                            hid[r, :], jnp.concatenate([block(one, 2), block(two, 2)], axis=1))
                        dacc[r, cols] += dot_t(both, jnp.concatenate(
                            [block(one, 0), block(two, 0), block(one, 1), block(two, 1)], axis=1))

            weight_grads(c, now)
            core_copy(j).wait_recv()

            @pl.loop(0, n)
            def _(k):
                pg[c, k] = pg[c, k] + core_in[j % 2, k, pl.ds(0, unit)]

            store(j).start()
            core_copy(j).wait_send()

        def begin_step(i):
            return min(2 * i + 1, i + max(pre - n, 0))

        @pl.loop(0, lag + chunks)
        def _(step):
            j = step - lag
            for a in range(first, pre):
                @pl.when(j == a - 2)
                def _():
                    weights.event(a, n - 1)

            for i in range(chunks - pre):
                for e in range(n):
                    @pl.when(step == begin_step(i) + e)
                    def _():
                        weights.event(pre + i, e)

            @pl.when(j >= 1)
            def _():
                store(j - 1).wait()
                feed.event(j - 1, 0)

            turn(j, feed.open)

            @pl.when(j >= 0)
            def _():
                compute(j)

            for i in range(chunks - pre):
                @pl.when(step == begin_step(i) + n - 1)
                def _():
                    weights.finish(pre + i)

            @pl.when((j + 1 >= pre) & (j + 1 >= 1) & (j + 1 < chunks))
            def _():
                for copy in loads(j + 1):
                    copy.start()

        store(chunks - 1).wait()
        feed.event(chunks - 1, 0)

        @pl.loop(0, ring)
        def _(m):
            part[m] = dacc[aligned(m, local), :].astype(BF16)

        for d in range(2):
            sums1.start(0, d)

        piece = local // 2

        def put(m):
            return fetch(
                out_stage.at[m % 2], out_hbm.at[m // 2, pl.ds(m % 2 * piece, piece)], m % 2)

        for m in range(2 * ring):
            if m > 1:
                put(m - 2).wait()
            out_stage[m % 2] = oacc[m * piece : (m + 1) * piece, :].astype(BF16)
            put(m).start()
        for m in range(2 * ring - 2, 2 * ring):
            put(m).wait()

    pl.run_scoped(
        feed_phase,
        pltpu.VMEM((rows, width), F32),
        pltpu.VMEM((rows, width), F32),
        pltpu.VMEM((3, 3, n, 2, bs, bs), BF16),
        pltpu.VMEM((2, n, unit, bs), BF16),
        pltpu.VMEM((rows, 2 * bs), BF16),
        pltpu.VMEM((rows, 2 * bs), BF16),
        pltpu.VMEM((rows, 2 * bs), BF16),
        pltpu.VMEM((2, local // 2, width), BF16),
    )

    done = [0 if chunks < begin else (num * (chunks - begin)) // den]
    last = 2 * (chunks - 1) + n - 2

    planned = list(plan)
    moves, opened = [], []

    def settle():
        while opened:
            line, j, e = opened.pop(0)
            line.close(j, e)
            if line is feed and (j, e) == (chunks - 1, n - 1):
                feed.result(j).wait()

    def point(later=False):
        settle()
        for _ in range(planned.pop(0) if planned else 1):
            settle()
            if done[0] <= last:
                tick = done[0]
                for e in range(n - 1, 0, -1):
                    if (tick - e + 1) % 2 == 0 and 0 <= (tick - e + 1) // 2 < chunks:
                        feed.open((tick - e + 1) // 2, e)
                        opened.append((feed, (tick - e + 1) // 2, e))
                done[0] += 1
            elif moves:
                j, e = moves.pop(0)
                att.open(j, e)
                opened.append((att, j, e))
        if not later:
            settle()

    def attention_phase(
        normed, wv, gains, q, k, v, mixed, stats, dmix, dq, dk, dv, dproj, resid, dres, small, lined,
        gsum, pg, cosine, sine,
    ):
        resid_in = fetch(residual, resid, 0)
        cot_in = fetch(cotangent, lined, 1)
        gains_in = fetch(w_full.at[0, :, :, pl.ds(4 * bs, 16)], gains, 2)
        saved = [
            fetch(src, dst, 3 + i)
            for i, (src, dst) in enumerate(
                ((normed_in, normed), (q_in, q), (k_in, k), (v_in, v), (mixed_in, mixed)))
        ]
        weight_loads = [
            pltpu.make_async_copy(
                w_full.at[g, :, :, pl.ds(i * bs, bs)], wv.at[i, g], load.at[i, g])
            for g in range(groups) for i in range(4)
        ]
        saved += [fetch(cosine_in, cosine, 8), fetch(sine_in, sine, 9), fetch(stats_in, stats, 10)]
        for copy in (resid_in, cot_in, gains_in, *saved, *weight_loads):
            copy.start()

        def gain_of(row, i):
            return gains[i // 2, i % 2, row : row + 1, :].astype(F32)

        tile = min(64, local)

        def norm_back(value_of, grad_of, row, emit):
            gsum[row : row + 1, :] = jnp.zeros((1, width), F32)

            @pl.loop(0, local // tile)
            def _(i):
                r = aligned(i, tile)
                scale = inverse_rms(value_of(r, pl.ds(0, width)))
                inner = jnp.zeros((tile, 1), F32)
                for b in range(2 * n):
                    cols = pl.ds(b * bs, bs)
                    value = value_of(r, cols)
                    grad = grad_of(r, cols)
                    gsum[row : row + 1, cols] += jnp.sum(
                        grad * value * scale, axis=0, keepdims=True)
                    inner += jnp.sum(grad * gain_of(row, b) * value, axis=-1, keepdims=True)
                pull = scale * scale * scale * (inner / width)
                for b in range(2 * n):
                    cols = pl.ds(b * bs, bs)
                    emit(r, cols,
                         scale * grad_of(r, cols) * gain_of(row, b) - value_of(r, cols) * pull)

        for kk in range(half):
            point()
            for d in range(2):
                sums1.add(kk, d)
                if kk < half - 1:
                    sums1.start(kk + 1, d)
        for copy in (resid_in, cot_in, gains_in):
            copy.wait()

        def emit_residual(r, cols, value):
            total = lined[r, cols].astype(F32) + value
            dres[r, cols] = total
            dres_full[at.t, r, cols] = total.astype(BF16)

        norm_back(lambda r, cols: resid[r, cols],
                  lambda r, cols: part[at.t, r, cols].astype(F32), 1, emit_residual)
        dres_ring.start(1)
        sums1.sent()
        second_in = fetch(out_hbm, part, 0)
        second_in.start()
        for h in range(2, half + 1):
            point()
            dres_ring.wait(h - 1)
            dres_ring.start(h)
        point()
        second_in.wait()
        dres_ring.wait(half)
        for d in range(2):
            sums2.start(0, d)
        for copy in (*saved, *weight_loads):
            copy.wait()

        def core_copy(g):
            return pltpu.make_async_remote_copy(
                pg.at[1 - c], core_in.at[g], acore_send.at[g], acore_recv.at[g],
                device_id={"dp": at.sib}, device_id_type=MESH)

        def store(g):
            return pltpu.make_async_copy(pg.at[c], att_summed.at[g], store_sem)

        def attend_back(g, between):
            gcols = pl.ds(g * bs, bs)
            lanes = group_lanes(heads, bs)
            columns = lax.broadcasted_iota(jnp.int32, (1, 128), 1)
            scale = jnp.asarray(HEAD_DIM ** (-0.5), BF16)
            dk[...] = jnp.zeros_like(dk)
            dv[...] = jnp.zeros_like(dv)
            for i in range(rows // q_tile):
                r = pl.ds(i * q_tile, q_tile)
                dq[r] = jnp.zeros((q_tile, bs), F32)

                @pl.loop(0, heads)
                def _(h):
                    mask = lanes == h
                    scaled = only(mask, q[r, gcols]) * scale
                    dmh = only(mask, dmix[r])
                    log_total = jnp.sum(
                        jnp.where(columns == g * heads + h, stats[r], 0.0), axis=-1, keepdims=True)
                    inner = jnp.sum(
                        dmh.astype(F32) * mixed[r, gcols].astype(F32), axis=-1, keepdims=True)
                    d_query = 0.0
                    for keys, scores in score_parts(scaled, k, gcols, i, q_tile):
                        probs = jnp.exp(scores - log_total)
                        d_probs = dot_t(dmh, v[keys, gcols])
                        d_scores = (probs * (d_probs - inner)).astype(BF16)
                        d_query += dot(d_scores, only(mask, k[keys, gcols]))
                        dk[keys] += t_dot(d_scores, scaled)
                        dv[keys] += t_dot(probs.astype(BF16), dmh)
                    dq[r] += d_query

                between(i)

        def weight_grads(g, cc):
            gcols = pl.ds(g * bs, bs)

            @pl.loop(0, n)
            def _(b):
                cols = aligned(2 * b + cc, bs)
                x = normed[:, :, cols].reshape(rows, bs)
                for i in range(3):
                    pg[cc, b, pl.ds(i * bs, bs)] = t_dot(x, dproj[i, :, gcols]).astype(BF16)
                pg[cc, b, pl.ds(3 * bs, bs)] = t_dot(
                    dres_full[:, :, cols].reshape(rows, bs), mixed[:, gcols]).astype(BF16)

        second = [0]

        def second_sum():
            if second[0] < half:
                kk = second[0]
                for d in range(2):
                    sums2.add(kk, d)
                    if kk < half - 1:
                        sums2.start(kk + 1, d)
                second[0] += 1

        tiles = rows // q_tile

        def between(i):
            point(later=i < tiles - 1)
            if i == tiles - 1:
                second_sum()

        for g in range(groups):
            gcols = pl.ds(g * bs, bs)

            @pl.loop(0, ring)
            def _(m):
                r = aligned(m, local)
                dmix[r] = dot(dres_full[m], wv[3, g].reshape(width, bs)).astype(BF16)

            attend_back(g, between)

            @pl.loop(0, ring)
            def _(m):
                r = aligned(m, local)
                for i, value in enumerate((dq[r] * HEAD_DIM ** (-0.5), dk[r])):
                    dproj[i, r, gcols] = rope(
                        value, cosine[r, :], sine[r, :], back=True).astype(BF16)
                dproj[2, r, gcols] = dv[r].astype(BF16)

            weight_grads(g, 1 - c)
            core_copy(g).start()
            weight_grads(g, c)
            core_copy(g).wait_recv()

            @pl.loop(0, n)
            def _(b):
                pg[c, b] = pg[c, b] + core_in[g, b]

            store(g).start()
            core_copy(g).wait_send()
            store(g).wait()
            att.event(g, 0)
            moves.extend((g, e) for e in range(1, n))

        while second[0] < half:
            second_sum()
        sums2.sent()

        @pl.loop(0, local // tile)
        def _(i):
            r = aligned(i, tile)
            lined[r] = (resid[r] + part[at.t, r].astype(F32)).astype(BF16)

        out_store = fetch(lined, output, 0)
        out_store.start()
        for way in (1, -1):
            pl.semaphore_signal(
                free_sem, inc=1, device_id={"tensor": at.member(way)}, device_id_type=MESH)

        def share(offset):
            m = at.member(offset)
            r = aligned(m, local)
            for b in range(n):
                block = sum(
                    dot_t(dproj[i, r, g * bs : (g + 1) * bs], wv[i, g, b].reshape(2 * bs, bs))
                    for i in range(3) for g in range(groups)
                )
                part[m, :, b * 2 * bs : (b + 1) * 2 * bs] = block.astype(BF16)

        share(half)
        pl.semaphore_wait(free_sem, 2)
        for d in range(2):
            sums3.start(0, d)

        tok_in = fetch(tokens, small, 1)
        dres_ring.sent()
        tok_in.start()
        point()
        for kk in range(1, half):
            for d in range(2):
                share((1 if d == 0 else -1) * (half - kk))
            for d in range(2):
                sums3.add(kk - 1, d)
                sums3.start(kk, d)
            point()
        share(0)
        point()
        for d in range(2):
            sums3.add(half - 1, d)
        tok_in.wait()
        out_store.wait()

        def emit_tokens(r, cols, value):
            lined[r, cols] = (dres[r, cols] + value).astype(BF16)

        norm_back(lambda r, cols: small[r, cols].astype(F32),
                  lambda r, cols: part[at.t, r, cols].astype(F32), 0, emit_tokens)
        token_store = fetch(lined, grad_tokens, 0)
        token_store.start()
        for b in range(2 * n):
            gparts[b, 0:2] = gsum[0:2, b * bs : (b + 1) * bs]
            gparts[b, 2:8] = jnp.zeros((6, bs), F32)
        over_dp = SmallSum("dp", 2 * at.z + c, 2 * n, lambda i: gparts.at[i], gland, g_send, g_recv)
        gone[...] = over_dp.total()
        over_ring = SmallSum("tensor", at.t, ring, lambda i: gone, gsecond, h_send, h_recv)
        gtwo[...] = over_ring.total()
        gain_store = fetch(gtwo, gain_grads, 1)
        gain_store.start()
        while done[0] <= last or moves:
            point()
        att.result(groups - 1).wait()
        token_store.wait()
        gain_store.wait()
        sums3.sent()

    cols = groups * bs
    pl.run_scoped(
        attention_phase,
        pltpu.VMEM((ring, local, width), BF16),
        pltpu.VMEM((4, groups, n, 2, bs, bs), BF16),
        pltpu.VMEM((n, 2, 16, bs), BF16),
        pltpu.VMEM((rows, cols), BF16),
        pltpu.VMEM((rows, cols), BF16),
        pltpu.VMEM((rows, cols), BF16),
        pltpu.VMEM((rows, cols), BF16),
        pltpu.VMEM((rows, 128), F32),
        pltpu.VMEM((rows, bs), BF16),
        pltpu.VMEM((rows, bs), F32),
        pltpu.VMEM((rows, bs), F32),
        pltpu.VMEM((rows, bs), F32),
        pltpu.VMEM((3, rows, cols), BF16),
        pltpu.VMEM((local, width), F32),
        pltpu.VMEM((local, width), F32),
        pltpu.VMEM((local, width), BF16),
        pltpu.VMEM((local, width), BF16),
        pltpu.VMEM((8, width), F32),
        pltpu.VMEM((2, n, 4 * bs, bs), BF16),
        pltpu.VMEM((rows, bs), F32),
        pltpu.VMEM((rows, bs), F32),
    )


def layer_part(
    n, ring, pre, pace, plan, ff_full, x, dy, residual, cotangent, tokens, normed, q, k, v, mixed, stats,
    w_full, cosine, sine, q_tile=256, tile=512,
):
    groups, _, _, _, bs = w_full.shape
    chunks, _, _, unit, _ = ff_full.shape
    local, width = tokens.shape
    rows = local * ring
    half = ring // 2
    any_ = pl.BlockSpec(memory_space=pl.ANY)
    dma = pltpu.SemaphoreType.DMA
    shape = jax.ShapeDtypeStruct
    big = (ring, local, width)
    wide = 4 * bs
    return pl.pallas_call(
        functools.partial(
            layer_kernel, n, ring, pre, pace, plan, min(q_tile, rows), min(tile, rows)),
        out_shape=[
            shape(ff_full.shape, BF16),
            shape((local, width), BF16),
            shape((local, width), BF16),
            shape((8, bs), F32),
            shape((chunks, unit, bs), BF16),
            shape((chunks, n, unit, bs), BF16),
            shape((2, chunks, n - 1, unit, bs), BF16),
            shape((groups, wide, bs), BF16),
            shape((groups, n, wide, bs), BF16),
            shape((2, groups, n - 1, wide, bs), BF16),
            shape(big, BF16),
        ],
        in_specs=[any_] * 15,
        out_specs=[any_] * 11,
        input_output_aliases={0: 0},
        scratch_shapes=[
            pltpu.VMEM(big, BF16),
            pltpu.VMEM((2, half, local, width), BF16),
            pltpu.VMEM(big, BF16),
            pltpu.VMEM((max(2, groups), n, wide, bs), BF16),
            pltpu.VMEM((2, n - 2, n // 2, wide, bs), BF16),
            pltpu.VMEM((blocks_at_once(n), wide, bs), BF16),
            pltpu.VMEM((wide, bs), BF16),
            pltpu.VMEM((2 * n, 8, bs), F32),
            pltpu.VMEM((2 * n - 1, 8, bs), F32),
            pltpu.VMEM((ring - 1, 8, bs), F32),
            pltpu.VMEM((8, bs), F32),
            pltpu.VMEM((8, bs), F32),
            dma((2, n - 1, chunks)), dma((2, n - 1, chunks)), dma((chunks,)), dma((chunks,)),
            dma((2, n - 1, chunks)), dma((2, n - 1, chunks)), dma((blocks_at_once(n),)), dma,
            dma((2, n - 1, groups)), dma((2, n - 1, groups)), dma((blocks_at_once(n),)), dma,
            dma((2,)), dma((2,)), dma((groups,)), dma((groups,)), dma,
            dma((2, half)), dma((2, half)), dma((2, half)), dma((2, half)),
            dma((2, half)), dma((2, half)), dma((2, half)), dma((2, half)),
            pltpu.SemaphoreType.REGULAR,
            dma((2 * n - 1,)), dma((2 * n - 1,)), dma((ring - 1,)), dma((ring - 1,)),
            dma((11,)), dma((4, max(4, groups))),
        ],
        compiler_params=pltpu.CompilerParams(
            collective_id=2, has_side_effects=True, vmem_limit_bytes=63 * 2**20),
    )(ff_full, x, dy, residual, cotangent, tokens, normed, q, k, v, mixed, stats,
      w_full, cosine, sine)


PREFETCH = 6
PACE = (1, 1, 2)
PLAN = (1, 2, 2, 2) + (1, 0, 1, 0) + (1, 1, 0, 1) + (1, 2, 1)


def pack_kernel(place, q, k, v, o, gain_attn, gain_mlp, gate, up, down, att, ff):
    bs = q.shape[0]

    @pl.when(pl.program_id(0) == 0)
    def _():
        row = lax.broadcasted_iota(jnp.int32, (16, bs), 0)
        first, second = (g[...].astype(F32) for g in (gain_attn, gain_mlp))
        gains = jnp.where(row == 0, first, jnp.where(row == 1, second, 0.0)).astype(BF16)
        for g in range(att.shape[0]):
            here = slice(g * bs, (g + 1) * bs)
            for i, ref in enumerate((q, k, v)):
                att[g, i * bs : (i + 1) * bs] = ref[:, here]
            att[g, 3 * bs : 4 * bs] = o[here].T
            att[g, 4 * bs : 4 * bs + 16] = gains

    for j in range(ff.shape[0]):
        here = slice(j * bs, (j + 1) * bs)
        ff[j, 0:bs] = gate[:, here]
        ff[j, bs : 2 * bs] = up[:, here]
        ff[j, 2 * bs : 3 * bs] = down[here].T


def chunks_at_once(chunks):
    return 4 if chunks % 4 == 0 else 1


def pack(w_query, w_key, w_value, w_out, gain_attn, gain_mlp, w_gate, w_up, w_down):
    bs = w_query.shape[0]
    n = lax.axis_size("dp") // 2
    groups, chunks = w_query.shape[1] // bs, w_gate.shape[1] // bs
    some = chunks_at_once(chunks)
    col = pl.BlockSpec((bs, groups * bs), lambda j, p: (0, 0))
    row = pl.BlockSpec((groups * bs, bs), lambda j, p: (0, 0))
    gain = pl.BlockSpec((1, bs), lambda j, p: (0, 0))
    wide = pl.BlockSpec((bs, some * bs), lambda j, p: (0, j))
    tall = pl.BlockSpec((some * bs, bs), lambda j, p: (j, 0))
    return pl.pallas_call(
        pack_kernel,
        out_shape=[
            jax.ShapeDtypeStruct((groups, n, 2, 4 * bs + 16, bs), BF16),
            jax.ShapeDtypeStruct((chunks, n, 2, 3 * bs, bs), BF16),
        ],
        grid_spec=pltpu.PrefetchScalarGridSpec(
            num_scalar_prefetch=1,
            grid=(chunks // some,),
            in_specs=[col, col, col, row, gain, gain, wide, wide, tall],
            out_specs=[
                pl.BlockSpec((groups, None, None, 4 * bs + 16, bs),
                             lambda j, p: (0, p[0], p[1], 0, 0)),
                pl.BlockSpec((some, None, None, 3 * bs, bs),
                             lambda j, p: (j, p[0], p[1], 0, 0)),
            ],
        ),
        compiler_params=pltpu.CompilerParams(vmem_limit_bytes=63 * 2**20),
    )(jnp.stack([lax.axis_index("dp") // 2, lax.axis_index("dp") % 2]),
      w_query, w_key, w_value, w_out, gain_attn.reshape(1, bs), gain_mlp.reshape(1, bs),
      w_gate, w_up, w_down)


def unpack_kernel(att, ff, q, k, v, o, gate, up, down):
    bs = q.shape[0]

    @pl.when(pl.program_id(0) == 0)
    def _():
        for g in range(att.shape[0]):
            here = slice(g * bs, (g + 1) * bs)
            for i, ref in enumerate((q, k, v)):
                ref[:, here] = att[g, i * bs : (i + 1) * bs].astype(F32)
            o[here] = att[g, 3 * bs : 4 * bs].astype(F32).T

    for j in range(ff.shape[0]):
        here = slice(j * bs, (j + 1) * bs)
        gate[:, here] = ff[j, 0:bs].astype(F32)
        up[:, here] = ff[j, bs : 2 * bs].astype(F32)
        down[here] = ff[j, 2 * bs : 3 * bs].astype(F32).T


def unpack(att, ff):
    groups, chunks, bs = att.shape[0], ff.shape[0], ff.shape[2]
    some = chunks_at_once(chunks)
    shape = jax.ShapeDtypeStruct
    col = pl.BlockSpec((bs, groups * bs), lambda j: (0, 0))
    row = pl.BlockSpec((groups * bs, bs), lambda j: (0, 0))
    wide = pl.BlockSpec((bs, some * bs), lambda j: (0, j))
    tall = pl.BlockSpec((some * bs, bs), lambda j: (j, 0))
    return pl.pallas_call(
        unpack_kernel,
        grid=(chunks // some,),
        out_shape=[shape((bs, groups * bs), F32)] * 3 + [shape((groups * bs, bs), F32)]
        + [shape((bs, chunks * bs), F32)] * 2 + [shape((chunks * bs, bs), F32)],
        in_specs=[
            pl.BlockSpec((groups, 4 * bs, bs), lambda j: (0, 0, 0)),
            pl.BlockSpec((some, 3 * bs, bs), lambda j: (j, 0, 0)),
        ],
        out_specs=[col] * 3 + [row] + [wide] * 2 + [tall],
        compiler_params=pltpu.CompilerParams(vmem_limit_bytes=63 * 2**20),
    )(att, ff)


def rotary_tables(row_count, width):
    frequency = rope_base ** (-np.arange(HEAD_DIM // 2) * 2.0 / HEAD_DIM)
    angles = (np.arange(row_count) % LEN)[:, None] * frequency[None, :]
    angles = np.tile(angles, (1, width // (HEAD_DIM // 2)))
    return np.cos(angles).astype(np.float32), np.sin(angles).astype(np.float32)


def shards(
    tokens, gain_attn, w_query, w_key, w_value, w_out, gain_mlp, w_gate, w_up, w_down, cotangent
):
    dp, ring = lax.axis_size("dp"), lax.axis_size("tensor")
    n = dp // 2
    local, width = tokens.shape
    rows = local * ring
    assert rows == LEN
    bs = w_query.shape[0]
    cosine, sine = rotary_tables(rows, bs)
    w_start, ff_start = pack(
        w_query, w_key, w_value, w_out, gain_attn, gain_mlp, w_gate, w_up, w_down
    )
    w_full, ff_full, normed, q, k, v, mixed, stats, residual, x, dy = forward_part(
        n, ring, PREFETCH, tokens, cotangent, w_start, ff_start, cosine, sine
    )
    _, output, grad_tokens, gain_grads, ff_grads, _, _, att_grads, _, _, _ = layer_part(
        n, ring, PREFETCH, PACE, PLAN, ff_full, x, dy, residual, cotangent, tokens,
        normed, q, k, v, mixed, stats, w_full, cosine, sine,
    )
    g_query, g_key, g_value, g_out, g_gate, g_up, g_down = unpack(att_grads, ff_grads)
    return (
        output,
        grad_tokens,
        gain_grads[0],
        g_query,
        g_key,
        g_value,
        g_out,
        gain_grads[1],
        g_gate,
        g_up,
        g_down,
    )


def solution(mesh):
    placed = (
        P(("dp", "tensor"), None),
        P("dp"),
        P("dp", "tensor"),
        P("dp", "tensor"),
        P("dp", "tensor"),
        P("tensor", "dp"),
        P("dp"),
        P("dp", "tensor"),
        P("dp", "tensor"),
        P("tensor", "dp"),
        P(("dp", "tensor"), None),
    )
    return jax.shard_map(
        shards,
        mesh=mesh,
        in_specs=placed,
        out_specs=(
            P(("dp", "tensor"), None),
            P(("dp", "tensor"), None),
            P("dp"),
            P("dp", "tensor"),
            P("dp", "tensor"),
            P("dp", "tensor"),
            P("tensor", "dp"),
            P("dp"),
            P("dp", "tensor"),
            P("dp", "tensor"),
            P("tensor", "dp"),
        ),
        check_vma=False,
    )
```
